128 devices in a mesh: fx: 16 (over y, z), fy: 8 (over x, core).
Axes of the slice: x: 4, y: 4, z: 4, core: 2. Of those that a mesh axis runs over, the one named last changes fastest.
Arguments:
- state: float32 [256, 48, 2048], P('fy', None, 'fx'), may hold values from -6 to 6
- coef: float32 [256, 2048], P('fy', 'fx'), may hold values from 0.05 to 0.24
- weight_table: float32 [64, 128, 128], replicated, may hold values from -0.5 to 0.5
- src_blocks: int32 [128, 128, 4], P(('fx', 'fy')), may hold values from 0 to 31
- dst_blocks: int32 [128, 128, 4], P(('fx', 'fy')), may hold values from 0 to 31
- weight_rows: int32 [128, 128, 4], P(('fx', 'fy')), may hold values from 0 to 63
- counts: int32 [128, 128], P(('fx', 'fy')), may hold values from 1 to 4, as said below
- brackets: int32 [13], replicated, may hold values from 0 to 14
- fractions: float32 [13], replicated, may hold values from 0 to 1
- w_in: bfloat16 [512, 39], replicated, may hold values from -1 to 1
- b_in: float32 [512], replicated, may hold values from -4 to 4
- w_mid: bfloat16 [512, 512], replicated, may hold values from -0.25 to 0.25
- b_mid: float32 [512], replicated, may hold values from -4 to 4
- w_out: bfloat16 [39, 512], replicated, may hold values from -0.25 to 0.25
Outputs:
- diffused_state: float32 [256, 48, 2048], P('fy', None, 'fx')
- tendency: float32 [256, 48, 2048], P('fy', None, 'fx')
The draws below stay inside these ranges and needn't reach their ends.
Inputs may be any that keep to these rules, and one draw needn't show every extreme that they name: At most 4 slots are used from one device to one owner; in every draw one owner receives 4 from every device. Slots at positions counts and beyond hold padding in src_blocks, dst_blocks and weight_rows.
All inputs are finite; a program needn't handle non-finite values.
Results may differ from the reference program's by a relative error of at most 0.0037.
Values sent between devices are 32-bit elements; how exact they have to be, the bound alone decides.
No kernel may reach another device: no remote copies, remote signals or barrier semaphores. Data moves between devices by JAX's collectives and lax.ppermute only.
A program may use at most 128 MiB of HBM per device.

```python
import jax
import jax.numpy as jnp
from jax import lax

V = 3
LEV = 16
P_SIZE = 13
HID = 512
CA = 128
CB = 32
CAP = 4
K = 64
SWEEPS = 4
DB = 32
NB = 256
NA = 2048
VL = 48
VP = 39
N_FX = 16
N_FY = 8


def draw_counts(key, part):
    key = jax.random.fold_in(key, 11)
    first, second = jax.random.split(key)
    ndev = N_FX * N_FY
    base = jax.random.randint(first, (ndev, ndev), 1, CAP + 1)
    busy = jax.random.randint(second, (), 0, ndev)
    column = jnp.arange(ndev, dtype=jnp.int32)[None, :] == busy
    return jnp.where(column, CAP, base).astype(jnp.int32)


def touch_ends(drawn, key, smallest, largest):
    extent = drawn.shape
    spot = [jax.random.randint(jax.random.fold_in(key, axis), (), 0, extent[axis]) for axis in range(len(extent))]
    drawn = drawn.at[tuple(spot)].set(smallest)
    longest = extent.index(max(extent))
    spot[longest] = (spot[longest] + 1) % extent[longest]
    return drawn.at[tuple(spot)].set(largest)


def steps_of(own_key, extent, cuts, smallest, largest):
    def one(dim, shards_of):
        heights = jax.random.uniform(jax.random.fold_in(jax.random.fold_in(own_key, 6), dim), (shards_of,), jnp.float32, smallest / len(cuts), largest / len(cuts))
        return jnp.repeat(jnp.exp(heights), extent[dim] // shards_of).reshape((-1,) + (1,) * (len(extent) - dim - 1))

    level = one(*cuts[0])
    for cut in cuts[1:]:
        level = level * one(*cut)
    return level


def normal_values(key, shape, scale, reach, shards=(), held_as=jnp.bfloat16):
    values = jax.random.normal(key, shape, jnp.float32) * scale
    if len(shards) > 0:
        values = steps_of(key, shape, shards, -0.22, 0.18) * values
    return jnp.clip(values, min=-reach, max=reach).astype(held_as)


def setup_inputs(seed: int = 0) -> dict:
    splits = jax.random.split(jax.random.key(seed), 15)
    state = normal_values(splits[0], (NB, VL, NA), 1.0, 6.0, ((0, 8), (2, 16)), jnp.float32)
    coef = jnp.clip(0.05 + 0.19 * jax.random.uniform(splits[1], (NB, NA), jnp.float32) ** steps_of(splits[1], (NB, NA), ((0, 8), (1, 16)), -0.2, 0.2), 0.05, 0.24)
    weight_table = normal_values(splits[2], (K, CA, CA), CA ** -0.5, 0.5, (), jnp.float32)
    src_blocks = touch_ends(jax.random.randint(splits[3], (N_FX * N_FY, N_FX * N_FY, CAP), 0, CB), jax.random.fold_in(splits[3], 1), 0, CB - 1).astype(jnp.int32)
    dst_blocks = touch_ends(jax.random.randint(splits[4], (N_FX * N_FY, N_FX * N_FY, CAP), 0, DB), jax.random.fold_in(splits[4], 1), 0, DB - 1).astype(jnp.int32)
    weight_rows = touch_ends(jax.random.randint(splits[5], (N_FX * N_FY, N_FX * N_FY, CAP), 0, K), jax.random.fold_in(splits[5], 1), 0, K - 1).astype(jnp.int32)
    counts = draw_counts(jax.random.fold_in(splits[14], 71), 0)
    brackets = touch_ends(jax.random.randint(splits[7], (P_SIZE,), 0, LEV - 1), jax.random.fold_in(splits[7], 1), 0, (LEV - 1) - 1).astype(jnp.int32)
    fractions = jnp.clip(jax.random.uniform(splits[8], (P_SIZE,), jnp.float32, 0.0, 1.0), 0.0, 1.0)
    w_in = normal_values(splits[9], (HID, VP), VP ** -0.5, 1.0)
    b_in = normal_values(splits[10], (HID,), 1.0, 4.0, (), jnp.float32)
    w_mid = normal_values(splits[11], (HID, HID), HID ** -0.5, 0.25)
    b_mid = normal_values(splits[12], (HID,), 1.0, 4.0, (), jnp.float32)
    w_out = normal_values(splits[13], (VP, HID), HID ** -0.5, 0.25)
    return dict(state=state, coef=coef, weight_table=weight_table, src_blocks=src_blocks, dst_blocks=dst_blocks, weight_rows=weight_rows, counts=counts, brackets=brackets, fractions=fractions, w_in=w_in, b_in=b_in, w_mid=w_mid, b_mid=b_mid, w_out=w_out)


HIGH_ACCURACY = lax.Precision.HIGHEST


def level_matrix(brackets, fractions, levels):
    cols = jnp.arange(levels, dtype=jnp.int32)
    lower = (cols[None, :] == brackets[:, None]).astype(jnp.float32)
    upper = (cols[None, :] == brackets[:, None] + 1).astype(jnp.float32)
    return lower * (1.0 - fractions[:, None]) + upper * fractions[:, None]


def apply_levels(values, remap_matrix):
    levels = remap_matrix.shape[1]
    lead = values.shape[:-2]
    width = values.shape[-1]
    divided_parts = values.reshape(lead + (values.shape[-2] // levels, levels, width))
    relocated_rows = jnp.einsum("fm,...qme->...qfe", remap_matrix, divided_parts, precision=HIGH_ACCURACY)
    return relocated_rows.reshape(lead + (-1, width))


def remap_blocks(rows, indices, table, transpose):
    total = rows.shape[0]
    group = min(64, total)
    rows_grouped = rows.reshape((total // group, group) + rows.shape[1:])
    index_grouped = indices.reshape(total // group, group)

    def one_group(pair):
        part, index = pair
        remap_matrices = jnp.take(table, index, axis=0)
        if transpose:
            return jnp.einsum("kbl,krl->kbr", part, remap_matrices, precision=HIGH_ACCURACY)
        return jnp.einsum("vrb,vbm->vrm", part, remap_matrices, precision=HIGH_ACCURACY)

    return lax.map(one_group, (rows_grouped, index_grouped)).reshape(rows.shape[:2] + (table.shape[2],))


def column_network(latlon, w_in, b_in, w_mid, b_mid, w_out):
    inputs = latlon.astype(jnp.bfloat16)
    first = jnp.einsum("hf,dfc->dhc", w_in, inputs, preferred_element_type=jnp.float32)
    first = jax.nn.gelu(first + b_in[None, :, None], approximate=True).astype(jnp.bfloat16)
    second = jnp.einsum("hk,dkc->dhc", w_mid, first, preferred_element_type=jnp.float32)
    second = jax.nn.gelu(second + b_mid[None, :, None], approximate=True).astype(jnp.bfloat16)
    return jnp.einsum("fh,dhc->dfc", w_out, second, preferred_element_type=jnp.float32)


def reference(state, coef, weight_table, src_blocks, dst_blocks, weight_rows, counts, brackets, fractions, w_in, b_in, w_mid, b_mid, w_out):
    field = state
    for sweep_index in range(SWEEPS):
        padded = jnp.pad(field, ((1, 1), (0, 0), (0, 0)))
        beside_all = jnp.roll(field, 1, axis=2) + jnp.roll(field, -1, axis=2)
        beside_all = beside_all + padded[2:] + padded[:-2]
        field = field + coef[:, None, :] * (beside_all - 4.0 * field)
    diffused_state = field
    ndev = N_FX * N_FY
    remap_matrix = level_matrix(brackets, fractions, LEV)
    on_pressure = apply_levels(diffused_state, remap_matrix)
    blocks = on_pressure.reshape(N_FY, CB, V * P_SIZE, N_FX, CA).transpose(3, 0, 1, 2, 4).reshape(ndev, CB, V * P_SIZE, CA)
    slots = jnp.arange(CAP, dtype=jnp.int32)
    owners = jnp.arange(ndev, dtype=jnp.int32)

    def forward(carry, inputs):
        dev_blocks, sources, targets, rows, used = inputs
        valid = (slots[None, :] < used[:, None]).astype(jnp.float32).reshape(-1)
        picked = jnp.take(dev_blocks, sources.reshape(-1), axis=0)
        values = remap_blocks(picked, rows.reshape(-1), weight_table, False) * valid[:, None, None]
        where = (owners[:, None] * DB + targets).reshape(-1)
        return carry.at[where].add(values), None

    start = jnp.zeros((ndev * DB, V * P_SIZE, CA), jnp.float32)
    latlon, unused = lax.scan(forward, start, (blocks, src_blocks, dst_blocks, weight_rows, counts))
    per_owner = latlon.reshape(ndev, DB, V * P_SIZE, CA)
    column_tend = lax.map(lambda band: column_network(band, w_in, b_in, w_mid, b_mid, w_out), per_owner)
    column_tend = column_tend.reshape(ndev * DB, V * P_SIZE, CA)

    def backward(carry, inputs):
        sources, targets, rows, used = inputs
        valid = (slots[None, :] < used[:, None]).astype(jnp.float32).reshape(-1)
        where = (owners[:, None] * DB + targets).reshape(-1)
        back = jnp.take(column_tend, where, axis=0)
        contrib = remap_blocks(back, rows.reshape(-1), weight_table, True) * valid[:, None, None]
        contrib = apply_levels(contrib, remap_matrix.T)
        dev_tend = jnp.zeros((CB, V * LEV, CA), jnp.float32).at[sources.reshape(-1)].add(contrib)
        return carry, dev_tend

    unused_two, dev_tends = lax.scan(backward, jnp.zeros((), jnp.float32), (src_blocks, dst_blocks, weight_rows, counts))
    tendency = dev_tends.reshape(N_FX, N_FY, CB, V * LEV, CA).transpose(1, 2, 3, 0, 4).reshape(CB * N_FY, V * LEV, CA * N_FX)
    return diffused_state, tendency
```

```python
import functools

import jax
import jax.numpy as jnp
from jax import lax
from jax.experimental import pallas as pl
from jax.experimental.pallas import tpu as pltpu
from jax.sharding import PartitionSpec as P

SWEEPS = 4
VMEM_LIMIT = 48 * 1024 * 1024
F32 = jnp.float32
BF16 = jnp.bfloat16
HIGHEST = lax.Precision.HIGHEST

VMEM_SPEC = pl.BlockSpec(memory_space=pltpu.VMEM)
SMEM_SPEC = pl.BlockSpec(memory_space=pltpu.SMEM)


def params():
    return pltpu.CompilerParams(vmem_limit_bytes=VMEM_LIMIT)


def pack_kernel(nrows, nlev, width, state, coef, top, bottom, first_out, last_out):
    halo = SWEEPS
    lane = lax.broadcasted_iota(jnp.int32, (nlev, width), 1)
    group = lane // halo
    lane_one = lax.broadcasted_iota(jnp.int32, (1, width), 1)
    group_one = lane_one // halo

    def rows_of(e):
        if e < halo:
            return top[e * nlev : (e + 1) * nlev, :], top[halo * nlev + e : halo * nlev + e + 1, :]
        if e < halo + nrows:
            return state[e - halo], coef[e - halo : e - halo + 1, :]
        b = e - halo - nrows
        return bottom[b * nlev : (b + 1) * nlev, :], bottom[halo * nlev + b : halo * nlev + b + 1, :]

    per = width // halo
    total = nrows + 2 * halo
    tiles = -(-total // per)
    first_out[...] = jnp.zeros_like(first_out)
    last_out[...] = jnp.zeros_like(last_out)
    for tile in range(tiles):
        first = jnp.zeros((nlev, width), F32)
        last = jnp.zeros((nlev, width), F32)
        first_c = jnp.zeros((1, width), F32)
        last_c = jnp.zeros((1, width), F32)
        for i in range(min(per, total - tile * per)):
            field, number = rows_of(tile * per + i)
            at = (halo * i) % width
            up = (halo * i + halo) % width
            first = jnp.where(group == i, pltpu.roll(field, at, 1) if at else field, first)
            last = jnp.where(group == i, pltpu.roll(field, up, 1) if up else field, last)
            first_c = jnp.where(group_one == i, pltpu.roll(number, at, 1) if at else number, first_c)
            last_c = jnp.where(group_one == i, pltpu.roll(number, up, 1) if up else number, last_c)
        first_out[tile * nlev : (tile + 1) * nlev, :] = first
        last_out[tile * nlev : (tile + 1) * nlev, :] = last
        first_out[tiles * nlev + tile : tiles * nlev + tile + 1, :] = first_c
        last_out[tiles * nlev + tile : tiles * nlev + tile + 1, :] = last_c


def sweep_kernel(
    nrows, nlev, width, state, coef, top, bottom, left, right, levels, field_out, source_out, a, b, c
):
    halo = SWEEPS
    per = width // halo
    total = nrows + 2 * halo
    tiles = -(-total // per)
    lane = lax.broadcasted_iota(jnp.int32, (nlev, width), 1)
    lane_one = lax.broadcasted_iota(jnp.int32, (1, width), 1)
    for e in range(total):
        if e < halo:
            field = top[e * nlev : (e + 1) * nlev, :]
            number = top[halo * nlev + e : halo * nlev + e + 1, :]
        elif e < halo + nrows:
            field = state[e - halo]
            number = coef[e - halo : e - halo + 1, :]
        else:
            r = e - halo - nrows
            field = bottom[r * nlev : (r + 1) * nlev, :]
            number = bottom[halo * nlev + r : halo * nlev + r + 1, :]
        tile, i = e // per, e % per
        to_low = (width - halo * i) % width
        to_high = (width - halo - halo * i) % width
        edges = []
        for where_, rows in ((lane, slice(tile * nlev, (tile + 1) * nlev)),
                             (lane_one, slice(tiles * nlev + tile, tiles * nlev + tile + 1))):
            r_tile = right[rows, :]
            l_tile = left[rows, :]
            r_part = pltpu.roll(r_tile, to_low, 1) if to_low else r_tile
            l_part = pltpu.roll(l_tile, to_high, 1) if to_high else l_tile
            edges.append(
                jnp.where(where_ < halo, r_part, jnp.where(where_ >= width - halo, l_part, 0.0))
            )
        a[e, :, 0:width] = field
        a[e, :, width : 2 * width] = edges[0]
        c[e, :, 0:width] = number
        c[e, :, width : 2 * width] = edges[1]

    def step(source, e):
        mid = source[e]
        beside = pltpu.roll(mid, 1, 1) + pltpu.roll(mid, 2 * width - 1, 1)
        beside = beside + source[e + 1] + source[e - 1]
        return mid + c[e] * (beside - 4.0 * mid)

    held, other = a, b
    for sweep in range(1, SWEEPS):

        def one(e, carry, held=held, other=other):
            other[e] = step(held, e)
            return carry

        lax.fori_loop(sweep, total - sweep, one, 0)
        held, other = other, held

    def final(r, carry):
        done = step(held, r + halo)[:, 0:width]
        field_out[r] = done
        source_out[r] = jnp.dot(
            levels[...], done, precision=HIGHEST, preferred_element_type=F32
        )
        return carry

    lax.fori_loop(0, nrows, final, 0)


def diffuse(state, coef, levels):
    nrows, nlev, width = state.shape
    halo = SWEEPS
    per = width // halo
    total = nrows + 2 * halo
    tiles = -(-total // per)
    nx, ny = lax.axis_size("fx"), lax.axis_size("fy")
    pad = -halo % 8
    blank = jnp.zeros((pad, width), F32)

    def row_message(rows):
        return jnp.concatenate(
            [state[rows].reshape(halo * nlev, width), coef[rows], blank], axis=0
        )

    down = [(i, i + 1) for i in range(ny - 1)]
    up = [(i + 1, i) for i in range(ny - 1)]
    top = lax.ppermute(row_message(slice(nrows - halo, nrows)), "fy", down)
    bottom = lax.ppermute(row_message(slice(0, halo)), "fy", up)
    edge = jax.ShapeDtypeStruct((tiles * nlev + 8, width), F32)
    first, last = pl.pallas_call(
        functools.partial(pack_kernel, nrows, nlev, width),
        out_shape=(edge, edge),
        in_specs=[VMEM_SPEC] * 4,
        out_specs=(VMEM_SPEC, VMEM_SPEC),
        compiler_params=params(),
        name="pack_edges",
    )(state, coef, top, bottom)
    ahead = [(i, (i + 1) % nx) for i in range(nx)]
    behind = [((i + 1) % nx, i) for i in range(nx)]
    left = lax.ppermute(last, "fx", ahead)
    right = lax.ppermute(first, "fx", behind)
    return pl.pallas_call(
        functools.partial(sweep_kernel, nrows, nlev, width),
        out_shape=(
            jax.ShapeDtypeStruct(state.shape, F32),
            jax.ShapeDtypeStruct((nrows, levels.shape[0], width), F32),
        ),
        in_specs=[VMEM_SPEC] * 7,
        out_specs=(VMEM_SPEC, VMEM_SPEC),
        scratch_shapes=[
            pltpu.VMEM((total, nlev, 2 * width), F32),
            pltpu.VMEM((total, nlev, 2 * width), F32),
            pltpu.VMEM((total, 1, 2 * width), F32),
        ],
        compiler_params=params(),
        name="sweeps",
    )(state, coef, top, bottom, left, right, levels)


def split(value):
    high = value.astype(BF16)
    low = (value - high.astype(F32)).astype(BF16)
    return high, low


def table_kernel(table, plain, turned):
    for k in range(table.shape[0]):
        weights = table[k]
        high, low = split(weights)
        plain[k, :, 0:128] = high
        plain[k, :, 128:256] = low
        high, low = split(weights.T)
        turned[k, :, 0:128] = high
        turned[k, :, 128:256] = low


def split_tables(table):
    count, rows, width = table.shape
    group = 8
    shape = jax.ShapeDtypeStruct((count, rows, 2 * width), BF16)
    return pl.pallas_call(
        table_kernel,
        grid=(count // group,),
        out_shape=(shape, shape),
        in_specs=[pl.BlockSpec((group, rows, width), lambda i: (i, 0, 0))],
        out_specs=(
            pl.BlockSpec((group, rows, 2 * width), lambda i: (i, 0, 0)),
            pl.BlockSpec((group, rows, 2 * width), lambda i: (i, 0, 0)),
        ),
        compiler_params=params(),
        name="split_tables",
    )(table)


UNROLL = 4


def list_kernel(groups, owners, cap, blocks, takes, gives, rows, counts, from_, to, which, number):
    def pair(i, at):
        g = i // owners
        o = i % owners
        for c in range(cap):
            from_[at + c] = g * blocks + takes[i, c]
            to[at + c] = o * blocks + gives[i, c]
            which[at + c] = rows[i, c]
        return at + counts[i, 0]

    end = lax.fori_loop(0, groups * owners, pair, 0)
    for c in range(UNROLL):
        from_[end + c] = 0
        to[end + c] = owners * blocks
        which[end + c] = 0
    number[0] = (end + UNROLL - 1) // UNROLL


def slot_list(takes, gives, rows, counts, blocks):
    groups, owners, cap = takes.shape
    size = groups * owners * cap + 2 * UNROLL
    one = jax.ShapeDtypeStruct((size,), jnp.int32)
    pairs = groups * owners
    return pl.pallas_call(
        functools.partial(list_kernel, groups, owners, cap, blocks),
        out_shape=(one, one, one, jax.ShapeDtypeStruct((1,), jnp.int32)),
        in_specs=[SMEM_SPEC] * 4,
        out_specs=(SMEM_SPEC,) * 4,
        name="slot_list",
    )(
        takes.reshape(pairs, cap),
        gives.reshape(pairs, cap),
        rows.reshape(pairs, cap),
        counts.reshape(pairs, 1),
    )


def remap_kernel(number, from_, to, which, blocks, tables, out, total):
    features, width = blocks.shape[1:]
    total[...] = jnp.zeros_like(total)

    def group(i, carry):
        products = []
        for u in range(UNROLL):
            s = i * UNROLL + u
            value = blocks[from_[s]]
            high = value.astype(BF16).astype(F32)
            both = jnp.concatenate([high, value - high], axis=0).astype(BF16)
            r = jnp.dot(both, tables[which[s]], preferred_element_type=F32)
            products.append(
                r[:features, :width] + r[:features, width:] + r[features:, :width]
            )
        for u in range(UNROLL):
            t = to[i * UNROLL + u]
            total[t] = total[t] + products[u]
        return carry

    lax.fori_loop(0, number[0], group, 0)
    out[...] = total[0 : out.shape[0]]


def remap(slots, blocks, tables, count):
    from_, to, which, number = slots
    shape = (count,) + blocks.shape[1:]
    return pl.pallas_call(
        remap_kernel,
        out_shape=jax.ShapeDtypeStruct(shape, F32),
        in_specs=[SMEM_SPEC] * 4 + [VMEM_SPEC] * 2,
        out_specs=VMEM_SPEC,
        scratch_shapes=[pltpu.VMEM((count + 1,) + blocks.shape[1:], F32)],
        compiler_params=params(),
        name="remap",
    )(number, from_, to, which, blocks, tables)


def gelu(x):
    inner = x * (0.7978845608028654 + (0.7978845608028654 * 0.044715) * (x * x))
    half = 0.5 * x
    return half + half * jnp.tanh(inner)


def network_kernel(latlon, w_in, b_in, w_mid, b_mid, w_out, out):
    def pair(i, carry):
        x = jnp.concatenate([latlon[2 * i], latlon[2 * i + 1]], axis=1).astype(BF16)
        first = jnp.dot(w_in[...], x, preferred_element_type=F32) + b_in[...]
        first = gelu(first).astype(BF16)
        second = jnp.dot(w_mid[...], first, preferred_element_type=F32) + b_mid[...]
        second = gelu(second).astype(BF16)
        tend = jnp.dot(w_out[...], second, preferred_element_type=F32)
        width = latlon.shape[2]
        out[2 * i] = tend[:, :width]
        out[2 * i + 1] = tend[:, width:]
        return carry

    lax.fori_loop(0, latlon.shape[0] // 2, pair, 0)


def column_network(latlon, w_in, b_in, w_mid, b_mid, w_out):
    return pl.pallas_call(
        network_kernel,
        out_shape=jax.ShapeDtypeStruct(latlon.shape, F32),
        in_specs=[VMEM_SPEC] * 6,
        out_specs=VMEM_SPEC,
        compiler_params=params(),
        name="column_network",
    )(latlon, w_in, b_in[:, None], w_mid, b_mid[:, None], w_out)


def raise_kernel(values, levels, out):
    for b in range(values.shape[0]):
        out[b] = jnp.dot(levels[...], values[b], precision=HIGHEST, preferred_element_type=F32)


def raise_levels(values, levels):
    return pl.pallas_call(
        raise_kernel,
        out_shape=jax.ShapeDtypeStruct(
            (values.shape[0], levels.shape[0], values.shape[2]), F32
        ),
        in_specs=[VMEM_SPEC] * 2,
        out_specs=VMEM_SPEC,
        compiler_params=params(),
        name="raise_levels",
    )(values, levels)


def level_matrix(brackets, fractions, nlev, variables, features):
    levels = nlev // variables
    cols = jnp.arange(levels, dtype=jnp.int32)
    lower = (cols[None, :] == brackets[:, None]).astype(F32)
    upper = (cols[None, :] == brackets[:, None] + 1).astype(F32)
    one = lower * (1.0 - fractions[:, None]) + upper * fractions[:, None]
    whole = (jnp.eye(variables, dtype=F32)[:, None, :, None] * one[None, :, None, :]).reshape(
        variables * one.shape[0], nlev
    )
    return jnp.pad(whole, ((0, features - whole.shape[0]), (0, 0)))


def per_device(
    state,
    coef,
    weight_table,
    src_blocks,
    dst_blocks,
    weight_rows,
    counts,
    brackets,
    fractions,
    w_in,
    b_in,
    w_mid,
    b_mid,
    w_out,
):
    nblocks, nlev, width = state.shape
    used_features = w_in.shape[1]
    features = -(-used_features // 8) * 8
    variables = used_features // brackets.shape[0]
    nx, ny = lax.axis_size("fx"), lax.axis_size("fy")
    mx, my = lax.axis_index("fx"), lax.axis_index("fy")
    ndev, cap = src_blocks.shape[1:]

    levels = level_matrix(brackets, fractions, nlev, variables, features)
    lists = jnp.concatenate(
        [src_blocks[0], dst_blocks[0], weight_rows[0], counts[0][:, None]], axis=1
    )
    along_x = lax.all_gather(lists, "fx", axis=0).reshape(nx, nx, ny, 3 * cap + 1)
    along_x = lax.dynamic_index_in_dim(along_x, mx, 1, keepdims=False)
    along_y = lax.all_gather(lists, "fy", axis=0).reshape(ny, nx, ny, 3 * cap + 1)
    along_y = lax.dynamic_index_in_dim(along_y, my, 2, keepdims=False)

    def parts(t):
        return t[..., :cap], t[..., cap : 2 * cap], t[..., 2 * cap : 3 * cap], t[..., 3 * cap]

    src, dst, row, cnt = parts(along_x)
    out_slots = slot_list(src, dst, row, cnt, nblocks)
    src, dst, row, cnt = (jnp.swapaxes(t, 0, 1) for t in parts(along_y))
    back_slots = slot_list(dst, src, row, cnt, nblocks)
    plain, turned = split_tables(weight_table)

    field, source = diffuse(state, coef, levels)
    gathered = lax.all_gather(source, "fx", axis=0, tiled=True)
    sums = remap(out_slots, gathered, plain, ny * nblocks)
    latlon = lax.psum_scatter(sums, "fy", scatter_dimension=0, tiled=True)
    spare = features - used_features
    tend = column_network(
        latlon,
        jnp.pad(w_in, ((0, 0), (0, spare))),
        b_in,
        w_mid,
        b_mid,
        jnp.pad(w_out, ((0, spare), (0, 0))),
    )
    back = lax.all_gather(tend, "fx", axis=0, tiled=True)
    sums = remap(back_slots, back, turned, ny * nblocks)
    returned = lax.psum_scatter(sums, "fy", scatter_dimension=0, tiled=True)
    return field, raise_levels(returned, levels.T)


def solution(mesh):
    placed = (
        P("fy", None, "fx"),
        P("fy", "fx"),
        P(),
        P(("fx", "fy"), None, None),
        P(("fx", "fy"), None, None),
        P(("fx", "fy"), None, None),
        P(("fx", "fy"), None),
        P(),
        P(),
        P(),
        P(),
        P(),
        P(),
        P(),
    )
    return jax.shard_map(
        per_device,
        mesh=mesh,
        in_specs=placed,
        out_specs=(P("fy", None, "fx"), P("fy", None, "fx")),
        check_vma=False,
    )
```

```python
import functools
import math

import jax
import jax.numpy as jnp
from jax import lax
from jax.experimental import pallas as pl
from jax.experimental.pallas import tpu as pltpu
from jax.sharding import PartitionSpec as P

SWEEPS = 4
ROWS = 4
F32 = jnp.float32
BF16 = jnp.bfloat16
HIGHEST = lax.Precision.HIGHEST

VMEM_SPEC = pl.BlockSpec(memory_space=pltpu.VMEM)
HBM_SPEC = pl.BlockSpec(memory_space=pltpu.HBM)
SMEM_SPEC = pl.BlockSpec(memory_space=pltpu.SMEM)


def params(mebibytes=32):
    return pltpu.CompilerParams(vmem_limit_bytes=mebibytes * 1024 * 1024)


def cost(microseconds):
    return pl.CostEstimate(
        flops=0, transcendentals=0, bytes_accessed=int(microseconds * 3_000_000)
    )


def pack_kernel(nrows, nlev, width, state, coef, top, bottom, first_out, last_out):
    halo = SWEEPS
    lane = lax.broadcasted_iota(jnp.int32, (nlev, width), 1)
    group = lane // halo
    lane_one = lax.broadcasted_iota(jnp.int32, (1, width), 1)
    group_one = lane_one // halo

    def rows_of(e):
        if e < halo:
            return top[e * nlev : (e + 1) * nlev, :], top[halo * nlev + e : halo * nlev + e + 1, :]
        if e < halo + nrows:
            return state[e - halo], coef[e - halo : e - halo + 1, :]
        b = e - halo - nrows
        return bottom[b * nlev : (b + 1) * nlev, :], bottom[halo * nlev + b : halo * nlev + b + 1, :]

    per = width // halo
    total = nrows + 2 * halo
    tiles = -(-total // per)
    first_out[...] = jnp.zeros_like(first_out)
    last_out[...] = jnp.zeros_like(last_out)
    for tile in range(tiles):
        first = jnp.zeros((nlev, width), F32)
        last = jnp.zeros((nlev, width), F32)
        first_c = jnp.zeros((1, width), F32)
        last_c = jnp.zeros((1, width), F32)
        for i in range(min(per, total - tile * per)):
            field, number = rows_of(tile * per + i)
            at = (halo * i) % width
            up = (halo * i + halo) % width
            first = jnp.where(group == i, pltpu.roll(field, at, 1) if at else field, first)
            last = jnp.where(group == i, pltpu.roll(field, up, 1) if up else field, last)
            first_c = jnp.where(group_one == i, pltpu.roll(number, at, 1) if at else number, first_c)
            last_c = jnp.where(group_one == i, pltpu.roll(number, up, 1) if up else number, last_c)
        first_out[tile * nlev : (tile + 1) * nlev, :] = first
        last_out[tile * nlev : (tile + 1) * nlev, :] = last
        first_out[tiles * nlev + tile : tiles * nlev + tile + 1, :] = first_c
        last_out[tiles * nlev + tile : tiles * nlev + tile + 1, :] = last_c


def sweep_kernel(
    nrows, nlev, width, state, coef, top, bottom, left, right, levels, marks, field_out, source_out, a, b, c
):
    halo = SWEEPS
    per = width // halo
    total = nrows + 2 * halo
    tiles = -(-total // per)
    lane = lax.broadcasted_iota(jnp.int32, (nlev, width), 1)
    lane_one = lax.broadcasted_iota(jnp.int32, (1, width), 1)
    for e in range(total):
        if e < halo:
            field = top[e * nlev : (e + 1) * nlev, :]
            number = top[halo * nlev + e : halo * nlev + e + 1, :]
        elif e < halo + nrows:
            field = state[e - halo]
            number = coef[e - halo : e - halo + 1, :]
        else:
            r = e - halo - nrows
            field = bottom[r * nlev : (r + 1) * nlev, :]
            number = bottom[halo * nlev + r : halo * nlev + r + 1, :]
        tile, i = e // per, e % per
        to_low = (width - halo * i) % width
        to_high = (width - halo - halo * i) % width
        edges = []
        for where_, rows in ((lane, slice(tile * nlev, (tile + 1) * nlev)),
                             (lane_one, slice(tiles * nlev + tile, tiles * nlev + tile + 1))):
            r_tile = right[rows, :]
            l_tile = left[rows, :]
            r_part = pltpu.roll(r_tile, to_low, 1) if to_low else r_tile
            l_part = pltpu.roll(l_tile, to_high, 1) if to_high else l_tile
            edges.append(
                jnp.where(where_ < halo, r_part, jnp.where(where_ >= width - halo, l_part, 0.0))
            )
        a[e, :, 0:width] = field
        a[e, :, width : 2 * width] = edges[0]
        c[e, :, 0:width] = number
        c[e, :, width : 2 * width] = edges[1]

    def step(source, e):
        mid = source[e]
        beside = pltpu.roll(mid, 1, 1) + pltpu.roll(mid, 2 * width - 1, 1)
        beside = beside + source[e + 1] + source[e - 1]
        return mid + c[e] * (beside - 4.0 * mid)

    held, other = a, b
    for sweep in range(1, SWEEPS):
        low, high = sweep, total - sweep
        steps = (high - low) // ROWS

        def some(i, carry, held=held, other=other, low=low):
            done = [step(held, low + i * ROWS + r) for r in range(ROWS)]
            for r in range(ROWS):
                other[low + i * ROWS + r] = done[r]
            return carry

        lax.fori_loop(0, steps, some, 0)
        for e in range(low + steps * ROWS, high):
            other[e] = step(held, e)
        held, other = other, held

    def final(i, carry):
        done = [step(held, i * ROWS + r + halo)[:, 0:width] for r in range(ROWS)]
        for r in range(ROWS):
            field_out[i * ROWS + r] = done[r]
        for r in range(0, ROWS, 2):
            pair = jnp.concatenate([done[r], done[r + 1]], axis=1)
            lowered = jnp.dot(
                levels[...], pair, precision=HIGHEST, preferred_element_type=F32
            )
            source_out[i * ROWS + r] = lowered[:, :width]
            source_out[i * ROWS + r + 1] = lowered[:, width:]
        return carry

    lax.fori_loop(0, nrows // ROWS, final, 0)
    spare = levels.shape[0] - 1
    for b in range(marks.shape[0]):
        source_out[b, spare : spare + 1, :] = marks[b : b + 1, :]


def diffuse(state, coef, levels, marks):
    nrows, nlev, width = state.shape
    halo = SWEEPS
    per = width // halo
    total = nrows + 2 * halo
    tiles = -(-total // per)
    nx, ny = lax.axis_size("fx"), lax.axis_size("fy")
    pad = -halo % 8
    blank = jnp.zeros((pad, width), F32)

    def row_message(rows):
        return jnp.concatenate(
            [state[rows].reshape(halo * nlev, width), coef[rows], blank], axis=0
        )

    down = [(i, i + 1) for i in range(ny - 1)]
    up = [(i + 1, i) for i in range(ny - 1)]
    top = lax.ppermute(row_message(slice(nrows - halo, nrows)), "fy", down)
    bottom = lax.ppermute(row_message(slice(0, halo)), "fy", up)
    edge = jax.ShapeDtypeStruct((tiles * nlev + 8, width), F32)
    first, last = pl.pallas_call(
        functools.partial(pack_kernel, nrows, nlev, width),
        out_shape=(edge, edge),
        in_specs=[VMEM_SPEC] * 4,
        out_specs=(VMEM_SPEC, VMEM_SPEC),
        compiler_params=params(),
        cost_estimate=cost(1),
        name="pack_edges",
    )(state, coef, top, bottom)
    ahead = [(i, (i + 1) % nx) for i in range(nx)]
    behind = [((i + 1) % nx, i) for i in range(nx)]
    left = lax.ppermute(last, "fx", ahead)
    right = lax.ppermute(first, "fx", behind)
    return pl.pallas_call(
        functools.partial(sweep_kernel, nrows, nlev, width),
        out_shape=(
            jax.ShapeDtypeStruct(state.shape, F32),
            jax.ShapeDtypeStruct((nrows, levels.shape[0], width), F32),
        ),
        in_specs=[VMEM_SPEC] * 8,
        out_specs=(VMEM_SPEC, VMEM_SPEC),
        scratch_shapes=[
            pltpu.VMEM((total, nlev, 2 * width), F32),
            pltpu.VMEM((total, nlev, 2 * width), F32),
            pltpu.VMEM((total, 1, 2 * width), F32),
        ],
        compiler_params=params(),
        cost_estimate=cost(9),
        name="sweeps",
    )(state, coef, top, bottom, left, right, levels, marks)


def split(value):
    high = value.astype(BF16)
    low = (value - high.astype(F32)).astype(BF16)
    return high, low


def table_kernel(turn, table, out):
    count, rows, width = table.shape
    for k in range(count):
        weights = table[k].T if turn else table[k]
        high, low = split(weights)
        out[k, :, 0:width] = high
        out[k, :, width:] = low
    out[count] = jnp.zeros((rows, 2 * width), BF16)


def split_table(table, turn):
    count, rows, width = table.shape
    return pl.pallas_call(
        functools.partial(table_kernel, turn),
        out_shape=jax.ShapeDtypeStruct((count + 1, rows, 2 * width), BF16),
        in_specs=[VMEM_SPEC],
        out_specs=VMEM_SPEC,
        compiler_params=params(),
        cost_estimate=cost(3),
        name="split_table",
    )(table)


UNROLL = 8


PLACES = 40


def list_kernel(zero_row, values, valid, table):
    sets, room = valid.shape
    fields = values.shape[1] // room
    slot = lax.broadcasted_iota(jnp.int32, (fields * room, room), 0)
    other = lax.broadcasted_iota(jnp.int32, (fields * room, room), 1)
    within = slot % room
    transposed = (((1,), (1,)), ((), ()))

    def spread_out(chosen):
        return lax.dot_general(
            chosen.astype(F32), valid[...], transposed, preferred_element_type=F32
        )

    ahead = spread_out(other < within)
    first = lax.broadcasted_iota(jnp.int32, ahead.shape, 0) // room * PLACES + 1
    place = jnp.where(spread_out(other == within) > 0.5, ahead.astype(jnp.int32) + first, -1)
    lane = lax.broadcasted_iota(jnp.int32, (fields * room, 128), 1)
    for s in range(sets):
        chosen = (place[:, s : s + 1] == lane).astype(F32)
        table[s : s + 1, :] = jnp.dot(
            values[s : s + 1, :], chosen, preferred_element_type=F32
        )
    lane = lax.broadcasted_iota(jnp.int32, table.shape, 1)
    weight_lane = (lane > 2 * PLACES) & (lane <= 3 * PLACES)
    rows = jnp.where(weight_lane, table[...] + float(zero_row), table[...])
    number = jnp.sum(valid[...], axis=1, keepdims=True)
    table[...] = jnp.where(lane == 0, number, rows)


def slot_table(src, dst, row, count, blocks, zero_row, forward):
    sets, groups, cap = src.shape
    valid = (jnp.arange(cap, dtype=F32)[None, None, :] < count[:, :, None]).astype(F32)
    taken, given = (src, dst) if forward else (dst, src)
    given = given + blocks * jnp.arange(groups, dtype=F32)[None, :, None]
    values = jnp.stack([taken, given, row - zero_row], axis=1).reshape(sets, 3 * groups * cap)
    return pl.pallas_call(
        functools.partial(list_kernel, zero_row),
        out_shape=jax.ShapeDtypeStruct((sets, 128), F32),
        in_specs=[VMEM_SPEC] * 2,
        out_specs=VMEM_SPEC,
        cost_estimate=cost(1),
        name="slot_table",
    )(values, valid.reshape(sets, groups * cap))


def own_kernel(groups, blocks, zero_row, src, dst, row, counts, table):
    cap, owners = src.shape
    sets = table.shape[0]
    lane = lax.broadcasted_iota(jnp.int32, (owners, owners), 1)
    below = lax.broadcasted_iota(jnp.int32, (owners, owners), 0)
    same = lane // groups == below // groups
    number = counts[...].astype(F32)
    ahead = jnp.dot(number, (same & (below < lane)).astype(F32), preferred_element_type=F32)
    keys = [jnp.where(c < counts[...], ahead.astype(jnp.int32) + 1 + c, -1) for c in range(cap)]
    keys = jnp.concatenate(keys + [jnp.zeros((8 - cap, owners), jnp.int32)], axis=0).astype(F32)
    keys = keys.T.astype(jnp.int32)
    mine = lax.broadcasted_iota(jnp.int32, (sets, owners), 1) // groups == lax.broadcasted_iota(
        jnp.int32, (sets, owners), 0
    )
    which = lax.broadcasted_iota(jnp.int32, (1, owners), 1) % groups
    rows = jnp.zeros((sets, owners), F32)
    for c in range(cap):
        key = keys[:, c : c + 1]
        for f, value in enumerate(
            (src[c : c + 1, :], dst[c : c + 1, :] + which * blocks, row[c : c + 1, :] - zero_row)
        ):
            chosen = ((lane == key + f * PLACES) & (key > 0)).astype(F32)
            held = jnp.where(mine, value.astype(F32), 0.0)
            rows = rows + jnp.dot(held, chosen, preferred_element_type=F32)
    place = lax.broadcasted_iota(jnp.int32, rows.shape, 1)
    rows = jnp.where((place > 2 * PLACES) & (place <= 3 * PLACES), rows + float(zero_row), rows)
    used = jnp.sum(jnp.where(mine, number, 0.0), axis=1, keepdims=True)
    table[...] = jnp.where(place == 0, used, rows)


def own_table(src, dst, row, counts, groups, blocks, zero_row):
    owners = counts.shape[1]
    return pl.pallas_call(
        functools.partial(own_kernel, groups, blocks, zero_row),
        out_shape=jax.ShapeDtypeStruct((owners // groups, owners), F32),
        in_specs=[VMEM_SPEC] * 4,
        out_specs=VMEM_SPEC,
        cost_estimate=cost(1),
        name="own_table",
    )(src[0].T, dst[0].T, row[0].T, counts)


def remap_kernel(first, sizes, own_rows, slots, order, lines, tables, *refs):
    arrays, refs = refs[: len(sizes)], refs[len(sizes) :]
    if not first:
        start, refs = refs[0], refs[1:]
    outs, refs = (refs[:1], refs[1:]) if first else (refs[:4], refs[4:])
    blocks, weights, total, products, held_rows, scalars, sems, late_sems = refs[:8]
    features, width = total.shape[1:]
    copies, at = [], 0
    for k, size in enumerate(sizes):
        copies.append(pltpu.make_async_copy(arrays[k], blocks.at[at : at + size], sems.at[k]))
        at += size
    copies.append(pltpu.make_async_copy(tables, weights, sems.at[len(sizes)]))
    for copy in copies:
        copy.start()
    if not first:
        started = refs[8]
        fetch = pltpu.make_async_copy(start, started, late_sems.at[0])
        fetch.start()
    total[...] = jnp.zeros_like(total)
    products[...] = jnp.zeros_like(products)
    for copy in copies:
        copy.wait()
    sets = order.shape[0]
    size = blocks.shape[0] // sets
    if own_rows:
        for p in range(sets):
            held_rows[p : p + 1, :] = blocks[
                p * size + slots[0], features - 1 : features, :
            ].astype(jnp.int32)
        rows_copy = pltpu.make_async_copy(held_rows, scalars, late_sems.at[1])
        rows_copy.start()
        rows_copy.wait()
        slots = scalars

    def add(row, i):
        held = [products[u] for u in range(UNROLL)]
        for u in range(UNROLL):
            t = slots[row, 1 + PLACES + i * UNROLL + u]
            total[t] = total[t] + held[u]

    def one_set(p, carry):
        row = order[p]

        def group(i, carry):
            made = []
            for u in range(UNROLL):
                value = blocks[p * size + slots[row, 1 + i * UNROLL + u]]
                high = value.astype(BF16).astype(F32)
                both = jnp.concatenate([high, value - high], axis=0).astype(BF16)
                weight = weights[slots[row, 1 + 2 * PLACES + i * UNROLL + u]]
                r = jnp.dot(both, weight, preferred_element_type=F32)
                made.append(r[:features, :width] + r[:features, width:] + r[features:, :width])
            add(*carry)
            for u in range(UNROLL):
                products[u] = made[u]
            return row, i

        return lax.fori_loop(0, (slots[row, 0] + UNROLL - 1) // UNROLL, group, carry)

    add(*lax.fori_loop(0, sets, one_set, (order[0], 0)))
    copies = []
    if first:
        copies.append(pltpu.make_async_copy(total, outs[0], sems.at[0]))
        copies[0].start()
    else:
        fetch.wait()
        half = size // 2
        for k in range(8):
            part = slice(k * 2 * half, (k + 1) * 2 * half)
            total[part] = total[part] + started[part]
        for k, out in enumerate(outs):
            core = lines[1] if k // 2 else 1 - lines[1]
            for place, away in enumerate(AWAY):
                owner = lax.rem(lines[0] + away, 4) * 2 + core
                copies.append(
                    pltpu.make_async_copy(
                        total.at[pl.ds(owner * 2 * half + (k % 2) * half, half)],
                        out.at[place * half : (place + 1) * half],
                        sems.at[k * 4 + place],
                    )
                )
                copies[-1].start()
    for copy in copies:
        copy.wait()


AWAY = (2, 1, 3, 0)
REMAP_MIB = 32


def remap(slots, order, lines, arrays, tables, count, start):
    block = arrays[0].shape[1:]
    sizes = [a.shape[0] for a in arrays]
    first = start is None
    own_rows = slots.ndim == 1
    sets = order.shape[0]
    operands = (slots, order, lines, tables) + tuple(arrays) + (() if first else (start,))
    outs = (count,) if first else (count // 4,) * 4
    return pl.pallas_call(
        functools.partial(remap_kernel, first, sizes, own_rows),
        out_shape=[jax.ShapeDtypeStruct((n,) + block, F32) for n in outs],
        in_specs=[SMEM_SPEC] * 3 + [HBM_SPEC] * (len(operands) - 3),
        out_specs=[HBM_SPEC] * len(outs),
        scratch_shapes=[
            pltpu.VMEM((sum(sizes),) + block, F32),
            pltpu.VMEM(tables.shape, BF16),
            pltpu.VMEM((count,) + block, F32),
            pltpu.VMEM((UNROLL,) + block, F32),
            pltpu.VMEM((sets, 128), jnp.int32),
            pltpu.SMEM((sets, 128), jnp.int32),
            pltpu.SemaphoreType.DMA((16,)),
            pltpu.SemaphoreType.DMA((2,)),
        ]
        + ([] if first else [pltpu.VMEM((count,) + block, F32)]),
        compiler_params=params(REMAP_MIB),
        cost_estimate=cost(12 if first else 8),
        name="remap",
    )(*operands)


EARLY_SETS = 10


def remap_all(slots, early_order, late_order, lines, sets, tables, count):
    (start,) = remap(slots, early_order, lines, sets[0], tables, count, None)
    return remap(slots, late_order, lines, sets[1], tables, count, start)


def step(value, along, other_core=False):
    ny = lax.axis_size("fy")
    pairs = []
    for y in range(ny):
        chip, core = divmod(y, 2)
        pairs.append((y, (chip + along) % (ny // 2) * 2 + (core ^ int(other_core))))
    return lax.ppermute(value, "fy", pairs)


def gather_sums(other, mine):
    n = mine.shape[0] // 4
    h = n // 2
    got = step(other, 0, True)
    far = mine[:n] + got[:n]
    up, down = step(far[:h], 1), step(far[h:], -1)
    plus = mine[n : 2 * n] + got[n : 2 * n]
    minus = mine[2 * n : 3 * n] + got[2 * n : 3 * n]
    plus = jnp.concatenate([plus[:h] + up, plus[h:]], axis=0)
    minus = jnp.concatenate([minus[:h], minus[h:] + down], axis=0)
    return mine, got, step(plus, 1), step(minus, -1)


def hop(value, first, by):
    nx, ny = lax.axis_size("fx"), lax.axis_size("fy")
    side = math.isqrt(nx)
    pairs = []
    for x in range(nx):
        for y in range(ny):
            slow, fast = divmod(x, side)
            if first == (y % 2 == 0):
                fast = (fast + by) % side
            else:
                slow = (slow + by) % side
            pairs.append((x * ny + y, (slow * side + fast) * ny + y))
    return lax.ppermute(value, ("fx", "fy"), pairs)


def spread(own, given=(), prepare=lambda given: given):
    n = own.shape[0]
    p, m = hop(own, True, 1), hop(own, True, -1)
    bp, bm = hop(own, False, 1), hop(own, False, -1)
    p, m, bp, bm, given = lax.optimization_barrier((p, m, bp, bm, given))
    opp = hop(p, True, 1)
    pm = jnp.concatenate([p, m], axis=0)
    pmp, pmm = hop(pm, False, 1), hop(pm, False, -1)
    bo = hop(bm, False, -1)
    made = prepare(given)
    opp, pmp, pmm, bo, made = lax.optimization_barrier((opp, pmp, pmm, bo, made))
    op, om = hop(opp, False, 1), hop(opp, False, -1)
    pmo = hop(pmm, False, -1)
    oo = hop(op, False, 1)
    return ([own, p, m, bp, bm, opp, pmp, pmm], [bo, op, om, pmo, oo]), made


def spread_order(mx, my):
    side = math.isqrt(lax.axis_size("fx"))
    slow, fast = mx // side, mx % side
    turned = my % 2
    places = [(0, 0), (1, 0), (-1, 0), (0, 1), (0, -1), (2, 0), (1, 1), (-1, 1), (1, -1), (-1, -1),
              (0, 2), (2, 1), (2, -1), (1, 2), (-1, 2), (2, 2)]
    a = jnp.array([p[0] for p in places], jnp.int32)
    b = jnp.array([p[1] for p in places], jnp.int32)
    from_fast = (fast - jnp.where(turned == 0, a, b) + side) % side
    from_slow = (slow - jnp.where(turned == 0, b, a) + side) % side
    return from_slow * side + from_fast


def gelu(x):
    inner = x * (0.7978845608028654 + (0.7978845608028654 * 0.044715) * (x * x))
    half = 0.5 * x
    return half + half * jnp.tanh(inner)


def summed(parts, b):
    mine, got, plus, minus = parts
    own = 3 * plus.shape[0]
    return (mine[own + b] + got[own + b]) + (plus[b] + minus[b])


def network_kernel(at, *refs):
    parts, (w_in, b_in, w_mid, b_mid, w_out), refs = refs[:4], refs[4:9], refs[9:]
    out = refs[-1]
    width = out.shape[2]
    count = parts[2].shape[0]

    def piece(i, carry):
        pairs = [i * 4 + 2 * k for k in range(2)]
        xs = [
            jnp.concatenate([summed(parts, b), summed(parts, b + 1)], axis=1).astype(BF16)
            for b in pairs
        ]
        firsts = [jnp.dot(w_in[...], x, preferred_element_type=F32) + b_in[...] for x in xs]
        firsts = [gelu(first).astype(BF16) for first in firsts]
        seconds = [jnp.dot(w_mid[...], h, preferred_element_type=F32) + b_mid[...] for h in firsts]
        seconds = [gelu(second).astype(BF16) for second in seconds]
        for b, second in zip(pairs, seconds):
            tend = jnp.dot(w_out[...], second, preferred_element_type=F32)
            out[at + b] = tend[:, :width]
            out[at + b + 1] = tend[:, width:]
        return carry

    lax.fori_loop(0, count // 4, piece, 0)


def column_network(parts, weights, count, at, begun):
    block = parts[2].shape[1:]
    operands = tuple(parts) + tuple(weights) + (() if begun is None else (begun,))
    return pl.pallas_call(
        functools.partial(network_kernel, at),
        out_shape=jax.ShapeDtypeStruct((count,) + block, F32),
        in_specs=[VMEM_SPEC] * len(operands),
        out_specs=VMEM_SPEC,
        input_output_aliases={} if begun is None else {len(operands) - 1: 0},
        compiler_params=params(),
        cost_estimate=cost(6),
        name="column_network",
    )(*operands)


def raise_kernel(*refs):
    levels, out = refs[-2:]
    width = out.shape[2]
    at = 0
    for parts in (refs[:4], refs[4:8]):
        count = parts[2].shape[0]
        for b in range(0, count, 2):
            pair = jnp.concatenate([summed(parts, b), summed(parts, b + 1)], axis=1)
            raised = jnp.dot(levels[...], pair, precision=HIGHEST, preferred_element_type=F32)
            out[at + b] = raised[:, :width]
            out[at + b + 1] = raised[:, width:]
        at += count


def raise_levels(halves, levels):
    count = sum(parts[2].shape[0] for parts in halves)
    shape = (count, levels.shape[0], halves[0][2].shape[2])
    return pl.pallas_call(
        raise_kernel,
        out_shape=jax.ShapeDtypeStruct(shape, F32),
        in_specs=[VMEM_SPEC] * 9,
        out_specs=VMEM_SPEC,
        compiler_params=params(),
        cost_estimate=cost(2),
        name="raise_levels",
    )(*halves[0], *halves[1], levels)


def level_matrix(brackets, fractions, nlev, variables, features):
    levels = nlev // variables
    cols = jnp.arange(levels, dtype=jnp.int32)
    lower = (cols[None, :] == brackets[:, None]).astype(F32)
    upper = (cols[None, :] == brackets[:, None] + 1).astype(F32)
    one = lower * (1.0 - fractions[:, None]) + upper * fractions[:, None]
    whole = (jnp.eye(variables, dtype=F32)[:, None, :, None] * one[None, :, None, :]).reshape(
        variables * one.shape[0], nlev
    )
    return jnp.pad(whole, ((0, features - whole.shape[0]), (0, 0)))


def per_device(
    state,
    coef,
    weight_table,
    src_blocks,
    dst_blocks,
    weight_rows,
    counts,
    brackets,
    fractions,
    w_in,
    b_in,
    w_mid,
    b_mid,
    w_out,
):
    nblocks, nlev, width = state.shape
    used_features = w_in.shape[1]
    features = -(-used_features // 8) * 8
    variables = used_features // brackets.shape[0]
    nx, ny = lax.axis_size("fx"), lax.axis_size("fy")
    mx, my = lax.axis_index("fx"), lax.axis_index("fy")
    ndev, cap = src_blocks.shape[1:]

    levels = level_matrix(brackets, fractions, nlev, variables, features)
    zero_row = weight_table.shape[0]
    order = spread_order(mx, my)
    spare = features - used_features
    given = (src_blocks, dst_blocks, weight_rows, counts)
    own_rows = own_table(*given, ny, nblocks, zero_row)
    plain = split_table(weight_table, False)

    field, source = diffuse(state, coef, levels, own_rows)
    straight = jnp.arange(EARLY_SETS, dtype=jnp.int32)
    place = mx.astype(jnp.int32).reshape(1)
    lines = jnp.stack([my // 2, my % 2]).astype(jnp.int32)

    def way_back(given):
        src, dst, row, cnt, weights = given
        lists = jnp.concatenate([src[0], dst[0], row[0], cnt[0][:, None]], axis=1).astype(F32)
        one = 3 * cap + 1
        lists = lists.reshape(nx, ny, one).transpose(1, 0, 2).reshape(ny, nx * one)
        lists = lax.all_gather(lists, "fy", axis=0)
        lists = lax.dynamic_index_in_dim(lists, my, 1, False).reshape(ny, nx, one)
        lists = lists.transpose(1, 0, 2)
        table = slot_table(
            lists[..., :cap],
            lists[..., cap : 2 * cap],
            lists[..., 2 * cap : 3 * cap],
            lists[..., 3 * cap],
            nblocks,
            zero_row,
            False,
        ).astype(jnp.int32)
        return table, split_table(weights, True)

    sets, (table, turned) = spread(source, given + (weight_table,), way_back)
    sums = remap_all(
        place, straight, straight[: nx - EARLY_SETS], lines, sets, plain, ny * nblocks
    )
    network = (
        jnp.pad(w_in, ((0, 0), (0, spare))),
        b_in[:, None],
        w_mid,
        b_mid[:, None],
        jnp.pad(w_out, ((0, spare), (0, 0))),
    )
    tend, half = None, nblocks // 2
    for k in range(2):
        parts = gather_sums(sums[k], sums[2 + k])
        tend = column_network(parts, network, nblocks, k * half, tend)
    sets, _ = spread(tend)
    sums = remap_all(
        table, order[:EARLY_SETS], order[EARLY_SETS:], lines, sets, turned, ny * nblocks
    )
    halves = [gather_sums(sums[k], sums[2 + k]) for k in range(2)]
    return field, raise_levels(halves, levels.T)


def solution(mesh):
    placed = (
        P("fy", None, "fx"),
        P("fy", "fx"),
        P(),
        P(("fx", "fy"), None, None),
        P(("fx", "fy"), None, None),
        P(("fx", "fy"), None, None),
        P(("fx", "fy"), None),
        P(),
        P(),
        P(),
        P(),
        P(),
        P(),
        P(),
    )
    return jax.shard_map(
        per_device,
        mesh=mesh,
        in_specs=placed,
        out_specs=(P("fy", None, "fx"), P("fy", None, "fx")),
        check_vma=False,
    )
```

```python
import functools
import math

import jax
import jax.numpy as jnp
from jax import lax
from jax.experimental import pallas as pl
from jax.experimental.pallas import tpu as pltpu
from jax.sharding import PartitionSpec as P

SWEEPS = 4
ROWS = 4
F32 = jnp.float32
BF16 = jnp.bfloat16
HIGHEST = lax.Precision.HIGHEST

VMEM_SPEC = pl.BlockSpec(memory_space=pltpu.VMEM)
HBM_SPEC = pl.BlockSpec(memory_space=pltpu.HBM)
SMEM_SPEC = pl.BlockSpec(memory_space=pltpu.SMEM)


def params(mebibytes=32):
    return pltpu.CompilerParams(vmem_limit_bytes=mebibytes * 1024 * 1024)


def cost(microseconds):
    return pl.CostEstimate(
        flops=0, transcendentals=0, bytes_accessed=int(microseconds * 3_000_000)
    )


def pack_kernel(nrows, nlev, width, state, coef, top, bottom, first_out, last_out):
    halo = SWEEPS
    lane = lax.broadcasted_iota(jnp.int32, (nlev, width), 1)
    group = lane // halo
    lane_one = lax.broadcasted_iota(jnp.int32, (1, width), 1)
    group_one = lane_one // halo

    def rows_of(e):
        if e < halo:
            return top[e * nlev : (e + 1) * nlev, :], top[halo * nlev + e : halo * nlev + e + 1, :]
        if e < halo + nrows:
            return state[e - halo], coef[e - halo : e - halo + 1, :]
        b = e - halo - nrows
        return bottom[b * nlev : (b + 1) * nlev, :], bottom[halo * nlev + b : halo * nlev + b + 1, :]

    per = width // halo
    total = nrows + 2 * halo
    tiles = -(-total // per)
    first_out[...] = jnp.zeros_like(first_out)
    last_out[...] = jnp.zeros_like(last_out)
    for tile in range(tiles):
        first = jnp.zeros((nlev, width), F32)
        last = jnp.zeros((nlev, width), F32)
        first_c = jnp.zeros((1, width), F32)
        last_c = jnp.zeros((1, width), F32)
        for i in range(min(per, total - tile * per)):
            field, number = rows_of(tile * per + i)
            at = (halo * i) % width
            up = (halo * i + halo) % width
            first = jnp.where(group == i, pltpu.roll(field, at, 1) if at else field, first)
            last = jnp.where(group == i, pltpu.roll(field, up, 1) if up else field, last)
            first_c = jnp.where(group_one == i, pltpu.roll(number, at, 1) if at else number, first_c)
            last_c = jnp.where(group_one == i, pltpu.roll(number, up, 1) if up else number, last_c)
        first_out[tile * nlev : (tile + 1) * nlev, :] = first
        last_out[tile * nlev : (tile + 1) * nlev, :] = last
        first_out[tiles * nlev + tile : tiles * nlev + tile + 1, :] = first_c
        last_out[tiles * nlev + tile : tiles * nlev + tile + 1, :] = last_c


def sweep_kernel(
    nrows, nlev, width, state, coef, top, bottom, left, right, levels, marks, field_out, source_out, a, b, c
):
    halo = SWEEPS
    per = width // halo
    total = nrows + 2 * halo
    tiles = -(-total // per)
    lane = lax.broadcasted_iota(jnp.int32, (nlev, width), 1)
    lane_one = lax.broadcasted_iota(jnp.int32, (1, width), 1)
    for e in range(total):
        if e < halo:
            field = top[e * nlev : (e + 1) * nlev, :]
            number = top[halo * nlev + e : halo * nlev + e + 1, :]
        elif e < halo + nrows:
            field = state[e - halo]
            number = coef[e - halo : e - halo + 1, :]
        else:
            r = e - halo - nrows
            field = bottom[r * nlev : (r + 1) * nlev, :]
            number = bottom[halo * nlev + r : halo * nlev + r + 1, :]
        tile, i = e // per, e % per
        to_low = (width - halo * i) % width
        to_high = (width - halo - halo * i) % width
        edges = []
        for where_, rows in ((lane, slice(tile * nlev, (tile + 1) * nlev)),
                             (lane_one, slice(tiles * nlev + tile, tiles * nlev + tile + 1))):
            r_tile = right[rows, :]
            l_tile = left[rows, :]
            r_part = pltpu.roll(r_tile, to_low, 1) if to_low else r_tile
            l_part = pltpu.roll(l_tile, to_high, 1) if to_high else l_tile
            edges.append(
                jnp.where(where_ < halo, r_part, jnp.where(where_ >= width - halo, l_part, 0.0))
            )
        a[e, :, 0:width] = field
        a[e, :, width : 2 * width] = edges[0]
        c[e, :, 0:width] = number
        c[e, :, width : 2 * width] = edges[1]

    def step(source, e):
        mid = source[e]
        beside = pltpu.roll(mid, 1, 1) + pltpu.roll(mid, 2 * width - 1, 1)
        beside = beside + source[e + 1] + source[e - 1]
        return mid + c[e] * (beside - 4.0 * mid)

    held, other = a, b
    for sweep in range(1, SWEEPS):
        low, high = sweep, total - sweep
        steps = (high - low) // ROWS

        def some(i, carry, held=held, other=other, low=low):
            done = [step(held, low + i * ROWS + r) for r in range(ROWS)]
            for r in range(ROWS):
                other[low + i * ROWS + r] = done[r]
            return carry

        lax.fori_loop(0, steps, some, 0)
        for e in range(low + steps * ROWS, high):
            other[e] = step(held, e)
        held, other = other, held

    def final(i, carry):
        done = [step(held, i * ROWS + r + halo)[:, 0:width] for r in range(ROWS)]
        for r in range(ROWS):
            field_out[i * ROWS + r] = done[r]
        for r in range(0, ROWS, 2):
            pair = jnp.concatenate([done[r], done[r + 1]], axis=1)
            lowered = jnp.dot(
                levels[...], pair, precision=HIGHEST, preferred_element_type=F32
            )
            source_out[i * ROWS + r] = lowered[:, :width]
            source_out[i * ROWS + r + 1] = lowered[:, width:]
        return carry

    lax.fori_loop(0, nrows // ROWS, final, 0)
    spare = levels.shape[0] - 1
    for b in range(marks.shape[0]):
        source_out[b, spare : spare + 1, :] = marks[b : b + 1, :]


def diffuse(state, coef, levels, marks):
    nrows, nlev, width = state.shape
    halo = SWEEPS
    per = width // halo
    total = nrows + 2 * halo
    tiles = -(-total // per)
    nx, ny = lax.axis_size("fx"), lax.axis_size("fy")
    pad = -halo % 8
    blank = jnp.zeros((pad, width), F32)

    def row_message(rows):
        return jnp.concatenate(
            [state[rows].reshape(halo * nlev, width), coef[rows], blank], axis=0
        )

    down = [(i, i + 1) for i in range(ny - 1)]
    up = [(i + 1, i) for i in range(ny - 1)]
    top = lax.ppermute(row_message(slice(nrows - halo, nrows)), "fy", down)
    bottom = lax.ppermute(row_message(slice(0, halo)), "fy", up)
    edge = jax.ShapeDtypeStruct((tiles * nlev + 8, width), F32)
    first, last = pl.pallas_call(
        functools.partial(pack_kernel, nrows, nlev, width),
        out_shape=(edge, edge),
        in_specs=[VMEM_SPEC] * 4,
        out_specs=(VMEM_SPEC, VMEM_SPEC),
        compiler_params=params(),
        cost_estimate=cost(1),
        name="pack_edges",
    )(state, coef, top, bottom)
    ahead = [(i, (i + 1) % nx) for i in range(nx)]
    behind = [((i + 1) % nx, i) for i in range(nx)]
    left = lax.ppermute(last, "fx", ahead)
    right = lax.ppermute(first, "fx", behind)
    return pl.pallas_call(
        functools.partial(sweep_kernel, nrows, nlev, width),
        out_shape=(
            jax.ShapeDtypeStruct(state.shape, F32),
            jax.ShapeDtypeStruct((nrows, levels.shape[0], width), F32),
        ),
        in_specs=[VMEM_SPEC] * 8,
        out_specs=(VMEM_SPEC, VMEM_SPEC),
        scratch_shapes=[
            pltpu.VMEM((total, nlev, 2 * width), F32),
            pltpu.VMEM((total, nlev, 2 * width), F32),
            pltpu.VMEM((total, 1, 2 * width), F32),
        ],
        compiler_params=params(),
        cost_estimate=cost(9),
        name="sweeps",
    )(state, coef, top, bottom, left, right, levels, marks)


def split(value):
    high = value.astype(BF16)
    low = (value - high.astype(F32)).astype(BF16)
    return high, low


def table_kernel(turn, table, out):
    count, rows, width = table.shape
    for k in range(count):
        weights = table[k].T if turn else table[k]
        high, low = split(weights)
        out[k, :, 0:width] = high
        out[k, :, width:] = low
    out[count] = jnp.zeros((rows, 2 * width), BF16)


def split_table(table, turn):
    count, rows, width = table.shape
    return pl.pallas_call(
        functools.partial(table_kernel, turn),
        out_shape=jax.ShapeDtypeStruct((count + 1, rows, 2 * width), BF16),
        in_specs=[VMEM_SPEC],
        out_specs=VMEM_SPEC,
        compiler_params=params(),
        cost_estimate=cost(3),
        name="split_table",
    )(table)


UNROLL = 8


PLACES = 40


def list_kernel(zero_row, values, valid, table):
    sets, room = valid.shape
    fields = values.shape[1] // room
    slot = lax.broadcasted_iota(jnp.int32, (fields * room, room), 0)
    other = lax.broadcasted_iota(jnp.int32, (fields * room, room), 1)
    within = slot % room
    transposed = (((1,), (1,)), ((), ()))

    def spread_out(chosen):
        return lax.dot_general(
            chosen.astype(F32), valid[...], transposed, preferred_element_type=F32
        )

    ahead = spread_out(other < within)
    first = lax.broadcasted_iota(jnp.int32, ahead.shape, 0) // room * PLACES + 1
    place = jnp.where(spread_out(other == within) > 0.5, ahead.astype(jnp.int32) + first, -1)
    lane = lax.broadcasted_iota(jnp.int32, (fields * room, 128), 1)
    for s in range(sets):
        chosen = (place[:, s : s + 1] == lane).astype(F32)
        table[s : s + 1, :] = jnp.dot(
            values[s : s + 1, :], chosen, preferred_element_type=F32
        )
    lane = lax.broadcasted_iota(jnp.int32, table.shape, 1)
    weight_lane = (lane > 2 * PLACES) & (lane <= 3 * PLACES)
    rows = jnp.where(weight_lane, table[...] + float(zero_row), table[...])
    number = jnp.sum(valid[...], axis=1, keepdims=True)
    table[...] = jnp.where(lane == 0, number, rows)


def slot_table(src, dst, row, count, blocks, zero_row, forward):
    sets, groups, cap = src.shape
    valid = (jnp.arange(cap, dtype=F32)[None, None, :] < count[:, :, None]).astype(F32)
    taken, given = (src, dst) if forward else (dst, src)
    given = given + blocks * jnp.arange(groups, dtype=F32)[None, :, None]
    values = jnp.stack([taken, given, row - zero_row], axis=1).reshape(sets, 3 * groups * cap)
    return pl.pallas_call(
        functools.partial(list_kernel, zero_row),
        out_shape=jax.ShapeDtypeStruct((sets, 128), F32),
        in_specs=[VMEM_SPEC] * 2,
        out_specs=VMEM_SPEC,
        cost_estimate=cost(1),
        name="slot_table",
    )(values, valid.reshape(sets, groups * cap))


def own_kernel(groups, blocks, zero_row, src, dst, row, counts, table):
    cap, owners = src.shape
    sets = table.shape[0]
    lane = lax.broadcasted_iota(jnp.int32, (owners, owners), 1)
    below = lax.broadcasted_iota(jnp.int32, (owners, owners), 0)
    same = lane // groups == below // groups
    number = counts[...].astype(F32)
    ahead = jnp.dot(number, (same & (below < lane)).astype(F32), preferred_element_type=F32)
    keys = [jnp.where(c < counts[...], ahead.astype(jnp.int32) + 1 + c, -1) for c in range(cap)]
    keys = jnp.concatenate(keys + [jnp.zeros((8 - cap, owners), jnp.int32)], axis=0).astype(F32)
    keys = keys.T.astype(jnp.int32)
    mine = lax.broadcasted_iota(jnp.int32, (sets, owners), 1) // groups == lax.broadcasted_iota(
        jnp.int32, (sets, owners), 0
    )
    which = lax.broadcasted_iota(jnp.int32, (1, owners), 1) % groups
    rows = jnp.zeros((sets, owners), F32)
    for c in range(cap):
        key = keys[:, c : c + 1]
        for f, value in enumerate(
            (src[c : c + 1, :], dst[c : c + 1, :] + which * blocks, row[c : c + 1, :] - zero_row)
        ):
            chosen = ((lane == key + f * PLACES) & (key > 0)).astype(F32)
            held = jnp.where(mine, value.astype(F32), 0.0)
            rows = rows + jnp.dot(held, chosen, preferred_element_type=F32)
    place = lax.broadcasted_iota(jnp.int32, rows.shape, 1)
    rows = jnp.where((place > 2 * PLACES) & (place <= 3 * PLACES), rows + float(zero_row), rows)
    used = jnp.sum(jnp.where(mine, number, 0.0), axis=1, keepdims=True)
    table[...] = jnp.where(place == 0, used, rows)


def own_table(src, dst, row, counts, groups, blocks, zero_row):
    owners = counts.shape[1]
    return pl.pallas_call(
        functools.partial(own_kernel, groups, blocks, zero_row),
        out_shape=jax.ShapeDtypeStruct((owners // groups, owners), F32),
        in_specs=[VMEM_SPEC] * 4,
        out_specs=VMEM_SPEC,
        cost_estimate=cost(1),
        name="own_table",
    )(src[0].T, dst[0].T, row[0].T, counts)


def remap_kernel(first, last, marked, sizes, own_rows, slots, order, lines, tables, *refs):
    arrays, refs = refs[: len(sizes)], refs[len(sizes) :]
    if not first:
        start, refs = refs[0], refs[1:]
    if marked:
        marks, refs = refs[0], refs[1:]
    outs, refs = (refs[:6], refs[6:]) if last else (refs[:1], refs[1:])
    blocks, weights, total, products, held_rows, scalars, sems, late_sems = refs[:8]
    features, width = total.shape[1:]
    copies, at = [], 0
    for k, size in enumerate(sizes):
        copies.append(pltpu.make_async_copy(arrays[k], blocks.at[at : at + size], sems.at[k]))
        at += size
    copies.append(pltpu.make_async_copy(tables, weights, sems.at[len(sizes)]))
    for copy in copies:
        copy.start()
    if not first:
        started = refs[8]
        fetch = pltpu.make_async_copy(start, started, late_sems.at[0])
        fetch.start()
    total[...] = jnp.zeros_like(total)
    products[...] = jnp.zeros_like(products)
    for copy in copies:
        copy.wait()
    sets = order.shape[0]
    size = blocks.shape[0] // sets
    if own_rows:
        for p in range(sets):
            held_rows[p : p + 1, :] = blocks[
                p * size + slots[0], features - 1 : features, :
            ].astype(jnp.int32)
        rows_copy = pltpu.make_async_copy(held_rows, scalars, late_sems.at[1])
        rows_copy.start()
        rows_copy.wait()
        slots = scalars

    def add(row, i):
        held = [products[u] for u in range(UNROLL)]
        for u in range(UNROLL):
            t = slots[row, 1 + PLACES + i * UNROLL + u]
            total[t] = total[t] + held[u]

    def one_set(p, carry):
        row = p if own_rows else order[p]

        def group(i, carry):
            made = []
            for u in range(UNROLL):
                value = blocks[p * size + slots[row, 1 + i * UNROLL + u]]
                high = value.astype(BF16).astype(F32)
                both = jnp.concatenate([high, value - high], axis=0).astype(BF16)
                weight = weights[slots[row, 1 + 2 * PLACES + i * UNROLL + u]]
                r = jnp.dot(both, weight, preferred_element_type=F32)
                made.append(r[:features, :width] + r[:features, width:] + r[features:, :width])
            add(*carry)
            for u in range(UNROLL):
                products[u] = made[u]
            return row, i

        return lax.fori_loop(0, (slots[row, 0] + UNROLL - 1) // UNROLL, group, carry)

    start_row = jnp.int32(0) if own_rows else order[0]
    add(*lax.fori_loop(0, sets, one_set, (start_row, jnp.int32(0))))
    if not first:
        fetch.wait()
        for k in range(8):
            part = slice(k * size, (k + 1) * size)
            total[part] = total[part] + started[part]
    if marked:
        for b in range(total.shape[0]):
            total[b, features - 1 : features, :] = jnp.zeros((1, width), F32)
        each = marks.shape[0] // 8
        for k in range(8):
            for h in range(each):
                at = k * size + (lines[0] * 2 + lines[1]) * (size // 8) + h
                total[at, features - 1 : features, :] = marks[k * each + h : k * each + h + 1, :]
    copies = []
    if not last:
        copies.append(pltpu.make_async_copy(total, outs[0], sems.at[0]))
        copies[0].start()
    else:
        half = size // 2
        for k in range(4):
            core = lines[1] if k // 2 else 1 - lines[1]
            for place, away in enumerate(AWAY):
                owner = lax.rem(lines[0] + away, 4) * 2 + core
                out, at = (outs[k], place) if k < 2 or place < 3 else (outs[k + 2], 0)
                copies.append(
                    pltpu.make_async_copy(
                        total.at[pl.ds(owner * 2 * half + (k % 2) * half, half)],
                        out.at[at * half : (at + 1) * half],
                        sems.at[k * 4 + place],
                    )
                )
                copies[-1].start()
    for copy in copies:
        copy.wait()


AWAY = (2, 1, 3, 0)
REMAP_MIB = 32


def remap(slots, order, lines, arrays, tables, count, start, last=False, marks=None):
    block = arrays[0].shape[1:]
    sizes = [a.shape[0] for a in arrays]
    first = start is None
    marked = marks is not None
    own_rows = slots.ndim == 1
    sets = order.shape[0]
    large = (tables,) + tuple(arrays) + (() if first else (start,))
    small = (marks,) if marked else ()
    quarter = count // 4
    outs = (quarter,) * 2 + (quarter * 3 // 4,) * 2 + (quarter // 4,) * 2 if last else (count,)
    return pl.pallas_call(
        functools.partial(remap_kernel, first, last, marked, sizes, own_rows),
        out_shape=[jax.ShapeDtypeStruct((n,) + block, F32) for n in outs],
        in_specs=[SMEM_SPEC] * 3 + [HBM_SPEC] * len(large) + [VMEM_SPEC] * len(small),
        out_specs=[HBM_SPEC] * len(outs),
        scratch_shapes=[
            pltpu.VMEM((sum(sizes),) + block, F32),
            pltpu.VMEM(tables.shape, BF16),
            pltpu.VMEM((count,) + block, F32),
            pltpu.VMEM((UNROLL,) + block, F32),
            pltpu.VMEM((sets, 128), jnp.int32),
            pltpu.SMEM((sets, 128), jnp.int32),
            pltpu.SemaphoreType.DMA((16,)),
            pltpu.SemaphoreType.DMA((2,)),
        ]
        + ([] if first else [pltpu.VMEM((count,) + block, F32)]),
        compiler_params=params(REMAP_MIB),
        cost_estimate=cost(8),
        name="remap",
    )(slots, order, lines, *large, *small)


def step(value, along, other_core=False):
    ny = lax.axis_size("fy")
    pairs = []
    for y in range(ny):
        chip, core = divmod(y, 2)
        pairs.append((y, (chip + along) % (ny // 2) * 2 + (core ^ int(other_core))))
    return lax.ppermute(value, "fy", pairs)


def gather_sums(other, mine, own):
    n = own.shape[0]
    h = n // 2
    got = step(other, 0, True)
    far = mine[:n] + got[:n]
    up, down = step(far[:h], 1), step(far[h:], -1)
    plus = mine[n : 2 * n] + got[n : 2 * n]
    minus = mine[2 * n :] + got[2 * n : 3 * n]
    plus = jnp.concatenate([plus[:h] + up, plus[h:]], axis=0)
    minus = jnp.concatenate([minus[:h], minus[h:] + down], axis=0)
    return own + got[3 * n :], step(plus, 1), step(minus, -1)


def hop(value, first, by):
    nx, ny = lax.axis_size("fx"), lax.axis_size("fy")
    side = math.isqrt(nx)
    pairs = []
    for x in range(nx):
        for y in range(ny):
            slow, fast = divmod(x, side)
            if first == (y % 2 == 0):
                fast = (fast + by) % side
            else:
                slow = (slow + by) % side
            pairs.append((x * ny + y, (slow * side + fast) * ny + y))
    return lax.ppermute(value, ("fx", "fy"), pairs)


def spread(own, given, before, weigh, count):
    barrier = lax.optimization_barrier
    own, given = barrier((own, given))
    p, m = hop(own, True, 1), hop(own, True, -1)
    bp, bm = hop(own, False, 1), hop(own, False, -1)
    ready = before(*given)
    p, m, bp, bm, ready = barrier((p, m, bp, bm, ready))
    slots, order, tables, marks, other = ready
    opp = hop(p, True, 1)
    pm = jnp.concatenate([p, m], axis=0)
    pmp, pmm = hop(pm, False, 1), hop(pm, False, -1)
    bo = hop(bm, False, -1)
    (sums,) = weigh(slots, order[:5], [own, p, m, bp, bm], tables, None, False, None)
    opp, pmp, pmm, bo, sums = barrier((opp, pmp, pmm, bo, sums))
    op, om = hop(opp, False, 1), hop(opp, False, -1)
    pmo = hop(pmm, False, -1)
    oo = hop(op, False, 1)
    (sums,) = weigh(slots, order[5:11], [opp, pmp, pmm, bo], tables, sums, False, None)
    marks = None if isinstance(marks, tuple) else marks
    return weigh(slots, order[11:], [op, om, pmo, oo], tables, sums, True, marks), other


def spread_order(mx, my):
    side = math.isqrt(lax.axis_size("fx"))
    slow, fast = mx // side, mx % side
    turned = my % 2
    places = [(0, 0), (1, 0), (-1, 0), (0, 1), (0, -1), (2, 0), (1, 1), (-1, 1), (1, -1), (-1, -1),
              (0, 2), (2, 1), (2, -1), (1, 2), (-1, 2), (2, 2)]
    a = jnp.array([p[0] for p in places], jnp.int32)
    b = jnp.array([p[1] for p in places], jnp.int32)
    from_fast = (fast - jnp.where(turned == 0, a, b) + side) % side
    from_slow = (slow - jnp.where(turned == 0, b, a) + side) % side
    return from_slow * side + from_fast


def gelu(x):
    inner = x * (0.7978845608028654 + (0.7978845608028654 * 0.044715) * (x * x))
    half = 0.5 * x
    return half + half * jnp.tanh(inner)


def summed(parts, b):
    own, plus, minus = parts
    return own[b] + (plus[b] + minus[b])


def network_kernel(at, *refs):
    parts, (w_in, b_in, w_mid, b_mid, w_out), refs = refs[:3], refs[3:8], refs[8:]
    out, spare_rows = refs[-2:]
    features, width = out.shape[1:]
    count = parts[2].shape[0]

    def piece(i, carry):
        pairs = [i * 4 + 2 * k for k in range(2)]
        blocks = [summed(parts, i * 4 + k) for k in range(4)]
        for k in range(4):
            spare_rows[pl.ds(i * 4 + k, 1), :] = blocks[k][features - 1 :]
        xs = [jnp.concatenate(blocks[k : k + 2], axis=1).astype(BF16) for k in (0, 2)]
        firsts = [jnp.dot(w_in[...], x, preferred_element_type=F32) + b_in[...] for x in xs]
        firsts = [gelu(first).astype(BF16) for first in firsts]
        seconds = [jnp.dot(w_mid[...], h, preferred_element_type=F32) + b_mid[...] for h in firsts]
        seconds = [gelu(second).astype(BF16) for second in seconds]
        for b, second in zip(pairs, seconds):
            tend = jnp.dot(w_out[...], second, preferred_element_type=F32)
            out[at + b] = tend[:, :width]
            out[at + b + 1] = tend[:, width:]
        return carry

    lax.fori_loop(0, count // 4, piece, 0)


def column_network(parts, weights, count, at, begun):
    block = parts[2].shape[1:]
    operands = tuple(parts) + tuple(weights) + (() if begun is None else (begun,))
    return pl.pallas_call(
        functools.partial(network_kernel, at),
        out_shape=(
            jax.ShapeDtypeStruct((count,) + block, F32),
            jax.ShapeDtypeStruct((parts[2].shape[0], block[1]), F32),
        ),
        in_specs=[VMEM_SPEC] * len(operands),
        out_specs=(VMEM_SPEC, VMEM_SPEC),
        input_output_aliases={} if begun is None else {len(operands) - 1: 0},
        compiler_params=params(),
        cost_estimate=cost(6),
        name="column_network",
    )(*operands)


def raise_kernel(*refs):
    levels, out = refs[-2:]
    width = out.shape[2]
    at = 0
    for parts in (refs[:3], refs[3:6]):
        count = parts[2].shape[0]
        for b in range(0, count, 2):
            pair = jnp.concatenate([summed(parts, b), summed(parts, b + 1)], axis=1)
            raised = jnp.dot(levels[...], pair, precision=HIGHEST, preferred_element_type=F32)
            out[at + b] = raised[:, :width]
            out[at + b + 1] = raised[:, width:]
        at += count


def raise_levels(halves, levels):
    count = sum(parts[2].shape[0] for parts in halves)
    shape = (count, levels.shape[0], halves[0][2].shape[2])
    return pl.pallas_call(
        raise_kernel,
        out_shape=jax.ShapeDtypeStruct(shape, F32),
        in_specs=[VMEM_SPEC] * 7,
        out_specs=VMEM_SPEC,
        compiler_params=params(),
        cost_estimate=cost(2),
        name="raise_levels",
    )(*halves[0], *halves[1], levels)


def level_matrix(brackets, fractions, nlev, variables, features):
    levels = nlev // variables
    cols = jnp.arange(levels, dtype=jnp.int32)
    lower = (cols[None, :] == brackets[:, None]).astype(F32)
    upper = (cols[None, :] == brackets[:, None] + 1).astype(F32)
    one = lower * (1.0 - fractions[:, None]) + upper * fractions[:, None]
    whole = (jnp.eye(variables, dtype=F32)[:, None, :, None] * one[None, :, None, :]).reshape(
        variables * one.shape[0], nlev
    )
    return jnp.pad(whole, ((0, features - whole.shape[0]), (0, 0)))


def per_device(
    state,
    coef,
    weight_table,
    src_blocks,
    dst_blocks,
    weight_rows,
    counts,
    brackets,
    fractions,
    w_in,
    b_in,
    w_mid,
    b_mid,
    w_out,
):
    nblocks, nlev, width = state.shape
    used_features = w_in.shape[1]
    features = -(-used_features // 8) * 8
    variables = used_features // brackets.shape[0]
    nx, ny = lax.axis_size("fx"), lax.axis_size("fy")
    mx, my = lax.axis_index("fx"), lax.axis_index("fy")
    ndev, cap = src_blocks.shape[1:]

    levels = level_matrix(brackets, fractions, nlev, variables, features)
    zero_row = weight_table.shape[0]
    order = spread_order(mx, my)
    spare = features - used_features
    place = mx.astype(jnp.int32).reshape(1)
    lines = jnp.stack([my // 2, my % 2]).astype(jnp.int32)
    one = 3 * cap + 1
    bands = ny * nblocks

    def weigh(slots, order, arrays, tables, start, last, marks):
        return remap(slots, order, lines, arrays, tables, bands, start, last, marks)

    def way_out(src, dst, row, cnt, weights, w_in, b_in, w_mid, b_mid, w_out):
        lists = jnp.concatenate([src[0], dst[0], row[0], cnt[0][:, None]], axis=1).astype(F32)
        lists = lists.reshape(nx, ny, one).transpose(1, 0, 2).reshape(ny, nx * one)
        lists = jnp.pad(lists, ((0, 0), (0, -nx * one % width))).reshape(-1, width)
        network = (
            jnp.pad(w_in, ((0, 0), (0, spare))),
            b_in[:, None],
            w_mid,
            b_mid[:, None],
            jnp.pad(w_out, ((0, spare), (0, 0))),
        )
        straight = jnp.arange(nx, dtype=jnp.int32)
        return place, straight, split_table(weights, False), lists, network

    def way_back(first, second, weights, order):
        rows = jnp.concatenate([first, second], axis=0).reshape(ny, -1, width)
        rows = rows[:, : -(-nx * one // width)].reshape(ny, -1)
        lists = rows[:, : nx * one].reshape(ny, nx, one).transpose(1, 0, 2)
        table = slot_table(
            lists[..., :cap],
            lists[..., cap : 2 * cap],
            lists[..., 2 * cap : 3 * cap],
            lists[..., 3 * cap],
            nblocks,
            zero_row,
            False,
        )
        return table.astype(jnp.int32), order, split_table(weights, True), (), ()

    own_rows = own_table(src_blocks, dst_blocks, weight_rows, counts, ny, nblocks, zero_row)
    field, source = diffuse(state, coef, levels, own_rows)
    given = (src_blocks, dst_blocks, weight_rows, counts, weight_table)
    given += (w_in, b_in, w_mid, b_mid, w_out)
    sums, network = spread(source, given, way_out, weigh, bands)
    half = nblocks // 2
    parts = gather_sums(*sums[0::2])
    tend, first = column_network(parts, network, nblocks, 0, None)
    parts = gather_sums(*sums[1::2])
    tend, second = column_network(parts, network, nblocks, half, tend)
    given = (first, second, weight_table, order)
    sums, _ = spread(tend, given, way_back, weigh, bands)
    halves = [gather_sums(*sums[k::2]) for k in range(2)]
    return field, raise_levels(halves, levels.T)


def solution(mesh):
    placed = (
        P("fy", None, "fx"),
        P("fy", "fx"),
        P(),
        P(("fx", "fy"), None, None),
        P(("fx", "fy"), None, None),
        P(("fx", "fy"), None, None),
        P(("fx", "fy"), None),
        P(),
        P(),
        P(),
        P(),
        P(),
        P(),
        P(),
    )
    return jax.shard_map(
        per_device,
        mesh=mesh,
        in_specs=placed,
        out_specs=(P("fy", None, "fx"), P("fy", None, "fx")),
        check_vma=False,
    )
```

```python
import functools
import math

import jax
import jax.numpy as jnp
from jax import lax
from jax.experimental import pallas as pl
from jax.experimental.pallas import tpu as pltpu
from jax.sharding import PartitionSpec as P

SWEEPS = 4
ROWS = 8
F32 = jnp.float32
BF16 = jnp.bfloat16
HIGHEST = lax.Precision.HIGHEST

VMEM_SPEC = pl.BlockSpec(memory_space=pltpu.VMEM)
HBM_SPEC = pl.BlockSpec(memory_space=pltpu.HBM)
SMEM_SPEC = pl.BlockSpec(memory_space=pltpu.SMEM)


def params(mebibytes=32):
    return pltpu.CompilerParams(vmem_limit_bytes=mebibytes * 1024 * 1024)


def cost(microseconds):
    return pl.CostEstimate(
        flops=0, transcendentals=0, bytes_accessed=int(microseconds * 3_000_000)
    )


def pack_kernel(nrows, nlev, width, state, coef, top, bottom, first_out, last_out):
    halo = SWEEPS
    lane = lax.broadcasted_iota(jnp.int32, (nlev, width), 1)
    group = lane // halo
    lane_one = lax.broadcasted_iota(jnp.int32, (1, width), 1)
    group_one = lane_one // halo

    def rows_of(e):
        if e < halo:
            return top[e * nlev : (e + 1) * nlev, :], top[halo * nlev + e : halo * nlev + e + 1, :]
        if e < halo + nrows:
            return state[e - halo], coef[e - halo : e - halo + 1, :]
        b = e - halo - nrows
        return bottom[b * nlev : (b + 1) * nlev, :], bottom[halo * nlev + b : halo * nlev + b + 1, :]

    per = width // halo
    total = nrows + 2 * halo
    tiles = -(-total // per)
    first_out[...] = jnp.zeros_like(first_out)
    last_out[...] = jnp.zeros_like(last_out)
    for tile in range(tiles):
        first = jnp.zeros((nlev, width), F32)
        last = jnp.zeros((nlev, width), F32)
        first_c = jnp.zeros((1, width), F32)
        last_c = jnp.zeros((1, width), F32)
        for i in range(min(per, total - tile * per)):
            field, number = rows_of(tile * per + i)
            at = (halo * i) % width
            up = (halo * i + halo) % width
            first = jnp.where(group == i, pltpu.roll(field, at, 1) if at else field, first)
            last = jnp.where(group == i, pltpu.roll(field, up, 1) if up else field, last)
            first_c = jnp.where(group_one == i, pltpu.roll(number, at, 1) if at else number, first_c)
            last_c = jnp.where(group_one == i, pltpu.roll(number, up, 1) if up else number, last_c)
        first_out[tile * nlev : (tile + 1) * nlev, :] = first
        last_out[tile * nlev : (tile + 1) * nlev, :] = last
        first_out[tiles * nlev + tile : tiles * nlev + tile + 1, :] = first_c
        last_out[tiles * nlev + tile : tiles * nlev + tile + 1, :] = last_c


def sweep_kernel(
    nrows, nlev, width, state, coef, top, bottom, left, right, levels, marks, field_out, source_out, a, b, c
):
    halo = SWEEPS
    per = width // halo
    total = nrows + 2 * halo
    tiles = -(-total // per)
    lane = lax.broadcasted_iota(jnp.int32, (nlev, width), 1)
    lane_one = lax.broadcasted_iota(jnp.int32, (1, width), 1)
    for e in range(total):
        if e < halo:
            field = top[e * nlev : (e + 1) * nlev, :]
            number = top[halo * nlev + e : halo * nlev + e + 1, :]
        elif e < halo + nrows:
            field = state[e - halo]
            number = coef[e - halo : e - halo + 1, :]
        else:
            r = e - halo - nrows
            field = bottom[r * nlev : (r + 1) * nlev, :]
            number = bottom[halo * nlev + r : halo * nlev + r + 1, :]
        tile, i = e // per, e % per
        to_low = (width - halo * i) % width
        to_high = (width - halo - halo * i) % width
        edges = []
        for where_, rows in ((lane, slice(tile * nlev, (tile + 1) * nlev)),
                             (lane_one, slice(tiles * nlev + tile, tiles * nlev + tile + 1))):
            r_tile = right[rows, :]
            l_tile = left[rows, :]
            r_part = pltpu.roll(r_tile, to_low, 1) if to_low else r_tile
            l_part = pltpu.roll(l_tile, to_high, 1) if to_high else l_tile
            edges.append(
                jnp.where(where_ < halo, r_part, jnp.where(where_ >= width - halo, l_part, 0.0))
            )
        a[e, :, 0:width] = field
        a[e, :, width : 2 * width] = edges[0]
        c[e, :, 0:width] = number
        c[e, :, width : 2 * width] = edges[1]

    def step(source, e):
        mid = source[e]
        beside = pltpu.roll(mid, 1, 1) + pltpu.roll(mid, 2 * width - 1, 1)
        beside = beside + source[e + 1] + source[e - 1]
        return mid + c[e] * (beside - 4.0 * mid)

    held, other = a, b
    for sweep in range(1, SWEEPS):
        low, high = sweep, total - sweep
        steps = (high - low) // ROWS

        def some(i, carry, held=held, other=other, low=low):
            done = [step(held, low + i * ROWS + r) for r in range(ROWS)]
            for r in range(ROWS):
                other[low + i * ROWS + r] = done[r]
            return carry

        lax.fori_loop(0, steps, some, 0)
        for e in range(low + steps * ROWS, high):
            other[e] = step(held, e)
        held, other = other, held

    high, low = split(levels[...])
    level_parts = jnp.concatenate([high, high, low], axis=1)

    def final(i, carry):
        done = [step(held, i * ROWS + r + halo)[:, 0:width] for r in range(ROWS)]
        for r in range(ROWS):
            field_out[i * ROWS + r] = done[r]
        for r in range(0, ROWS, 2):
            pair = jnp.concatenate([done[r], done[r + 1]], axis=1)
            high, low = split(pair)
            parts = jnp.concatenate([high, low, high], axis=0)
            lowered = jnp.dot(level_parts, parts, preferred_element_type=F32)
            source_out[i * ROWS + r] = lowered[:, :width]
            source_out[i * ROWS + r + 1] = lowered[:, width:]
        return carry

    lax.fori_loop(0, nrows // ROWS, final, 0)
    spare = levels.shape[0] - 1
    for b in range(marks.shape[0]):
        source_out[b, spare : spare + 1, :] = marks[b : b + 1, :]


def diffuse(state, coef, levels, marks):
    nrows, nlev, width = state.shape
    halo = SWEEPS
    per = width // halo
    total = nrows + 2 * halo
    tiles = -(-total // per)
    nx, ny = lax.axis_size("fx"), lax.axis_size("fy")
    pad = -halo % 8
    blank = jnp.zeros((pad, width), F32)

    def row_message(rows):
        return jnp.concatenate(
            [state[rows].reshape(halo * nlev, width), coef[rows], blank], axis=0
        )

    down = [(i, i + 1) for i in range(ny - 1)]
    up = [(i + 1, i) for i in range(ny - 1)]
    top = lax.ppermute(row_message(slice(nrows - halo, nrows)), "fy", down)
    bottom = lax.ppermute(row_message(slice(0, halo)), "fy", up)
    edge = jax.ShapeDtypeStruct((tiles * nlev + 8, width), F32)
    first, last = pl.pallas_call(
        functools.partial(pack_kernel, nrows, nlev, width),
        out_shape=(edge, edge),
        in_specs=[VMEM_SPEC] * 4,
        out_specs=(VMEM_SPEC, VMEM_SPEC),
        compiler_params=params(),
        cost_estimate=cost(1),
        name="pack_edges",
    )(state, coef, top, bottom)
    ahead = [(i, (i + 1) % nx) for i in range(nx)]
    behind = [((i + 1) % nx, i) for i in range(nx)]
    left = lax.ppermute(last, "fx", ahead)
    right = lax.ppermute(first, "fx", behind)
    return pl.pallas_call(
        functools.partial(sweep_kernel, nrows, nlev, width),
        out_shape=(
            jax.ShapeDtypeStruct(state.shape, F32),
            jax.ShapeDtypeStruct((nrows, levels.shape[0], width), F32),
        ),
        in_specs=[VMEM_SPEC] * 8,
        out_specs=(VMEM_SPEC, VMEM_SPEC),
        scratch_shapes=[
            pltpu.VMEM((total, nlev, 2 * width), F32),
            pltpu.VMEM((total, nlev, 2 * width), F32),
            pltpu.VMEM((total, 1, 2 * width), F32),
        ],
        compiler_params=params(),
        cost_estimate=cost(9),
        name="sweeps",
    )(state, coef, top, bottom, left, right, levels, marks)


def split(value):
    high = value.astype(BF16)
    low = (value - high.astype(F32)).astype(BF16)
    return high, low


def table_kernel(turn, table, out):
    count, rows, width = table.shape
    for k in range(count):
        weights = table[k].T if turn else table[k]
        high, low = split(weights)
        out[k, :, 0:width] = high
        out[k, :, width:] = low
    out[count] = jnp.zeros((rows, 2 * width), BF16)


def split_table(table, turn):
    count, rows, width = table.shape
    return pl.pallas_call(
        functools.partial(table_kernel, turn),
        out_shape=jax.ShapeDtypeStruct((count + 1, rows, 2 * width), BF16),
        in_specs=[VMEM_SPEC],
        out_specs=VMEM_SPEC,
        compiler_params=params(),
        cost_estimate=cost(3),
        name="split_table",
    )(table)


UNROLL = 8


PLACES = 40


def list_kernel(zero_row, values, valid, table):
    sets, room = valid.shape
    fields = values.shape[1] // room
    slot = lax.broadcasted_iota(jnp.int32, (fields * room, room), 0)
    other = lax.broadcasted_iota(jnp.int32, (fields * room, room), 1)
    within = slot % room
    transposed = (((1,), (1,)), ((), ()))

    def spread_out(chosen):
        return lax.dot_general(
            chosen.astype(F32), valid[...], transposed, preferred_element_type=F32
        )

    ahead = spread_out(other < within)
    first = lax.broadcasted_iota(jnp.int32, ahead.shape, 0) // room * PLACES + 1
    place = jnp.where(spread_out(other == within) > 0.5, ahead.astype(jnp.int32) + first, -1)
    lane = lax.broadcasted_iota(jnp.int32, (fields * room, 128), 1)
    for s in range(sets):
        chosen = (place[:, s : s + 1] == lane).astype(F32)
        table[s : s + 1, :] = jnp.dot(
            values[s : s + 1, :], chosen, preferred_element_type=F32
        )
    lane = lax.broadcasted_iota(jnp.int32, table.shape, 1)
    weight_lane = (lane > 2 * PLACES) & (lane <= 3 * PLACES)
    rows = jnp.where(weight_lane, table[...] + float(zero_row), table[...])
    number = jnp.sum(valid[...], axis=1, keepdims=True)
    table[...] = jnp.where(lane == 0, number, rows)


def slot_table(src, dst, row, count, blocks, zero_row, forward):
    sets, groups, cap = src.shape
    valid = (jnp.arange(cap, dtype=F32)[None, None, :] < count[:, :, None]).astype(F32)
    taken, given = (src, dst) if forward else (dst, src)
    given = given + blocks * jnp.arange(groups, dtype=F32)[None, :, None]
    values = jnp.stack([taken, given, row - zero_row], axis=1).reshape(sets, 3 * groups * cap)
    return pl.pallas_call(
        functools.partial(list_kernel, zero_row),
        out_shape=jax.ShapeDtypeStruct((sets, 128), F32),
        in_specs=[VMEM_SPEC] * 2,
        out_specs=VMEM_SPEC,
        cost_estimate=cost(1),
        name="slot_table",
    )(values, valid.reshape(sets, groups * cap))


def own_kernel(groups, blocks, zero_row, src, dst, row, counts, table):
    cap, owners = src.shape
    sets = table.shape[0]
    lane = lax.broadcasted_iota(jnp.int32, (owners, owners), 1)
    below = lax.broadcasted_iota(jnp.int32, (owners, owners), 0)
    same = lane // groups == below // groups
    number = counts[...].astype(F32)
    ahead = jnp.dot(number, (same & (below < lane)).astype(F32), preferred_element_type=F32)
    keys = [jnp.where(c < counts[...], ahead.astype(jnp.int32) + 1 + c, -1) for c in range(cap)]
    keys = jnp.concatenate(keys + [jnp.zeros((8 - cap, owners), jnp.int32)], axis=0).astype(F32)
    keys = keys.T.astype(jnp.int32)
    mine = lax.broadcasted_iota(jnp.int32, (sets, owners), 1) // groups == lax.broadcasted_iota(
        jnp.int32, (sets, owners), 0
    )
    which = lax.broadcasted_iota(jnp.int32, (1, owners), 1) % groups
    rows = jnp.zeros((sets, owners), F32)
    for c in range(cap):
        key = keys[:, c : c + 1]
        for f, value in enumerate(
            (src[c : c + 1, :], dst[c : c + 1, :] + which * blocks, row[c : c + 1, :] - zero_row)
        ):
            chosen = ((lane == key + f * PLACES) & (key > 0)).astype(F32)
            held = jnp.where(mine, value.astype(F32), 0.0)
            rows = rows + jnp.dot(held, chosen, preferred_element_type=F32)
    place = lax.broadcasted_iota(jnp.int32, rows.shape, 1)
    rows = jnp.where((place > 2 * PLACES) & (place <= 3 * PLACES), rows + float(zero_row), rows)
    used = jnp.sum(jnp.where(mine, number, 0.0), axis=1, keepdims=True)
    table[...] = jnp.where(place == 0, used, rows)


def own_table(src, dst, row, counts, groups, blocks, zero_row):
    owners = counts.shape[1]
    return pl.pallas_call(
        functools.partial(own_kernel, groups, blocks, zero_row),
        out_shape=jax.ShapeDtypeStruct((owners // groups, owners), F32),
        in_specs=[VMEM_SPEC] * 4,
        out_specs=VMEM_SPEC,
        cost_estimate=cost(1),
        name="own_table",
    )(src[0].T, dst[0].T, row[0].T, counts)


def remap_kernel(first, last, marked, sizes, own_rows, slots, order, lines, tables, *refs):
    arrays, refs = refs[: len(sizes)], refs[len(sizes) :]
    if not first:
        start, refs = refs[0], refs[1:]
    if marked:
        marks, refs = refs[0], refs[1:]
    outs, refs = (refs[:6], refs[6:]) if last else (refs[:1], refs[1:])
    blocks, weights, total, products, tiles, held_rows, scalars, sems, late_sems, row_sems = refs[:10]
    features, width = total.shape[1:]
    sets = order.shape[0]
    size = blocks.shape[0] // sets
    at, row_copies, copies = 0, [], []
    for k, array in enumerate(arrays):
        if own_rows:
            for j in range(sizes[k] // size):
                row_copies.append(
                    pltpu.make_async_copy(
                        array.at[pl.ds(j * size + slots[0], 1), features - 8 : features],
                        tiles.at[at // size + j : at // size + j + 1],
                        row_sems.at[at // size + j],
                    )
                )
        part = blocks.at[at : at + sizes[k]]
        copies.append(pltpu.make_async_copy(array, part, sems.at[k]))
        at += sizes[k]
    fetch_weights = pltpu.make_async_copy(tables, weights, late_sems.at[2])
    for copy in row_copies + [fetch_weights] + copies:
        copy.start()
    if not first:
        started = refs[10]
        fetch = pltpu.make_async_copy(start, started, late_sems.at[0])
        fetch.start()
    total[...] = jnp.zeros_like(total)
    products[...] = jnp.zeros_like(products)
    if own_rows:
        for p, copy in enumerate(row_copies):
            copy.wait()
            held_rows[p : p + 1, :] = tiles[p, 7:8, :].astype(jnp.int32)
        rows_copy = pltpu.make_async_copy(held_rows, scalars, late_sems.at[1])
        rows_copy.start()
        rows_copy.wait()
        slots = scalars
    fetch_weights.wait()

    def add(row, i):
        held = [products[u] for u in range(UNROLL)]
        for u in range(UNROLL):
            t = slots[row, 1 + PLACES + i * UNROLL + u]
            total[t] = total[t] + held[u]

    def one_set(p, carry):
        row = p if own_rows else order[p]

        def group(i, carry):
            made = []
            for u in range(UNROLL):
                value = blocks[p * size + slots[row, 1 + i * UNROLL + u]]
                high = value.astype(BF16).astype(F32)
                both = jnp.concatenate([high, value - high], axis=0).astype(BF16)
                weight = weights[slots[row, 1 + 2 * PLACES + i * UNROLL + u]]
                r = jnp.dot(both, weight, preferred_element_type=F32)
                made.append(r[:features, :width] + r[:features, width:] + r[features:, :width])
            add(*carry)
            for u in range(UNROLL):
                products[u] = made[u]
            return row, i

        return lax.fori_loop(0, (slots[row, 0] + UNROLL - 1) // UNROLL, group, carry)

    carry, at = (jnp.int32(0) if own_rows else order[0], jnp.int32(0)), 0
    for k, copy in enumerate(copies):
        copy.wait()
        carry = lax.fori_loop(at // size, (at + sizes[k]) // size, one_set, carry)
        at += sizes[k]
    add(*carry)
    if not first:
        fetch.wait()
        for k in range(8):
            part = slice(k * size, (k + 1) * size)
            total[part] = total[part] + started[part]
    if marked:
        for b in range(total.shape[0]):
            total[b, features - 1 : features, :] = jnp.zeros((1, width), F32)
        each = marks.shape[0] // 8
        for k in range(8):
            for h in range(each):
                at = k * size + (lines[0] * 2 + lines[1]) * (size // 8) + h
                total[at, features - 1 : features, :] = marks[k * each + h : k * each + h + 1, :]
    copies = []
    if not last:
        copies.append(pltpu.make_async_copy(total, outs[0], sems.at[0]))
        copies[0].start()
    else:
        half = size // 2
        for k in range(4):
            core = lines[1] if k // 2 else 1 - lines[1]
            for place, away in enumerate(AWAY):
                owner = lax.rem(lines[0] + away, 4) * 2 + core
                out, at = (outs[k], place) if k < 2 or place < 3 else (outs[k + 2], 0)
                copies.append(
                    pltpu.make_async_copy(
                        total.at[pl.ds(owner * 2 * half + (k % 2) * half, half)],
                        out.at[at * half : (at + 1) * half],
                        sems.at[k * 4 + place],
                    )
                )
                copies[-1].start()
    for copy in copies:
        copy.wait()


AWAY = (2, 1, 3, 0)
REMAP_MIB = 32


def remap(slots, order, lines, arrays, tables, count, start, last=False, marks=None):
    block = arrays[0].shape[1:]
    sizes = [a.shape[0] for a in arrays]
    first = start is None
    marked = marks is not None
    own_rows = slots.ndim == 1
    sets = order.shape[0]
    large = (tables,) + tuple(arrays) + (() if first else (start,))
    small = (marks,) if marked else ()
    quarter = count // 4
    outs = (quarter,) * 2 + (quarter * 3 // 4,) * 2 + (quarter // 4,) * 2 if last else (count,)
    return pl.pallas_call(
        functools.partial(remap_kernel, first, last, marked, sizes, own_rows),
        out_shape=[jax.ShapeDtypeStruct((n,) + block, F32) for n in outs],
        in_specs=[SMEM_SPEC] * 3 + [HBM_SPEC] * len(large) + [VMEM_SPEC] * len(small),
        out_specs=[HBM_SPEC] * len(outs),
        scratch_shapes=[
            pltpu.VMEM((sum(sizes),) + block, F32),
            pltpu.VMEM(tables.shape, BF16),
            pltpu.VMEM((count,) + block, F32),
            pltpu.VMEM((UNROLL,) + block, F32),
            pltpu.VMEM((sets, 8, block[1]), F32),
            pltpu.VMEM((sets, 128), jnp.int32),
            pltpu.SMEM((sets, 128), jnp.int32),
            pltpu.SemaphoreType.DMA((16,)),
            pltpu.SemaphoreType.DMA((3,)),
            pltpu.SemaphoreType.DMA((sets,)),
        ]
        + ([] if first else [pltpu.VMEM((count,) + block, F32)]),
        compiler_params=params(REMAP_MIB),
        cost_estimate=cost(8),
        name="remap",
    )(slots, order, lines, *large, *small)


def step(value, along, other_core=False):
    ny = lax.axis_size("fy")
    pairs = []
    for y in range(ny):
        chip, core = divmod(y, 2)
        pairs.append((y, (chip + along) % (ny // 2) * 2 + (core ^ int(other_core))))
    return lax.ppermute(value, "fy", pairs)


def gather_sums(other, mine, own):
    n = own.shape[0]
    h = n // 2
    got = step(other, 0, True)
    far = mine[:n] + got[:n]
    up, down = step(far[:h], 1), step(far[h:], -1)
    plus = mine[n : 2 * n] + got[n : 2 * n]
    minus = mine[2 * n :] + got[2 * n : 3 * n]
    plus = jnp.concatenate([plus[:h] + up, plus[h:]], axis=0)
    minus = jnp.concatenate([minus[:h], minus[h:] + down], axis=0)
    return own + got[3 * n :], step(plus, 1), step(minus, -1)


def hop(value, first, by):
    nx, ny = lax.axis_size("fx"), lax.axis_size("fy")
    side = math.isqrt(nx)
    pairs = []
    for x in range(nx):
        for y in range(ny):
            slow, fast = divmod(x, side)
            if first == (y % 2 == 0):
                fast = (fast + by) % side
            else:
                slow = (slow + by) % side
            pairs.append((x * ny + y, (slow * side + fast) * ny + y))
    return lax.ppermute(value, ("fx", "fy"), pairs)


def spread(own, given, before, weigh, count):
    barrier = lax.optimization_barrier
    own, given = barrier((own, given))
    p, m = hop(own, True, 1), hop(own, True, -1)
    bp, bm = hop(own, False, 1), hop(own, False, -1)
    ready = before(*given)
    p, m, bp, bm, ready = barrier((p, m, bp, bm, ready))
    slots, order, tables, marks, other = ready
    opp = hop(p, True, 1)
    pm = jnp.concatenate([p, m], axis=0)
    pmp, pmm = hop(pm, False, 1), hop(pm, False, -1)
    bo = hop(bm, False, -1)
    (sums,) = weigh(slots, order[:5], [own, p, m, bp, bm], tables, None, False, None)
    opp, sums = barrier((opp, sums))
    pmm, bo = barrier((pmm, bo))
    op, om = hop(opp, False, 1), hop(opp, False, -1)
    pmo = hop(pmm, False, -1)
    oo = hop(op, False, 1)
    (sums,) = weigh(slots, order[5:12], [opp, pmp, pmm, bo, op], tables, sums, False, None)
    marks = None if isinstance(marks, tuple) else marks
    return weigh(slots, order[12:], [om, pmo, oo], tables, sums, True, marks), other


def spread_order(mx, my):
    side = math.isqrt(lax.axis_size("fx"))
    slow, fast = mx // side, mx % side
    turned = my % 2
    places = [(0, 0), (1, 0), (-1, 0), (0, 1), (0, -1), (2, 0), (1, 1), (-1, 1), (1, -1), (-1, -1),
              (0, 2), (2, 1), (2, -1), (1, 2), (-1, 2), (2, 2)]
    a = jnp.array([p[0] for p in places], jnp.int32)
    b = jnp.array([p[1] for p in places], jnp.int32)
    from_fast = (fast - jnp.where(turned == 0, a, b) + side) % side
    from_slow = (slow - jnp.where(turned == 0, b, a) + side) % side
    return from_slow * side + from_fast


def gelu(x):
    inner = x * (0.7978845608028654 + (0.7978845608028654 * 0.044715) * (x * x))
    half = 0.5 * x
    return half + half * jnp.tanh(inner)


def summed(parts, b):
    own, plus, minus = parts
    return own[b] + (plus[b] + minus[b])


def network_kernel(at, *refs):
    parts, (w_in, b_in, w_mid, b_mid, w_out), refs = refs[:3], refs[3:8], refs[8:]
    out, spare_rows = refs[-2:]
    features, width = out.shape[1:]
    count = parts[2].shape[0]

    def piece(i, carry):
        pairs = [i * 4 + 2 * k for k in range(2)]
        blocks = [summed(parts, i * 4 + k) for k in range(4)]
        for k in range(4):
            spare_rows[pl.ds(i * 4 + k, 1), :] = blocks[k][features - 1 :]
        xs = [jnp.concatenate(blocks[k : k + 2], axis=1).astype(BF16) for k in (0, 2)]
        firsts = [jnp.dot(w_in[...], x, preferred_element_type=F32) + b_in[...] for x in xs]
        firsts = [gelu(first).astype(BF16) for first in firsts]
        seconds = [jnp.dot(w_mid[...], h, preferred_element_type=F32) + b_mid[...] for h in firsts]
        seconds = [gelu(second).astype(BF16) for second in seconds]
        for b, second in zip(pairs, seconds):
            tend = jnp.dot(w_out[...], second, preferred_element_type=F32)
            out[at + b] = tend[:, :width]
            out[at + b + 1] = tend[:, width:]
        return carry

    lax.fori_loop(0, count // 4, piece, 0)


def column_network(parts, weights, count, at, begun):
    block = parts[2].shape[1:]
    operands = tuple(parts) + tuple(weights) + (() if begun is None else (begun,))
    return pl.pallas_call(
        functools.partial(network_kernel, at),
        out_shape=(
            jax.ShapeDtypeStruct((count,) + block, F32),
            jax.ShapeDtypeStruct((parts[2].shape[0], block[1]), F32),
        ),
        in_specs=[VMEM_SPEC] * len(operands),
        out_specs=(VMEM_SPEC, VMEM_SPEC),
        input_output_aliases={} if begun is None else {len(operands) - 1: 0},
        compiler_params=params(),
        cost_estimate=cost(6),
        name="column_network",
    )(*operands)


def raise_kernel(*refs):
    levels, out = refs[-2:]
    width = out.shape[2]
    at = 0
    for parts in (refs[:3], refs[3:6]):
        count = parts[2].shape[0]
        for b in range(0, count, 2):
            pair = jnp.concatenate([summed(parts, b), summed(parts, b + 1)], axis=1)
            raised = jnp.dot(levels[...], pair, precision=HIGHEST, preferred_element_type=F32)
            out[at + b] = raised[:, :width]
            out[at + b + 1] = raised[:, width:]
        at += count


def raise_levels(halves, levels):
    count = sum(parts[2].shape[0] for parts in halves)
    shape = (count, levels.shape[0], halves[0][2].shape[2])
    return pl.pallas_call(
        raise_kernel,
        out_shape=jax.ShapeDtypeStruct(shape, F32),
        in_specs=[VMEM_SPEC] * 7,
        out_specs=VMEM_SPEC,
        compiler_params=params(),
        cost_estimate=cost(2),
        name="raise_levels",
    )(*halves[0], *halves[1], levels)


def level_matrix(brackets, fractions, nlev, variables, features):
    levels = nlev // variables
    cols = jnp.arange(levels, dtype=jnp.int32)
    lower = (cols[None, :] == brackets[:, None]).astype(F32)
    upper = (cols[None, :] == brackets[:, None] + 1).astype(F32)
    one = lower * (1.0 - fractions[:, None]) + upper * fractions[:, None]
    whole = (jnp.eye(variables, dtype=F32)[:, None, :, None] * one[None, :, None, :]).reshape(
        variables * one.shape[0], nlev
    )
    return jnp.pad(whole, ((0, features - whole.shape[0]), (0, 0)))


def per_device(
    state,
    coef,
    weight_table,
    src_blocks,
    dst_blocks,
    weight_rows,
    counts,
    brackets,
    fractions,
    w_in,
    b_in,
    w_mid,
    b_mid,
    w_out,
):
    nblocks, nlev, width = state.shape
    used_features = w_in.shape[1]
    features = -(-used_features // 8) * 8
    variables = used_features // brackets.shape[0]
    nx, ny = lax.axis_size("fx"), lax.axis_size("fy")
    mx, my = lax.axis_index("fx"), lax.axis_index("fy")
    ndev, cap = src_blocks.shape[1:]

    levels = level_matrix(brackets, fractions, nlev, variables, features)
    zero_row = weight_table.shape[0]
    order = spread_order(mx, my)
    spare = features - used_features
    place = mx.astype(jnp.int32).reshape(1)
    lines = jnp.stack([my // 2, my % 2]).astype(jnp.int32)
    one = 3 * cap + 1
    bands = ny * nblocks

    def weigh(slots, order, arrays, tables, start, last, marks):
        return remap(slots, order, lines, arrays, tables, bands, start, last, marks)

    def way_out(src, dst, row, cnt, weights, w_in, b_in, w_mid, b_mid, w_out):
        lists = jnp.concatenate([src[0], dst[0], row[0], cnt[0][:, None]], axis=1).astype(F32)
        lists = lists.reshape(nx, ny, one).transpose(1, 0, 2).reshape(ny, nx * one)
        lists = jnp.pad(lists, ((0, 0), (0, -nx * one % width))).reshape(-1, width)
        network = (
            jnp.pad(w_in, ((0, 0), (0, spare))),
            b_in[:, None],
            w_mid,
            b_mid[:, None],
            jnp.pad(w_out, ((0, spare), (0, 0))),
        )
        straight = jnp.arange(nx, dtype=jnp.int32)
        return place, straight, split_table(weights, False), lists, network

    def way_back(first, second, weights, order):
        rows = jnp.concatenate([first, second], axis=0).reshape(ny, -1, width)
        rows = rows[:, : -(-nx * one // width)].reshape(ny, -1)
        lists = rows[:, : nx * one].reshape(ny, nx, one).transpose(1, 0, 2)
        table = slot_table(
            lists[..., :cap],
            lists[..., cap : 2 * cap],
            lists[..., 2 * cap : 3 * cap],
            lists[..., 3 * cap],
            nblocks,
            zero_row,
            False,
        )
        return table.astype(jnp.int32), order, split_table(weights, True), (), ()

    own_rows = own_table(src_blocks, dst_blocks, weight_rows, counts, ny, nblocks, zero_row)
    field, source = diffuse(state, coef, levels, own_rows)
    given = (src_blocks, dst_blocks, weight_rows, counts, weight_table)
    given += (w_in, b_in, w_mid, b_mid, w_out)
    sums, network = spread(source, given, way_out, weigh, bands)
    half = nblocks // 2
    parts = gather_sums(*sums[0::2])
    tend, first = column_network(parts, network, nblocks, 0, None)
    parts = gather_sums(*sums[1::2])
    tend, second = column_network(parts, network, nblocks, half, tend)
    given = (first, second, weight_table, order)
    sums, _ = spread(tend, given, way_back, weigh, bands)
    halves = [gather_sums(*sums[k::2]) for k in range(2)]
    return field, raise_levels(halves, levels.T)


def solution(mesh):
    placed = (
        P("fy", None, "fx"),
        P("fy", "fx"),
        P(),
        P(("fx", "fy"), None, None),
        P(("fx", "fy"), None, None),
        P(("fx", "fy"), None, None),
        P(("fx", "fy"), None),
        P(),
        P(),
        P(),
        P(),
        P(),
        P(),
        P(),
    )
    return jax.shard_map(
        per_device,
        mesh=mesh,
        in_specs=placed,
        out_specs=(P("fy", None, "fx"), P("fy", None, "fx")),
        check_vma=False,
    )
```

```python
import functools
import math

import jax
import jax.numpy as jnp
from jax import lax
from jax.experimental import pallas as pl
from jax.experimental.pallas import tpu as pltpu
from jax.sharding import PartitionSpec as P

SWEEPS = 4
ROWS = 16
F32 = jnp.float32
BF16 = jnp.bfloat16
HIGHEST = lax.Precision.HIGHEST

VMEM_SPEC = pl.BlockSpec(memory_space=pltpu.VMEM)
HBM_SPEC = pl.BlockSpec(memory_space=pltpu.HBM)
SMEM_SPEC = pl.BlockSpec(memory_space=pltpu.SMEM)


def params(mebibytes=32):
    return pltpu.CompilerParams(vmem_limit_bytes=mebibytes * 1024 * 1024)


def cost(microseconds):
    return pl.CostEstimate(
        flops=0, transcendentals=0, bytes_accessed=int(microseconds * 3_000_000)
    )


def pack_kernel(nrows, nlev, width, state, coef, top, bottom, first_out, last_out):
    halo = SWEEPS
    lane = lax.broadcasted_iota(jnp.int32, (nlev, width), 1)
    group = lane // halo
    lane_one = lax.broadcasted_iota(jnp.int32, (1, width), 1)
    group_one = lane_one // halo

    def rows_of(e):
        if e < halo:
            return top[e * nlev : (e + 1) * nlev, :], top[halo * nlev + e : halo * nlev + e + 1, :]
        if e < halo + nrows:
            return state[e - halo], coef[e - halo : e - halo + 1, :]
        b = e - halo - nrows
        return bottom[b * nlev : (b + 1) * nlev, :], bottom[halo * nlev + b : halo * nlev + b + 1, :]

    per = width // halo
    total = nrows + 2 * halo
    tiles = -(-total // per)
    first_out[...] = jnp.zeros_like(first_out)
    last_out[...] = jnp.zeros_like(last_out)
    for tile in range(tiles):
        first = jnp.zeros((nlev, width), F32)
        last = jnp.zeros((nlev, width), F32)
        first_c = jnp.zeros((1, width), F32)
        last_c = jnp.zeros((1, width), F32)
        for i in range(min(per, total - tile * per)):
            field, number = rows_of(tile * per + i)
            at = (halo * i) % width
            up = (halo * i + halo) % width
            first = jnp.where(group == i, pltpu.roll(field, at, 1) if at else field, first)
            last = jnp.where(group == i, pltpu.roll(field, up, 1) if up else field, last)
            first_c = jnp.where(group_one == i, pltpu.roll(number, at, 1) if at else number, first_c)
            last_c = jnp.where(group_one == i, pltpu.roll(number, up, 1) if up else number, last_c)
        first_out[tile * nlev : (tile + 1) * nlev, :] = first
        last_out[tile * nlev : (tile + 1) * nlev, :] = last
        first_out[tiles * nlev + tile : tiles * nlev + tile + 1, :] = first_c
        last_out[tiles * nlev + tile : tiles * nlev + tile + 1, :] = last_c


def sweep_kernel(
    nrows, nlev, width, state, coef, top, bottom, left, right, levels, marks, field_out, source_out, a, b, c
):
    halo = SWEEPS
    per = width // halo
    total = nrows + 2 * halo
    tiles = -(-total // per)
    lane = lax.broadcasted_iota(jnp.int32, (nlev, width), 1)
    lane_one = lax.broadcasted_iota(jnp.int32, (1, width), 1)
    for e in range(total):
        if e < halo:
            field = top[e * nlev : (e + 1) * nlev, :]
            number = top[halo * nlev + e : halo * nlev + e + 1, :]
        elif e < halo + nrows:
            field = state[e - halo]
            number = coef[e - halo : e - halo + 1, :]
        else:
            r = e - halo - nrows
            field = bottom[r * nlev : (r + 1) * nlev, :]
            number = bottom[halo * nlev + r : halo * nlev + r + 1, :]
        tile, i = e // per, e % per
        to_low = (width - halo * i) % width
        to_high = (width - halo - halo * i) % width
        edges = []
        for where_, rows in ((lane, slice(tile * nlev, (tile + 1) * nlev)),
                             (lane_one, slice(tiles * nlev + tile, tiles * nlev + tile + 1))):
            r_tile = right[rows, :]
            l_tile = left[rows, :]
            r_part = pltpu.roll(r_tile, to_low, 1) if to_low else r_tile
            l_part = pltpu.roll(l_tile, to_high, 1) if to_high else l_tile
            edges.append(
                jnp.where(where_ < halo, r_part, jnp.where(where_ >= width - halo, l_part, 0.0))
            )
        a[e, :, 0:width] = field
        a[e, :, width : 2 * width] = edges[0]
        c[e, :, 0:width] = number
        c[e, :, width : 2 * width] = edges[1]

    def step(source, e):
        mid = source[e]
        beside = pltpu.roll(mid, 1, 1) + pltpu.roll(mid, 2 * width - 1, 1)
        beside = beside + source[e + 1] + source[e - 1]
        return mid + c[e] * (beside - 4.0 * mid)

    held, other = a, b
    for sweep in range(1, SWEEPS):
        low, high = sweep, total - sweep
        steps = (high - low) // ROWS

        def some(i, carry, held=held, other=other, low=low):
            done = [step(held, low + i * ROWS + r) for r in range(ROWS)]
            for r in range(ROWS):
                other[low + i * ROWS + r] = done[r]
            return carry

        lax.fori_loop(0, steps, some, 0)
        for e in range(low + steps * ROWS, high):
            other[e] = step(held, e)
        held, other = other, held

    high, low = split(levels[...])
    level_parts = jnp.concatenate([high, high, low], axis=1)

    def final(i, carry):
        done = [step(held, i * ROWS + r + halo)[:, 0:width] for r in range(ROWS)]
        for r in range(ROWS):
            field_out[i * ROWS + r] = done[r]
        for r in range(0, ROWS, 2):
            pair = jnp.concatenate([done[r], done[r + 1]], axis=1)
            high, low = split(pair)
            parts = jnp.concatenate([high, low, high], axis=0)
            lowered = jnp.dot(level_parts, parts, preferred_element_type=F32)
            source_out[i * ROWS + r] = lowered[:, :width]
            source_out[i * ROWS + r + 1] = lowered[:, width:]
        return carry

    lax.fori_loop(0, nrows // ROWS, final, 0)
    spare = levels.shape[0] - 1
    for b in range(marks.shape[0]):
        source_out[b, spare : spare + 1, :] = marks[b : b + 1, :]


def diffuse(state, coef, levels, marks):
    nrows, nlev, width = state.shape
    halo = SWEEPS
    per = width // halo
    total = nrows + 2 * halo
    tiles = -(-total // per)
    nx, ny = lax.axis_size("fx"), lax.axis_size("fy")
    pad = -halo % 8
    blank = jnp.zeros((pad, width), F32)

    def row_message(rows):
        return jnp.concatenate(
            [state[rows].reshape(halo * nlev, width), coef[rows], blank], axis=0
        )

    down = [(i, i + 1) for i in range(ny - 1)]
    up = [(i + 1, i) for i in range(ny - 1)]
    top = lax.ppermute(row_message(slice(nrows - halo, nrows)), "fy", down)
    bottom = lax.ppermute(row_message(slice(0, halo)), "fy", up)
    edge = jax.ShapeDtypeStruct((tiles * nlev + 8, width), F32)
    first, last = pl.pallas_call(
        functools.partial(pack_kernel, nrows, nlev, width),
        out_shape=(edge, edge),
        in_specs=[VMEM_SPEC] * 4,
        out_specs=(VMEM_SPEC, VMEM_SPEC),
        compiler_params=params(),
        cost_estimate=cost(1),
        name="pack_edges",
    )(state, coef, top, bottom)
    ahead = [(i, (i + 1) % nx) for i in range(nx)]
    behind = [((i + 1) % nx, i) for i in range(nx)]
    left = lax.ppermute(last, "fx", ahead)
    right = lax.ppermute(first, "fx", behind)
    return pl.pallas_call(
        functools.partial(sweep_kernel, nrows, nlev, width),
        out_shape=(
            jax.ShapeDtypeStruct(state.shape, F32),
            jax.ShapeDtypeStruct((nrows, levels.shape[0], width), F32),
        ),
        in_specs=[VMEM_SPEC] * 8,
        out_specs=(VMEM_SPEC, VMEM_SPEC),
        scratch_shapes=[
            pltpu.VMEM((total, nlev, 2 * width), F32),
            pltpu.VMEM((total, nlev, 2 * width), F32),
            pltpu.VMEM((total, 1, 2 * width), F32),
        ],
        compiler_params=params(),
        cost_estimate=cost(9),
        name="sweeps",
    )(state, coef, top, bottom, left, right, levels, marks)


def split(value):
    high = value.astype(BF16)
    low = (value - high.astype(F32)).astype(BF16)
    return high, low


def table_kernel(turn, table, out):
    count, rows, width = table.shape
    for k in range(count):
        weights = table[k].T if turn else table[k]
        high, low = split(weights)
        out[k, :, 0:width] = high
        out[k, :, width:] = low
    out[count] = jnp.zeros((rows, 2 * width), BF16)


def split_table(table, turn):
    count, rows, width = table.shape
    return pl.pallas_call(
        functools.partial(table_kernel, turn),
        out_shape=jax.ShapeDtypeStruct((count + 1, rows, 2 * width), BF16),
        in_specs=[VMEM_SPEC],
        out_specs=VMEM_SPEC,
        compiler_params=params(),
        cost_estimate=cost(3),
        name="split_table",
    )(table)


UNROLL = 8


PLACES = 40


def list_kernel(zero_row, values, valid, table):
    sets, room = valid.shape
    fields = values.shape[1] // room
    slot = lax.broadcasted_iota(jnp.int32, (fields * room, room), 0)
    other = lax.broadcasted_iota(jnp.int32, (fields * room, room), 1)
    within = slot % room
    transposed = (((1,), (1,)), ((), ()))

    def spread_out(chosen):
        return lax.dot_general(
            chosen.astype(F32), valid[...], transposed, preferred_element_type=F32
        )

    ahead = spread_out(other < within)
    first = lax.broadcasted_iota(jnp.int32, ahead.shape, 0) // room * PLACES + 1
    place = jnp.where(spread_out(other == within) > 0.5, ahead.astype(jnp.int32) + first, -1)
    lane = lax.broadcasted_iota(jnp.int32, (fields * room, 128), 1)
    for s in range(sets):
        chosen = (place[:, s : s + 1] == lane).astype(F32)
        table[s : s + 1, :] = jnp.dot(
            values[s : s + 1, :], chosen, preferred_element_type=F32
        )
    lane = lax.broadcasted_iota(jnp.int32, table.shape, 1)
    weight_lane = (lane > 2 * PLACES) & (lane <= 3 * PLACES)
    rows = jnp.where(weight_lane, table[...] + float(zero_row), table[...])
    number = jnp.sum(valid[...], axis=1, keepdims=True)
    table[...] = jnp.where(lane == 0, number, rows)


def slot_table(src, dst, row, count, blocks, zero_row, forward):
    sets, groups, cap = src.shape
    valid = (jnp.arange(cap, dtype=F32)[None, None, :] < count[:, :, None]).astype(F32)
    taken, given = (src, dst) if forward else (dst, src)
    given = given + blocks * jnp.arange(groups, dtype=F32)[None, :, None]
    values = jnp.stack([taken, given, row - zero_row], axis=1).reshape(sets, 3 * groups * cap)
    return pl.pallas_call(
        functools.partial(list_kernel, zero_row),
        out_shape=jax.ShapeDtypeStruct((sets, 128), F32),
        in_specs=[VMEM_SPEC] * 2,
        out_specs=VMEM_SPEC,
        cost_estimate=cost(1),
        name="slot_table",
    )(values, valid.reshape(sets, groups * cap))


def own_kernel(groups, blocks, zero_row, src, dst, row, counts, table):
    cap, owners = src.shape
    sets = table.shape[0]
    lane = lax.broadcasted_iota(jnp.int32, (owners, owners), 1)
    below = lax.broadcasted_iota(jnp.int32, (owners, owners), 0)
    same = lane // groups == below // groups
    number = counts[...].astype(F32)
    ahead = jnp.dot(number, (same & (below < lane)).astype(F32), preferred_element_type=F32)
    keys = [jnp.where(c < counts[...], ahead.astype(jnp.int32) + 1 + c, -1) for c in range(cap)]
    keys = jnp.concatenate(keys + [jnp.zeros((8 - cap, owners), jnp.int32)], axis=0).astype(F32)
    keys = keys.T.astype(jnp.int32)
    mine = lax.broadcasted_iota(jnp.int32, (sets, owners), 1) // groups == lax.broadcasted_iota(
        jnp.int32, (sets, owners), 0
    )
    which = lax.broadcasted_iota(jnp.int32, (1, owners), 1) % groups
    rows = jnp.zeros((sets, owners), F32)
    for c in range(cap):
        key = keys[:, c : c + 1]
        for f, value in enumerate(
            (src[c : c + 1, :], dst[c : c + 1, :] + which * blocks, row[c : c + 1, :] - zero_row)
        ):
            chosen = ((lane == key + f * PLACES) & (key > 0)).astype(F32)
            held = jnp.where(mine, value.astype(F32), 0.0)
            rows = rows + jnp.dot(held, chosen, preferred_element_type=F32)
    place = lax.broadcasted_iota(jnp.int32, rows.shape, 1)
    rows = jnp.where((place > 2 * PLACES) & (place <= 3 * PLACES), rows + float(zero_row), rows)
    used = jnp.sum(jnp.where(mine, number, 0.0), axis=1, keepdims=True)
    table[...] = jnp.where(place == 0, used, rows)


def own_table(src, dst, row, counts, groups, blocks, zero_row):
    owners = counts.shape[1]
    return pl.pallas_call(
        functools.partial(own_kernel, groups, blocks, zero_row),
        out_shape=jax.ShapeDtypeStruct((owners // groups, owners), F32),
        in_specs=[VMEM_SPEC] * 4,
        out_specs=VMEM_SPEC,
        cost_estimate=cost(1),
        name="own_table",
    )(src[0].T, dst[0].T, row[0].T, counts)


def remap_kernel(first, last, marked, sizes, own_rows, slots, order, lines, tables, *refs):
    arrays, refs = refs[: len(sizes)], refs[len(sizes) :]
    if not first:
        start, refs = refs[0], refs[1:]
    if marked:
        marks, refs = refs[0], refs[1:]
    outs, refs = (refs[:6], refs[6:]) if last else (refs[:1], refs[1:])
    blocks, total, products, tiles, held_rows, scalars, sems, late_sems, row_sems = refs
    features, width = total.shape[1:]
    sets = order.shape[0]
    size = blocks.shape[0] // sets
    at, row_copies, copies = 0, [], []
    for k, array in enumerate(arrays):
        if own_rows:
            for j in range(sizes[k] // size):
                row_copies.append(
                    pltpu.make_async_copy(
                        array.at[pl.ds(j * size + slots[0], 1), features - 8 : features],
                        tiles.at[at // size + j : at // size + j + 1],
                        row_sems.at[at // size + j],
                    )
                )
        part = blocks.at[at : at + sizes[k]]
        copies.append(pltpu.make_async_copy(array, part, sems.at[k]))
        at += sizes[k]
    for copy in row_copies + copies:
        copy.start()
    total[...] = jnp.zeros_like(total)
    products[...] = jnp.zeros_like(products)
    if own_rows:
        for p, copy in enumerate(row_copies):
            copy.wait()
            held_rows[p : p + 1, :] = tiles[p, 7:8, :].astype(jnp.int32)
        rows_copy = pltpu.make_async_copy(held_rows, scalars, late_sems.at[0])
        rows_copy.start()
        rows_copy.wait()
        slots = scalars

    def add(row, i):
        held = [products[u] for u in range(UNROLL)]
        for u in range(UNROLL):
            t = slots[row, 1 + PLACES + i * UNROLL + u]
            total[t] = total[t] + held[u]

    def one_set(p, carry):
        row = p if own_rows else order[p]

        def group(i, carry):
            made = []
            for u in range(UNROLL):
                value = blocks[p * size + slots[row, 1 + i * UNROLL + u]]
                high = value.astype(BF16).astype(F32)
                both = jnp.concatenate([high, value - high], axis=0).astype(BF16)
                weight = tables[slots[row, 1 + 2 * PLACES + i * UNROLL + u]]
                r = jnp.dot(both, weight, preferred_element_type=F32)
                made.append(r[:features, :width] + r[:features, width:] + r[features:, :width])
            add(*carry)
            for u in range(UNROLL):
                products[u] = made[u]
            return row, i

        return lax.fori_loop(0, (slots[row, 0] + UNROLL - 1) // UNROLL, group, carry)

    carry, at = (jnp.int32(0) if own_rows else order[0], jnp.int32(0)), 0
    for k, copy in enumerate(copies):
        copy.wait()
        carry = lax.fori_loop(at // size, (at + sizes[k]) // size, one_set, carry)
        at += sizes[k]
    add(*carry)
    if not first:
        for k in range(8):
            part = slice(k * size, (k + 1) * size)
            total[part] = total[part] + start[part]
    if marked:
        for b in range(total.shape[0]):
            total[b, features - 1 : features, :] = jnp.zeros((1, width), F32)
        each = marks.shape[0] // 8
        for k in range(8):
            for h in range(each):
                at = k * size + (lines[0] * 2 + lines[1]) * (size // 8) + h
                total[at, features - 1 : features, :] = marks[k * each + h : k * each + h + 1, :]
    copies = []
    if not last:
        copies.append(pltpu.make_async_copy(total, outs[0], sems.at[0]))
        copies[0].start()
    else:
        half = size // 2
        for k in range(4):
            core = lines[1] if k // 2 else 1 - lines[1]
            for place, away in enumerate(AWAY):
                owner = lax.rem(lines[0] + away, 4) * 2 + core
                out, at = (outs[k], place) if k < 2 or place < 3 else (outs[k + 2], 0)
                copies.append(
                    pltpu.make_async_copy(
                        total.at[pl.ds(owner * 2 * half + (k % 2) * half, half)],
                        out.at[at * half : (at + 1) * half],
                        sems.at[k * 4 + place],
                    )
                )
                copies[-1].start()
    for copy in copies:
        copy.wait()


AWAY = (2, 1, 3, 0)
REMAP_MIB = 16


def remap(slots, order, lines, arrays, tables, count, start, last=False, marks=None):
    block = arrays[0].shape[1:]
    sizes = [a.shape[0] for a in arrays]
    first = start is None
    marked = marks is not None
    own_rows = slots.ndim == 1
    sets = order.shape[0]
    large = tuple(arrays)
    small = (() if first else (start,)) + ((marks,) if marked else ())
    quarter = count // 4
    outs = (quarter,) * 2 + (quarter * 3 // 4,) * 2 + (quarter // 4,) * 2 if last else (count,)
    return pl.pallas_call(
        functools.partial(remap_kernel, first, last, marked, sizes, own_rows),
        out_shape=[jax.ShapeDtypeStruct((n,) + block, F32) for n in outs],
        in_specs=[SMEM_SPEC] * 3 + [VMEM_SPEC] + [HBM_SPEC] * len(large) + [VMEM_SPEC] * len(small),
        out_specs=[HBM_SPEC] * len(outs),
        scratch_shapes=[
            pltpu.VMEM((sum(sizes),) + block, F32),
            pltpu.VMEM((count,) + block, F32),
            pltpu.VMEM((UNROLL,) + block, F32),
            pltpu.VMEM((sets, 8, block[1]), F32),
            pltpu.VMEM((sets, 128), jnp.int32),
            pltpu.SMEM((sets, 128), jnp.int32),
            pltpu.SemaphoreType.DMA((16,)),
            pltpu.SemaphoreType.DMA((1,)),
            pltpu.SemaphoreType.DMA((sets,)),
        ],
        compiler_params=params(REMAP_MIB),
        cost_estimate=cost(8),
        name="remap",
    )(slots, order, lines, tables, *large, *small)


def step(value, along, other_core=False):
    ny = lax.axis_size("fy")
    pairs = []
    for y in range(ny):
        chip, core = divmod(y, 2)
        pairs.append((y, (chip + along) % (ny // 2) * 2 + (core ^ int(other_core))))
    return lax.ppermute(value, "fy", pairs)


def gather_sums(other, mine, own):
    n = own.shape[0]
    h = n // 2
    got = step(other, 0, True)
    far = mine[:n] + got[:n]
    up, down = step(far[:h], 1), step(far[h:], -1)
    plus = mine[n : 2 * n] + got[n : 2 * n]
    minus = mine[2 * n :] + got[2 * n : 3 * n]
    plus = jnp.concatenate([plus[:h] + up, plus[h:]], axis=0)
    minus = jnp.concatenate([minus[:h], minus[h:] + down], axis=0)
    return own + got[3 * n :], step(plus, 1), step(minus, -1)


def hop(value, first, by):
    nx, ny = lax.axis_size("fx"), lax.axis_size("fy")
    side = math.isqrt(nx)
    pairs = []
    for x in range(nx):
        for y in range(ny):
            slow, fast = divmod(x, side)
            if first == (y % 2 == 0):
                fast = (fast + by) % side
            else:
                slow = (slow + by) % side
            pairs.append((x * ny + y, (slow * side + fast) * ny + y))
    return lax.ppermute(value, ("fx", "fy"), pairs)


def spread(own, given, before, weigh, count):
    barrier = lax.optimization_barrier
    own, given = barrier((own, given))
    p, m = hop(own, True, 1), hop(own, True, -1)
    bp, bm = hop(own, False, 1), hop(own, False, -1)
    ready = before(*given)
    p, m, bp, bm, ready = barrier((p, m, bp, bm, ready))
    slots, order, tables, marks, other = ready
    opp = hop(p, True, 1)
    pm = jnp.concatenate([p, m], axis=0)
    pmp, pmm = hop(pm, False, 1), hop(pm, False, -1)
    bo = hop(bm, False, -1)
    (sums,) = weigh(slots, order[:5], [own, p, m, bp, bm], tables, None, False, None)
    opp, sums = barrier((opp, sums))
    pmm, bo = barrier((pmm, bo))
    op, om = hop(opp, False, 1), hop(opp, False, -1)
    pmo = hop(pmm, False, -1)
    oo = hop(op, False, 1)
    (sums,) = weigh(slots, order[5:12], [opp, pmp, pmm, bo, op], tables, sums, False, None)
    marks = None if isinstance(marks, tuple) else marks
    return weigh(slots, order[12:], [om, pmo, oo], tables, sums, True, marks), other


def spread_order(mx, my):
    side = math.isqrt(lax.axis_size("fx"))
    slow, fast = mx // side, mx % side
    turned = my % 2
    places = [(0, 0), (1, 0), (-1, 0), (0, 1), (0, -1), (2, 0), (1, 1), (-1, 1), (1, -1), (-1, -1),
              (0, 2), (2, 1), (2, -1), (1, 2), (-1, 2), (2, 2)]
    a = jnp.array([p[0] for p in places], jnp.int32)
    b = jnp.array([p[1] for p in places], jnp.int32)
    from_fast = (fast - jnp.where(turned == 0, a, b) + side) % side
    from_slow = (slow - jnp.where(turned == 0, b, a) + side) % side
    return from_slow * side + from_fast


def gelu(x):
    inner = x * (0.7978845608028654 + (0.7978845608028654 * 0.044715) * (x * x))
    half = 0.5 * x
    return half + half * jnp.tanh(inner)


def summed(parts, b):
    own, plus, minus = parts
    return own[b] + (plus[b] + minus[b])


STEP = 8


def network_kernel(at, *refs):
    parts, (w_in, b_in, w_mid, b_mid, w_out), refs = refs[:3], refs[3:8], refs[8:]
    out, spare_rows = refs[-2:]
    features, width = out.shape[1:]
    count = parts[2].shape[0]

    def piece(i, carry):
        pairs = [i * STEP + k for k in range(0, STEP, 2)]
        blocks = [summed(parts, i * STEP + k) for k in range(STEP)]
        for k in range(STEP):
            spare_rows[pl.ds(i * STEP + k, 1), :] = blocks[k][features - 1 :]
        xs = [jnp.concatenate(blocks[k : k + 2], axis=1).astype(BF16) for k in range(0, STEP, 2)]
        firsts = [jnp.dot(w_in[...], x, preferred_element_type=F32) + b_in[...] for x in xs]
        firsts = [gelu(first).astype(BF16) for first in firsts]
        seconds = [jnp.dot(w_mid[...], h, preferred_element_type=F32) + b_mid[...] for h in firsts]
        seconds = [gelu(second).astype(BF16) for second in seconds]
        for b, second in zip(pairs, seconds):
            tend = jnp.dot(w_out[...], second, preferred_element_type=F32)
            out[at + b] = tend[:, :width]
            out[at + b + 1] = tend[:, width:]
        return carry

    lax.fori_loop(0, count // STEP, piece, 0)


def column_network(parts, weights, count, at, begun):
    block = parts[2].shape[1:]
    operands = tuple(parts) + tuple(weights) + (() if begun is None else (begun,))
    return pl.pallas_call(
        functools.partial(network_kernel, at),
        out_shape=(
            jax.ShapeDtypeStruct((count,) + block, F32),
            jax.ShapeDtypeStruct((parts[2].shape[0], block[1]), F32),
        ),
        in_specs=[VMEM_SPEC] * len(operands),
        out_specs=(VMEM_SPEC, VMEM_SPEC),
        input_output_aliases={} if begun is None else {len(operands) - 1: 0},
        compiler_params=params(),
        cost_estimate=cost(6),
        name="column_network",
    )(*operands)


def raise_kernel(*refs):
    levels, out = refs[-2:]
    width = out.shape[2]
    at = 0
    for parts in (refs[:3], refs[3:6]):
        count = parts[2].shape[0]
        for b in range(0, count, 2):
            pair = jnp.concatenate([summed(parts, b), summed(parts, b + 1)], axis=1)
            raised = jnp.dot(levels[...], pair, precision=HIGHEST, preferred_element_type=F32)
            out[at + b] = raised[:, :width]
            out[at + b + 1] = raised[:, width:]
        at += count


def raise_levels(halves, levels):
    count = sum(parts[2].shape[0] for parts in halves)
    shape = (count, levels.shape[0], halves[0][2].shape[2])
    return pl.pallas_call(
        raise_kernel,
        out_shape=jax.ShapeDtypeStruct(shape, F32),
        in_specs=[VMEM_SPEC] * 7,
        out_specs=VMEM_SPEC,
        compiler_params=params(),
        cost_estimate=cost(2),
        name="raise_levels",
    )(*halves[0], *halves[1], levels)


def level_matrix(brackets, fractions, nlev, variables, features):
    levels = nlev // variables
    cols = jnp.arange(levels, dtype=jnp.int32)
    lower = (cols[None, :] == brackets[:, None]).astype(F32)
    upper = (cols[None, :] == brackets[:, None] + 1).astype(F32)
    one = lower * (1.0 - fractions[:, None]) + upper * fractions[:, None]
    whole = (jnp.eye(variables, dtype=F32)[:, None, :, None] * one[None, :, None, :]).reshape(
        variables * one.shape[0], nlev
    )
    return jnp.pad(whole, ((0, features - whole.shape[0]), (0, 0)))


def per_device(
    state,
    coef,
    weight_table,
    src_blocks,
    dst_blocks,
    weight_rows,
    counts,
    brackets,
    fractions,
    w_in,
    b_in,
    w_mid,
    b_mid,
    w_out,
):
    nblocks, nlev, width = state.shape
    used_features = w_in.shape[1]
    features = -(-used_features // 8) * 8
    variables = used_features // brackets.shape[0]
    nx, ny = lax.axis_size("fx"), lax.axis_size("fy")
    mx, my = lax.axis_index("fx"), lax.axis_index("fy")
    ndev, cap = src_blocks.shape[1:]

    levels = level_matrix(brackets, fractions, nlev, variables, features)
    zero_row = weight_table.shape[0]
    order = spread_order(mx, my)
    spare = features - used_features
    place = mx.astype(jnp.int32).reshape(1)
    lines = jnp.stack([my // 2, my % 2]).astype(jnp.int32)
    one = 3 * cap + 1
    bands = ny * nblocks

    def weigh(slots, order, arrays, tables, start, last, marks):
        return remap(slots, order, lines, arrays, tables, bands, start, last, marks)

    def way_out(src, dst, row, cnt, weights, w_in, b_in, w_mid, b_mid, w_out):
        lists = jnp.concatenate([src[0], dst[0], row[0], cnt[0][:, None]], axis=1).astype(F32)
        lists = lists.reshape(nx, ny, one).transpose(1, 0, 2).reshape(ny, nx * one)
        lists = jnp.pad(lists, ((0, 0), (0, -nx * one % width))).reshape(-1, width)
        network = (
            jnp.pad(w_in, ((0, 0), (0, spare))),
            b_in[:, None],
            w_mid,
            b_mid[:, None],
            jnp.pad(w_out, ((0, spare), (0, 0))),
        )
        straight = jnp.arange(nx, dtype=jnp.int32)
        return place, straight, split_table(weights, False), lists, network

    def way_back(first, second, weights, order):
        rows = jnp.concatenate([first, second], axis=0).reshape(ny, -1, width)
        rows = rows[:, : -(-nx * one // width)].reshape(ny, -1)
        lists = rows[:, : nx * one].reshape(ny, nx, one).transpose(1, 0, 2)
        table = slot_table(
            lists[..., :cap],
            lists[..., cap : 2 * cap],
            lists[..., 2 * cap : 3 * cap],
            lists[..., 3 * cap],
            nblocks,
            zero_row,
            False,
        )
        return table.astype(jnp.int32), order, split_table(weights, True), (), ()

    own_rows = own_table(src_blocks, dst_blocks, weight_rows, counts, ny, nblocks, zero_row)
    field, source = diffuse(state, coef, levels, own_rows)
    given = (src_blocks, dst_blocks, weight_rows, counts, weight_table)
    given += (w_in, b_in, w_mid, b_mid, w_out)
    sums, network = spread(source, given, way_out, weigh, bands)
    half = nblocks // 2
    parts = gather_sums(*sums[0::2])
    tend, first = column_network(parts, network, nblocks, 0, None)
    parts = gather_sums(*sums[1::2])
    tend, second = column_network(parts, network, nblocks, half, tend)
    given = (first, second, weight_table, order)
    sums, _ = spread(tend, given, way_back, weigh, bands)
    halves = [gather_sums(*sums[k::2]) for k in range(2)]
    return field, raise_levels(halves, levels.T)


def solution(mesh):
    placed = (
        P("fy", None, "fx"),
        P("fy", "fx"),
        P(),
        P(("fx", "fy"), None, None),
        P(("fx", "fy"), None, None),
        P(("fx", "fy"), None, None),
        P(("fx", "fy"), None),
        P(),
        P(),
        P(),
        P(),
        P(),
        P(),
        P(),
    )
    return jax.shard_map(
        per_device,
        mesh=mesh,
        in_specs=placed,
        out_specs=(P("fy", None, "fx"), P("fy", None, "fx")),
        check_vma=False,
    )
```

```python
import functools
import math

import jax
import jax.numpy as jnp
import numpy as np
from jax import lax
from jax.experimental import pallas as pl
from jax.experimental.pallas import tpu as pltpu
from jax.sharding import PartitionSpec as P

SWEEPS = 4
ROWS = 16
F32 = jnp.float32
BF16 = jnp.bfloat16
HIGHEST = lax.Precision.HIGHEST

VMEM_SPEC = pl.BlockSpec(memory_space=pltpu.VMEM)
HBM_SPEC = pl.BlockSpec(memory_space=pltpu.HBM)
SMEM_SPEC = pl.BlockSpec(memory_space=pltpu.SMEM)


def params(mebibytes=32):
    return pltpu.CompilerParams(vmem_limit_bytes=mebibytes * 1024 * 1024)


def cost(microseconds):
    return pl.CostEstimate(
        flops=0, transcendentals=0, bytes_accessed=int(microseconds * 3_000_000)
    )


def pack_kernel(nrows, nlev, width, state, coef, top, bottom, first_out, last_out):
    halo = SWEEPS
    lane = lax.broadcasted_iota(jnp.int32, (nlev, width), 1)
    group = lane // halo
    lane_one = lax.broadcasted_iota(jnp.int32, (1, width), 1)
    group_one = lane_one // halo

    def rows_of(e):
        if e < halo:
            return top[e * nlev : (e + 1) * nlev, :], top[halo * nlev + e : halo * nlev + e + 1, :]
        if e < halo + nrows:
            return state[e - halo], coef[e - halo : e - halo + 1, :]
        b = e - halo - nrows
        return bottom[b * nlev : (b + 1) * nlev, :], bottom[halo * nlev + b : halo * nlev + b + 1, :]

    per = width // halo
    total = nrows + 2 * halo
    tiles = -(-total // per)
    first_out[...] = jnp.zeros_like(first_out)
    last_out[...] = jnp.zeros_like(last_out)
    for tile in range(tiles):
        first = jnp.zeros((nlev, width), F32)
        last = jnp.zeros((nlev, width), F32)
        first_c = jnp.zeros((1, width), F32)
        last_c = jnp.zeros((1, width), F32)
        for i in range(min(per, total - tile * per)):
            field, number = rows_of(tile * per + i)
            at = (halo * i) % width
            up = (halo * i + halo) % width
            first = jnp.where(group == i, pltpu.roll(field, at, 1) if at else field, first)
            last = jnp.where(group == i, pltpu.roll(field, up, 1) if up else field, last)
            first_c = jnp.where(group_one == i, pltpu.roll(number, at, 1) if at else number, first_c)
            last_c = jnp.where(group_one == i, pltpu.roll(number, up, 1) if up else number, last_c)
        first_out[tile * nlev : (tile + 1) * nlev, :] = first
        last_out[tile * nlev : (tile + 1) * nlev, :] = last
        first_out[tiles * nlev + tile : tiles * nlev + tile + 1, :] = first_c
        last_out[tiles * nlev + tile : tiles * nlev + tile + 1, :] = last_c


def sweep_kernel(
    nrows, nlev, width, state, coef, top, bottom, left, right, levels, marks, field_out, source_out, a, b, c
):
    halo = SWEEPS
    per = width // halo
    total = nrows + 2 * halo
    tiles = -(-total // per)
    lane = lax.broadcasted_iota(jnp.int32, (nlev, width), 1)
    lane_one = lax.broadcasted_iota(jnp.int32, (1, width), 1)
    for e in range(total):
        if e < halo:
            field = top[e * nlev : (e + 1) * nlev, :]
            number = top[halo * nlev + e : halo * nlev + e + 1, :]
        elif e < halo + nrows:
            field = state[e - halo]
            number = coef[e - halo : e - halo + 1, :]
        else:
            r = e - halo - nrows
            field = bottom[r * nlev : (r + 1) * nlev, :]
            number = bottom[halo * nlev + r : halo * nlev + r + 1, :]
        tile, i = e // per, e % per
        to_low = (width - halo * i) % width
        to_high = (width - halo - halo * i) % width
        edges = []
        for where_, rows in ((lane, slice(tile * nlev, (tile + 1) * nlev)),
                             (lane_one, slice(tiles * nlev + tile, tiles * nlev + tile + 1))):
            r_tile = right[rows, :]
            l_tile = left[rows, :]
            r_part = pltpu.roll(r_tile, to_low, 1) if to_low else r_tile
            l_part = pltpu.roll(l_tile, to_high, 1) if to_high else l_tile
            edges.append(
                jnp.where(where_ < halo, r_part, jnp.where(where_ >= width - halo, l_part, 0.0))
            )
        a[e, :, 0:width] = field
        a[e, :, width : 2 * width] = edges[0]
        c[e, :, 0:width] = number
        c[e, :, width : 2 * width] = edges[1]

    def step(source, e):
        mid = source[e]
        beside = pltpu.roll(mid, 1, 1) + pltpu.roll(mid, 2 * width - 1, 1)
        beside = beside + source[e + 1] + source[e - 1]
        return mid + c[e] * (beside - 4.0 * mid)

    held, other = a, b
    for sweep in range(1, SWEEPS):
        low, high = sweep, total - sweep
        steps = (high - low) // ROWS

        def some(i, carry, held=held, other=other, low=low):
            done = [step(held, low + i * ROWS + r) for r in range(ROWS)]
            for r in range(ROWS):
                other[low + i * ROWS + r] = done[r]
            return carry

        lax.fori_loop(0, steps, some, 0)
        for e in range(low + steps * ROWS, high):
            other[e] = step(held, e)
        held, other = other, held

    high, low = split(levels[...])
    level_parts = jnp.concatenate([high, high, low], axis=1)

    def final(i, carry):
        done = [step(held, i * ROWS + r + halo)[:, 0:width] for r in range(ROWS)]
        for r in range(ROWS):
            field_out[i * ROWS + r] = done[r]
        for r in range(0, ROWS, 2):
            pair = jnp.concatenate([done[r], done[r + 1]], axis=1)
            high, low = split(pair)
            parts = jnp.concatenate([high, low, high], axis=0)
            lowered = jnp.dot(level_parts, parts, preferred_element_type=F32)
            source_out[i * ROWS + r] = lowered[:, :width]
            source_out[i * ROWS + r + 1] = lowered[:, width:]
        return carry

    lax.fori_loop(0, nrows // ROWS, final, 0)
    spare = levels.shape[0] - 1
    for b in range(marks.shape[0]):
        source_out[b, spare : spare + 1, :] = marks[b : b + 1, :]


def diffuse(state, coef, levels, marks):
    nrows, nlev, width = state.shape
    halo = SWEEPS
    per = width // halo
    total = nrows + 2 * halo
    tiles = -(-total // per)
    nx, ny = lax.axis_size("fx"), lax.axis_size("fy")
    pad = -halo % 8
    blank = jnp.zeros((pad, width), F32)

    def row_message(rows):
        return jnp.concatenate(
            [state[rows].reshape(halo * nlev, width), coef[rows], blank], axis=0
        )

    down = [(i, i + 1) for i in range(ny - 1)]
    up = [(i + 1, i) for i in range(ny - 1)]
    top = lax.ppermute(row_message(slice(nrows - halo, nrows)), "fy", down)
    bottom = lax.ppermute(row_message(slice(0, halo)), "fy", up)
    edge = jax.ShapeDtypeStruct((tiles * nlev + 8, width), F32)
    first, last = pl.pallas_call(
        functools.partial(pack_kernel, nrows, nlev, width),
        out_shape=(edge, edge),
        in_specs=[VMEM_SPEC] * 4,
        out_specs=(VMEM_SPEC, VMEM_SPEC),
        compiler_params=params(),
        cost_estimate=cost(1),
        name="pack_edges",
    )(state, coef, top, bottom)
    ahead = [(i, (i + 1) % nx) for i in range(nx)]
    behind = [((i + 1) % nx, i) for i in range(nx)]
    left = lax.ppermute(last, "fx", ahead)
    right = lax.ppermute(first, "fx", behind)
    return pl.pallas_call(
        functools.partial(sweep_kernel, nrows, nlev, width),
        out_shape=(
            jax.ShapeDtypeStruct(state.shape, F32),
            jax.ShapeDtypeStruct((nrows, levels.shape[0], width), F32),
        ),
        in_specs=[VMEM_SPEC] * 8,
        out_specs=(VMEM_SPEC, VMEM_SPEC),
        scratch_shapes=[
            pltpu.VMEM((total, nlev, 2 * width), F32),
            pltpu.VMEM((total, nlev, 2 * width), F32),
            pltpu.VMEM((total, 1, 2 * width), F32),
        ],
        compiler_params=params(),
        cost_estimate=cost(9),
        name="sweeps",
    )(state, coef, top, bottom, left, right, levels, marks)


def split(value):
    high = value.astype(BF16)
    low = (value - high.astype(F32)).astype(BF16)
    return high, low


def table_kernel(turn, table, out):
    count, rows, width = table.shape
    for k in range(count):
        weights = table[k].T if turn else table[k]
        high, low = split(weights)
        out[k, :, 0:width] = high
        out[k, :, width:] = low
    out[count] = jnp.zeros((rows, 2 * width), BF16)


def split_table(table, turn):
    count, rows, width = table.shape
    return pl.pallas_call(
        functools.partial(table_kernel, turn),
        out_shape=jax.ShapeDtypeStruct((count + 1, rows, 2 * width), BF16),
        in_specs=[VMEM_SPEC],
        out_specs=VMEM_SPEC,
        compiler_params=params(),
        cost_estimate=cost(3),
        name="split_table",
    )(table)


UNROLL = 8


PLACES = 40


def list_kernel(zero_row, values, valid, table):
    sets, room = valid.shape
    fields = values.shape[1] // room
    slot = lax.broadcasted_iota(jnp.int32, (fields * room, room), 0)
    other = lax.broadcasted_iota(jnp.int32, (fields * room, room), 1)
    within = slot % room
    transposed = (((1,), (1,)), ((), ()))

    def spread_out(chosen):
        return lax.dot_general(
            chosen.astype(F32), valid[...], transposed, preferred_element_type=F32
        )

    ahead = spread_out(other < within)
    first = lax.broadcasted_iota(jnp.int32, ahead.shape, 0) // room * PLACES + 1
    place = jnp.where(spread_out(other == within) > 0.5, ahead.astype(jnp.int32) + first, -1)
    lane = lax.broadcasted_iota(jnp.int32, (fields * room, 128), 1)
    for s in range(sets):
        chosen = (place[:, s : s + 1] == lane).astype(F32)
        table[s : s + 1, :] = jnp.dot(
            values[s : s + 1, :], chosen, preferred_element_type=F32
        )
    lane = lax.broadcasted_iota(jnp.int32, table.shape, 1)
    weight_lane = (lane > 2 * PLACES) & (lane <= 3 * PLACES)
    rows = jnp.where(weight_lane, table[...] + float(zero_row), table[...])
    number = jnp.sum(valid[...], axis=1, keepdims=True)
    table[...] = jnp.where(lane == 0, number, rows)


def slot_table(src, dst, row, count, blocks, zero_row, forward):
    sets, groups, cap = src.shape
    valid = (np.arange(cap, dtype=np.float32)[None, None, :] < count[:, :, None]).astype(F32)
    taken, given = (src, dst) if forward else (dst, src)
    given = given + blocks * np.arange(groups, dtype=np.float32)[None, :, None]
    values = jnp.stack([taken, given, row - zero_row], axis=1).reshape(sets, 3 * groups * cap)
    return pl.pallas_call(
        functools.partial(list_kernel, zero_row),
        out_shape=jax.ShapeDtypeStruct((sets, 128), F32),
        in_specs=[VMEM_SPEC] * 2,
        out_specs=VMEM_SPEC,
        cost_estimate=cost(1),
        name="slot_table",
    )(values, valid.reshape(sets, groups * cap))


def own_kernel(groups, blocks, zero_row, src, dst, row, counts, table):
    cap, owners = src.shape
    sets = table.shape[0]
    lane = lax.broadcasted_iota(jnp.int32, (owners, owners), 1)
    below = lax.broadcasted_iota(jnp.int32, (owners, owners), 0)
    same = lane // groups == below // groups
    number = counts[...].astype(F32)
    ahead = jnp.dot(number, (same & (below < lane)).astype(F32), preferred_element_type=F32)
    keys = [jnp.where(c < counts[...], ahead.astype(jnp.int32) + 1 + c, -1) for c in range(cap)]
    keys = jnp.concatenate(keys + [jnp.zeros((8 - cap, owners), jnp.int32)], axis=0).astype(F32)
    keys = keys.T.astype(jnp.int32)
    mine = lax.broadcasted_iota(jnp.int32, (sets, owners), 1) // groups == lax.broadcasted_iota(
        jnp.int32, (sets, owners), 0
    )
    which = lax.broadcasted_iota(jnp.int32, (1, owners), 1) % groups
    rows = jnp.zeros((sets, owners), F32)
    for c in range(cap):
        key = keys[:, c : c + 1]
        for f, value in enumerate(
            (src[c : c + 1, :], dst[c : c + 1, :] + which * blocks, row[c : c + 1, :] - zero_row)
        ):
            chosen = ((lane == key + f * PLACES) & (key > 0)).astype(F32)
            held = jnp.where(mine, value.astype(F32), 0.0)
            rows = rows + jnp.dot(held, chosen, preferred_element_type=F32)
    place = lax.broadcasted_iota(jnp.int32, rows.shape, 1)
    rows = jnp.where((place > 2 * PLACES) & (place <= 3 * PLACES), rows + float(zero_row), rows)
    used = jnp.sum(jnp.where(mine, number, 0.0), axis=1, keepdims=True)
    table[...] = jnp.where(place == 0, used, rows)


def own_table(src, dst, row, counts, groups, blocks, zero_row):
    owners = counts.shape[1]
    return pl.pallas_call(
        functools.partial(own_kernel, groups, blocks, zero_row),
        out_shape=jax.ShapeDtypeStruct((owners // groups, owners), F32),
        in_specs=[VMEM_SPEC] * 4,
        out_specs=VMEM_SPEC,
        cost_estimate=cost(1),
        name="own_table",
    )(src[0].T, dst[0].T, row[0].T, counts)


def remap_kernel(first, last, marked, sizes, own_rows, slots, order, lines, tables, *refs):
    arrays, refs = refs[: len(sizes)], refs[len(sizes) :]
    if not first:
        start, refs = refs[0], refs[1:]
    if marked:
        marks, refs = refs[0], refs[1:]
    outs, refs = (refs[:6], refs[6:]) if last else (refs[:1], refs[1:])
    blocks, total, products, tiles, held_rows, scalars, sems, late_sems, row_sems = refs
    features, width = total.shape[1:]
    sets = order.shape[0]
    size = blocks.shape[0] // sets
    at, row_copies, copies = 0, [], []
    for k, array in enumerate(arrays):
        if own_rows:
            for j in range(sizes[k] // size):
                row_copies.append(
                    pltpu.make_async_copy(
                        array.at[pl.ds(j * size + slots[0], 1), features - 8 : features],
                        tiles.at[at // size + j : at // size + j + 1],
                        row_sems.at[at // size + j],
                    )
                )
        part = blocks.at[at : at + sizes[k]]
        copies.append(pltpu.make_async_copy(array, part, sems.at[k]))
        at += sizes[k]
    for copy in row_copies + copies:
        copy.start()
    total[...] = jnp.zeros_like(total)
    products[...] = jnp.zeros_like(products)
    if own_rows:
        for p, copy in enumerate(row_copies):
            copy.wait()
            held_rows[p : p + 1, :] = tiles[p, 7:8, :].astype(jnp.int32)
        rows_copy = pltpu.make_async_copy(held_rows, scalars, late_sems.at[0])
        rows_copy.start()
        rows_copy.wait()
        slots = scalars

    def add(row, i):
        held = [products[u] for u in range(UNROLL)]
        for u in range(UNROLL):
            t = slots[row, 1 + PLACES + i * UNROLL + u]
            total[t] = total[t] + held[u]

    def one_set(p, carry):
        row = p if own_rows else order[p]

        def group(i, carry):
            made = []
            for u in range(UNROLL):
                value = blocks[p * size + slots[row, 1 + i * UNROLL + u]]
                high = value.astype(BF16).astype(F32)
                both = jnp.concatenate([high, value - high], axis=0).astype(BF16)
                weight = tables[slots[row, 1 + 2 * PLACES + i * UNROLL + u]]
                r = jnp.dot(both, weight, preferred_element_type=F32)
                made.append(r[:features, :width] + r[:features, width:] + r[features:, :width])
            add(*carry)
            for u in range(UNROLL):
                products[u] = made[u]
            return row, i

        return lax.fori_loop(0, (slots[row, 0] + UNROLL - 1) // UNROLL, group, carry)

    carry, at = (jnp.int32(0) if own_rows else order[0], jnp.int32(0)), 0
    for k, copy in enumerate(copies):
        copy.wait()
        carry = lax.fori_loop(at // size, (at + sizes[k]) // size, one_set, carry)
        at += sizes[k]
    add(*carry)
    if not first:
        for k in range(8):
            part = slice(k * size, (k + 1) * size)
            total[part] = total[part] + start[part]
    if marked:
        for b in range(total.shape[0]):
            total[b, features - 1 : features, :] = jnp.zeros((1, width), F32)
        each = marks.shape[0] // 8
        for k in range(8):
            for h in range(each):
                at = k * size + (lines[0] * 2 + lines[1]) * (size // 8) + h
                total[at, features - 1 : features, :] = marks[k * each + h : k * each + h + 1, :]
    copies = []
    if not last:
        copies.append(pltpu.make_async_copy(total, outs[0], sems.at[0]))
        copies[0].start()
    else:
        half = size // 2
        for k in range(4):
            core = lines[1] if k // 2 else 1 - lines[1]
            for place, away in enumerate(AWAY):
                owner = lax.rem(lines[0] + away, 4) * 2 + core
                out, at = (outs[k], place) if k < 2 or place < 3 else (outs[k + 2], 0)
                copies.append(
                    pltpu.make_async_copy(
                        total.at[pl.ds(owner * 2 * half + (k % 2) * half, half)],
                        out.at[at * half : (at + 1) * half],
                        sems.at[k * 4 + place],
                    )
                )
                copies[-1].start()
    for copy in copies:
        copy.wait()


AWAY = (2, 1, 3, 0)
REMAP_MIB = 16


def remap(slots, order, lines, arrays, tables, count, start, last=False, marks=None):
    block = arrays[0].shape[1:]
    sizes = [a.shape[0] for a in arrays]
    first = start is None
    marked = marks is not None
    own_rows = slots.ndim == 1
    sets = order.shape[0]
    large = tuple(arrays)
    small = (() if first else (start,)) + ((marks,) if marked else ())
    quarter = count // 4
    outs = (quarter,) * 2 + (quarter * 3 // 4,) * 2 + (quarter // 4,) * 2 if last else (count,)
    return pl.pallas_call(
        functools.partial(remap_kernel, first, last, marked, sizes, own_rows),
        out_shape=[jax.ShapeDtypeStruct((n,) + block, F32) for n in outs],
        in_specs=[SMEM_SPEC] * 3 + [VMEM_SPEC] + [HBM_SPEC] * len(large) + [VMEM_SPEC] * len(small),
        out_specs=[HBM_SPEC] * len(outs),
        scratch_shapes=[
            pltpu.VMEM((sum(sizes),) + block, F32),
            pltpu.VMEM((count,) + block, F32),
            pltpu.VMEM((UNROLL,) + block, F32),
            pltpu.VMEM((sets, 8, block[1]), F32),
            pltpu.VMEM((sets, 128), jnp.int32),
            pltpu.SMEM((sets, 128), jnp.int32),
            pltpu.SemaphoreType.DMA((16,)),
            pltpu.SemaphoreType.DMA((1,)),
            pltpu.SemaphoreType.DMA((sets,)),
        ],
        compiler_params=params(REMAP_MIB),
        cost_estimate=cost(8),
        name="remap",
    )(slots, order, lines, tables, *large, *small)


def step(value, along, other_core=False):
    ny = lax.axis_size("fy")
    pairs = []
    for y in range(ny):
        chip, core = divmod(y, 2)
        pairs.append((y, (chip + along) % (ny // 2) * 2 + (core ^ int(other_core))))
    return lax.ppermute(value, "fy", pairs)


def gather_sums(other, mine, own):
    n = own.shape[0]
    h = n // 2
    got = step(other, 0, True)
    far = mine[:n] + got[:n]
    far, mine, got = lax.optimization_barrier((far, mine, got))
    up, down = step(far[:h], 1), step(far[h:], -1)
    plus = mine[n : 2 * n] + got[n : 2 * n]
    minus = mine[2 * n :] + got[2 * n : 3 * n]
    plus = jnp.concatenate([plus[:h] + up, plus[h:]], axis=0)
    minus = jnp.concatenate([minus[:h], minus[h:] + down], axis=0)
    return own + got[3 * n :], step(plus, 1), step(minus, -1)


def hop(value, first, by):
    nx, ny = lax.axis_size("fx"), lax.axis_size("fy")
    side = math.isqrt(nx)
    pairs = []
    for x in range(nx):
        for y in range(ny):
            slow, fast = divmod(x, side)
            if first == (y % 2 == 0):
                fast = (fast + by) % side
            else:
                slow = (slow + by) % side
            pairs.append((x * ny + y, (slow * side + fast) * ny + y))
    return lax.ppermute(value, ("fx", "fy"), pairs)


def spread(own, given, before, weigh, count):
    barrier = lax.optimization_barrier
    own, given = barrier((own, given))
    p, m = hop(own, True, 1), hop(own, True, -1)
    bp, bm = hop(own, False, 1), hop(own, False, -1)
    ready = before(*given)
    p, m, bp, bm, ready = barrier((p, m, bp, bm, ready))
    slots, order, tables, marks, other = ready
    opp = hop(p, True, 1)
    pm = jnp.concatenate([p, m], axis=0)
    pmp, pmm = hop(pm, False, 1), hop(pm, False, -1)
    bo = hop(bp, False, 1)
    (sums,) = weigh(slots, order[:5], [own, p, m, bp, bm], tables, None, False, None)
    opp, sums = barrier((opp, sums))
    op, om = hop(opp, False, 1), hop(opp, False, -1)
    pmo = hop(pmm, False, -1)
    oo = hop(op, False, 1)
    (sums,) = weigh(slots, order[5:11], [opp, pmp, pmm, op], tables, sums, False, None)
    marks = None if isinstance(marks, tuple) else marks
    return weigh(slots, order[11:], [bo, om, pmo, oo], tables, sums, True, marks), other


def spread_order(mx, my):
    side = math.isqrt(lax.axis_size("fx"))
    slow, fast = mx // side, mx % side
    turned = my % 2
    places = [(0, 0), (1, 0), (-1, 0), (0, 1), (0, -1), (2, 0), (1, 1), (-1, 1), (1, -1), (-1, -1),
              (2, 1), (0, 2), (2, -1), (1, 2), (-1, 2), (2, 2)]
    a = jnp.array([p[0] for p in places], jnp.int32)
    b = jnp.array([p[1] for p in places], jnp.int32)
    from_fast = (fast - jnp.where(turned == 0, a, b) + side) % side
    from_slow = (slow - jnp.where(turned == 0, b, a) + side) % side
    return from_slow * side + from_fast


def gelu(x):
    inner = x * (0.7978845608028654 + (0.7978845608028654 * 0.044715) * (x * x))
    half = 0.5 * x
    return half + half * jnp.tanh(inner)


def summed(parts, b):
    own, plus, minus = parts
    return own[b] + (plus[b] + minus[b])


STEP = 16


def network_kernel(at, *refs):
    parts, (w_in, b_in, w_mid, b_mid, w_out), refs = refs[:3], refs[3:8], refs[8:]
    out, spare_rows = refs[-2:]
    features, width = out.shape[1:]
    count = parts[2].shape[0]

    def piece(i, carry):
        pairs = [i * STEP + k for k in range(0, STEP, 2)]
        blocks = [summed(parts, i * STEP + k) for k in range(STEP)]
        for k in range(STEP):
            spare_rows[pl.ds(i * STEP + k, 1), :] = blocks[k][features - 1 :]
        xs = [jnp.concatenate(blocks[k : k + 2], axis=1).astype(BF16) for k in range(0, STEP, 2)]
        firsts = [jnp.dot(w_in[...], x, preferred_element_type=F32) + b_in[...] for x in xs]
        firsts = [gelu(first).astype(BF16) for first in firsts]
        seconds = [jnp.dot(w_mid[...], h, preferred_element_type=F32) + b_mid[...] for h in firsts]
        seconds = [gelu(second).astype(BF16) for second in seconds]
        for b, second in zip(pairs, seconds):
            tend = jnp.dot(w_out[...], second, preferred_element_type=F32)
            out[at + b] = tend[:, :width]
            out[at + b + 1] = tend[:, width:]
        return carry

    lax.fori_loop(0, count // STEP, piece, 0)


def column_network(parts, weights, count, at, begun):
    block = parts[2].shape[1:]
    operands = tuple(parts) + tuple(weights) + (() if begun is None else (begun,))
    return pl.pallas_call(
        functools.partial(network_kernel, at),
        out_shape=(
            jax.ShapeDtypeStruct((count,) + block, F32),
            jax.ShapeDtypeStruct((parts[2].shape[0], block[1]), F32),
        ),
        in_specs=[VMEM_SPEC] * len(operands),
        out_specs=(VMEM_SPEC, VMEM_SPEC),
        input_output_aliases={} if begun is None else {len(operands) - 1: 0},
        compiler_params=params(),
        cost_estimate=cost(6),
        name="column_network",
    )(*operands)


def raise_kernel(*refs):
    levels, out = refs[-2:]
    width = out.shape[2]
    at = 0
    for parts in (refs[:3], refs[3:6]):
        count = parts[2].shape[0]
        for b in range(0, count, 2):
            pair = jnp.concatenate([summed(parts, b), summed(parts, b + 1)], axis=1)
            raised = jnp.dot(levels[...], pair, precision=HIGHEST, preferred_element_type=F32)
            out[at + b] = raised[:, :width]
            out[at + b + 1] = raised[:, width:]
        at += count


def raise_levels(halves, levels):
    count = sum(parts[2].shape[0] for parts in halves)
    shape = (count, levels.shape[0], halves[0][2].shape[2])
    return pl.pallas_call(
        raise_kernel,
        out_shape=jax.ShapeDtypeStruct(shape, F32),
        in_specs=[VMEM_SPEC] * 7,
        out_specs=VMEM_SPEC,
        compiler_params=params(),
        cost_estimate=cost(2),
        name="raise_levels",
    )(*halves[0], *halves[1], levels)


def level_matrix(brackets, fractions, nlev, variables, features):
    levels = nlev // variables
    cols = jnp.arange(levels, dtype=jnp.int32)
    lower = (cols[None, :] == brackets[:, None]).astype(F32)
    upper = (cols[None, :] == brackets[:, None] + 1).astype(F32)
    one = lower * (1.0 - fractions[:, None]) + upper * fractions[:, None]
    whole = (jnp.eye(variables, dtype=F32)[:, None, :, None] * one[None, :, None, :]).reshape(
        variables * one.shape[0], nlev
    )
    return jnp.pad(whole, ((0, features - whole.shape[0]), (0, 0)))


def per_device(
    state,
    coef,
    weight_table,
    src_blocks,
    dst_blocks,
    weight_rows,
    counts,
    brackets,
    fractions,
    w_in,
    b_in,
    w_mid,
    b_mid,
    w_out,
):
    nblocks, nlev, width = state.shape
    used_features = w_in.shape[1]
    features = -(-used_features // 8) * 8
    variables = used_features // brackets.shape[0]
    nx, ny = lax.axis_size("fx"), lax.axis_size("fy")
    mx, my = lax.axis_index("fx"), lax.axis_index("fy")
    ndev, cap = src_blocks.shape[1:]

    levels = level_matrix(brackets, fractions, nlev, variables, features)
    zero_row = weight_table.shape[0]
    order = spread_order(mx, my)
    spare = features - used_features
    place = mx.astype(jnp.int32).reshape(1)
    lines = jnp.stack([my // 2, my % 2]).astype(jnp.int32)
    one = 3 * cap + 1
    bands = ny * nblocks

    def weigh(slots, order, arrays, tables, start, last, marks):
        return remap(slots, order, lines, arrays, tables, bands, start, last, marks)

    def way_out(src, dst, row, cnt, weights, w_in, b_in, w_mid, b_mid, w_out):
        lists = jnp.concatenate([src[0], dst[0], row[0], cnt[0][:, None]], axis=1).astype(F32)
        lists = lists.reshape(nx, ny, one).transpose(1, 0, 2).reshape(ny, nx * one)
        lists = jnp.pad(lists, ((0, 0), (0, -nx * one % width))).reshape(-1, width)
        network = (
            jnp.pad(w_in, ((0, 0), (0, spare))),
            b_in[:, None],
            w_mid,
            b_mid[:, None],
            jnp.pad(w_out, ((0, spare), (0, 0))),
        )
        straight = jnp.arange(nx, dtype=jnp.int32)
        return place, straight, split_table(weights, False), lists, network

    def way_back(first, second, weights, order):
        rows = jnp.concatenate([first, second], axis=0).reshape(ny, -1, width)
        rows = rows[:, : -(-nx * one // width)].reshape(ny, -1)
        lists = rows[:, : nx * one].reshape(ny, nx, one).transpose(1, 0, 2)
        table = slot_table(
            lists[..., :cap],
            lists[..., cap : 2 * cap],
            lists[..., 2 * cap : 3 * cap],
            lists[..., 3 * cap],
            nblocks,
            zero_row,
            False,
        )
        return table.astype(jnp.int32), order, split_table(weights, True), (), ()

    own_rows = own_table(src_blocks, dst_blocks, weight_rows, counts, ny, nblocks, zero_row)
    field, source = diffuse(state, coef, levels, own_rows)
    given = (src_blocks, dst_blocks, weight_rows, counts, weight_table)
    given += (w_in, b_in, w_mid, b_mid, w_out)
    sums, network = spread(source, given, way_out, weigh, bands)
    half = nblocks // 2
    parts = gather_sums(*sums[0::2])
    tend, first = column_network(parts, network, nblocks, 0, None)
    parts = gather_sums(*sums[1::2])
    tend, second = column_network(parts, network, nblocks, half, tend)
    given = (first, second, weight_table, order)
    sums, _ = spread(tend, given, way_back, weigh, bands)
    halves = [gather_sums(*sums[k::2]) for k in range(2)]
    return field, raise_levels(halves, levels.T)


def solution(mesh):
    placed = (
        P("fy", None, "fx"),
        P("fy", "fx"),
        P(),
        P(("fx", "fy"), None, None),
        P(("fx", "fy"), None, None),
        P(("fx", "fy"), None, None),
        P(("fx", "fy"), None),
        P(),
        P(),
        P(),
        P(),
        P(),
        P(),
        P(),
    )
    return jax.shard_map(
        per_device,
        mesh=mesh,
        in_specs=placed,
        out_specs=(P("fy", None, "fx"), P("fy", None, "fx")),
        check_vma=False,
    )
```

```python
import functools
import math

import jax
import jax.numpy as jnp
import numpy as np
from jax import lax
from jax.experimental import pallas as pl
from jax.experimental.pallas import tpu as pltpu
from jax.sharding import PartitionSpec as P

SWEEPS = 4
ROWS = 16
F32 = jnp.float32
BF16 = jnp.bfloat16
HIGHEST = lax.Precision.HIGHEST

VMEM_SPEC = pl.BlockSpec(memory_space=pltpu.VMEM)
HBM_SPEC = pl.BlockSpec(memory_space=pltpu.HBM)
SMEM_SPEC = pl.BlockSpec(memory_space=pltpu.SMEM)


def params(mebibytes=32):
    return pltpu.CompilerParams(vmem_limit_bytes=mebibytes * 1024 * 1024)


def cost(microseconds):
    return pl.CostEstimate(
        flops=0, transcendentals=0, bytes_accessed=int(microseconds * 3_000_000)
    )


def pack_kernel(nrows, nlev, width, state, coef, top, bottom, first_out, last_out):
    halo = SWEEPS
    lane = lax.broadcasted_iota(jnp.int32, (nlev, width), 1)
    group = lane // halo
    lane_one = lax.broadcasted_iota(jnp.int32, (1, width), 1)
    group_one = lane_one // halo

    def rows_of(e):
        if e < halo:
            return top[e * nlev : (e + 1) * nlev, :], top[halo * nlev + e : halo * nlev + e + 1, :]
        if e < halo + nrows:
            return state[e - halo], coef[e - halo : e - halo + 1, :]
        b = e - halo - nrows
        return bottom[b * nlev : (b + 1) * nlev, :], bottom[halo * nlev + b : halo * nlev + b + 1, :]

    per = width // halo
    total = nrows + 2 * halo
    tiles = -(-total // per)
    first_out[...] = jnp.zeros_like(first_out)
    last_out[...] = jnp.zeros_like(last_out)
    for tile in range(tiles):
        first = jnp.zeros((nlev, width), F32)
        last = jnp.zeros((nlev, width), F32)
        first_c = jnp.zeros((1, width), F32)
        last_c = jnp.zeros((1, width), F32)
        for i in range(min(per, total - tile * per)):
            field, number = rows_of(tile * per + i)
            at = (halo * i) % width
            up = (halo * i + halo) % width
            first = jnp.where(group == i, pltpu.roll(field, at, 1) if at else field, first)
            last = jnp.where(group == i, pltpu.roll(field, up, 1) if up else field, last)
            first_c = jnp.where(group_one == i, pltpu.roll(number, at, 1) if at else number, first_c)
            last_c = jnp.where(group_one == i, pltpu.roll(number, up, 1) if up else number, last_c)
        first_out[tile * nlev : (tile + 1) * nlev, :] = first
        last_out[tile * nlev : (tile + 1) * nlev, :] = last
        first_out[tiles * nlev + tile : tiles * nlev + tile + 1, :] = first_c
        last_out[tiles * nlev + tile : tiles * nlev + tile + 1, :] = last_c


def sweep_kernel(
    nrows, nlev, width, state, coef, top, bottom, left, right, levels, marks, field_out, source_out, a, b, c
):
    halo = SWEEPS
    per = width // halo
    total = nrows + 2 * halo
    tiles = -(-total // per)
    lane = lax.broadcasted_iota(jnp.int32, (nlev, width), 1)
    lane_one = lax.broadcasted_iota(jnp.int32, (1, width), 1)
    for e in range(total):
        if e < halo:
            field = top[e * nlev : (e + 1) * nlev, :]
            number = top[halo * nlev + e : halo * nlev + e + 1, :]
        elif e < halo + nrows:
            field = state[e - halo]
            number = coef[e - halo : e - halo + 1, :]
        else:
            r = e - halo - nrows
            field = bottom[r * nlev : (r + 1) * nlev, :]
            number = bottom[halo * nlev + r : halo * nlev + r + 1, :]
        tile, i = e // per, e % per
        to_low = (width - halo * i) % width
        to_high = (width - halo - halo * i) % width
        edges = []
        for where_, rows in ((lane, slice(tile * nlev, (tile + 1) * nlev)),
                             (lane_one, slice(tiles * nlev + tile, tiles * nlev + tile + 1))):
            r_tile = right[rows, :]
            l_tile = left[rows, :]
            r_part = pltpu.roll(r_tile, to_low, 1) if to_low else r_tile
            l_part = pltpu.roll(l_tile, to_high, 1) if to_high else l_tile
            edges.append(
                jnp.where(where_ < halo, r_part, jnp.where(where_ >= width - halo, l_part, 0.0))
            )
        a[e, :, 0:width] = field
        a[e, :, width : 2 * width] = edges[0]
        c[e, :, 0:width] = number
        c[e, :, width : 2 * width] = edges[1]

    def step(source, e):
        mid = source[e]
        beside = pltpu.roll(mid, 1, 1) + pltpu.roll(mid, 2 * width - 1, 1)
        beside = beside + source[e + 1] + source[e - 1]
        return mid + c[e] * (beside - 4.0 * mid)

    held, other = a, b
    for sweep in range(1, SWEEPS):
        low, high = sweep, total - sweep
        steps = (high - low) // ROWS

        def some(i, carry, held=held, other=other, low=low):
            done = [step(held, low + i * ROWS + r) for r in range(ROWS)]
            for r in range(ROWS):
                other[low + i * ROWS + r] = done[r]
            return carry

        lax.fori_loop(0, steps, some, 0)
        for e in range(low + steps * ROWS, high):
            other[e] = step(held, e)
        held, other = other, held

    high, low = split(levels[...])
    level_parts = jnp.concatenate([high, high, low], axis=1)

    def final(i, carry):
        done = [step(held, i * ROWS + r + halo)[:, 0:width] for r in range(ROWS)]
        for r in range(ROWS):
            field_out[i * ROWS + r] = done[r]
        for r in range(0, ROWS, 2):
            pair = jnp.concatenate([done[r], done[r + 1]], axis=1)
            high, low = split(pair)
            parts = jnp.concatenate([high, low, high], axis=0)
            lowered = jnp.dot(level_parts, parts, preferred_element_type=F32)
            source_out[i * ROWS + r] = lowered[:, :width]
            source_out[i * ROWS + r + 1] = lowered[:, width:]
        return carry

    lax.fori_loop(0, nrows // ROWS, final, 0)
    spare = levels.shape[0] - 1
    for b in range(marks.shape[0]):
        source_out[b, spare : spare + 1, :] = marks[b : b + 1, :]


def diffuse(state, coef, levels, marks):
    nrows, nlev, width = state.shape
    halo = SWEEPS
    per = width // halo
    total = nrows + 2 * halo
    tiles = -(-total // per)
    nx, ny = lax.axis_size("fx"), lax.axis_size("fy")
    pad = -halo % 8
    blank = jnp.zeros((pad, width), F32)

    def row_message(rows):
        return jnp.concatenate(
            [state[rows].reshape(halo * nlev, width), coef[rows], blank], axis=0
        )

    down = [(i, i + 1) for i in range(ny - 1)]
    up = [(i + 1, i) for i in range(ny - 1)]
    top = lax.ppermute(row_message(slice(nrows - halo, nrows)), "fy", down)
    bottom = lax.ppermute(row_message(slice(0, halo)), "fy", up)
    edge = jax.ShapeDtypeStruct((tiles * nlev + 8, width), F32)
    first, last = pl.pallas_call(
        functools.partial(pack_kernel, nrows, nlev, width),
        out_shape=(edge, edge),
        in_specs=[VMEM_SPEC] * 4,
        out_specs=(VMEM_SPEC, VMEM_SPEC),
        compiler_params=params(),
        cost_estimate=cost(1),
        name="pack_edges",
    )(state, coef, top, bottom)
    ahead = [(i, (i + 1) % nx) for i in range(nx)]
    behind = [((i + 1) % nx, i) for i in range(nx)]
    left = lax.ppermute(last, "fx", ahead)
    right = lax.ppermute(first, "fx", behind)
    return pl.pallas_call(
        functools.partial(sweep_kernel, nrows, nlev, width),
        out_shape=(
            jax.ShapeDtypeStruct(state.shape, F32),
            jax.ShapeDtypeStruct((nrows, levels.shape[0], width), F32),
        ),
        in_specs=[VMEM_SPEC] * 8,
        out_specs=(VMEM_SPEC, VMEM_SPEC),
        scratch_shapes=[
            pltpu.VMEM((total, nlev, 2 * width), F32),
            pltpu.VMEM((total, nlev, 2 * width), F32),
            pltpu.VMEM((total, 1, 2 * width), F32),
        ],
        compiler_params=params(),
        cost_estimate=cost(9),
        name="sweeps",
    )(state, coef, top, bottom, left, right, levels, marks)


def split(value):
    high = value.astype(BF16)
    low = (value - high.astype(F32)).astype(BF16)
    return high, low


def table_kernel(turn, table, out):
    count, rows, width = table.shape
    for k in range(count):
        weights = table[k].T if turn else table[k]
        high, low = split(weights)
        out[k, :, 0:width] = high
        out[k, :, width:] = low
    out[count] = jnp.zeros((rows, 2 * width), BF16)


def split_table(table, turn):
    count, rows, width = table.shape
    return pl.pallas_call(
        functools.partial(table_kernel, turn),
        out_shape=jax.ShapeDtypeStruct((count + 1, rows, 2 * width), BF16),
        in_specs=[VMEM_SPEC],
        out_specs=VMEM_SPEC,
        compiler_params=params(),
        cost_estimate=cost(3),
        name="split_table",
    )(table)


UNROLL = 8


PLACES = 40


def list_kernel(zero_row, values, valid, table):
    sets, room = valid.shape
    fields = values.shape[1] // room
    slot = lax.broadcasted_iota(jnp.int32, (fields * room, room), 0)
    other = lax.broadcasted_iota(jnp.int32, (fields * room, room), 1)
    within = slot % room
    transposed = (((1,), (1,)), ((), ()))

    def spread_out(chosen):
        return lax.dot_general(
            chosen.astype(F32), valid[...], transposed, preferred_element_type=F32
        )

    ahead = spread_out(other < within)
    first = lax.broadcasted_iota(jnp.int32, ahead.shape, 0) // room * PLACES + 1
    place = jnp.where(spread_out(other == within) > 0.5, ahead.astype(jnp.int32) + first, -1)
    lane = lax.broadcasted_iota(jnp.int32, (fields * room, 128), 1)
    for s in range(sets):
        chosen = (place[:, s : s + 1] == lane).astype(F32)
        table[s : s + 1, :] = jnp.dot(
            values[s : s + 1, :], chosen, preferred_element_type=F32
        )
    lane = lax.broadcasted_iota(jnp.int32, table.shape, 1)
    weight_lane = (lane > 2 * PLACES) & (lane <= 3 * PLACES)
    rows = jnp.where(weight_lane, table[...] + float(zero_row), table[...])
    number = jnp.sum(valid[...], axis=1, keepdims=True)
    table[...] = jnp.where(lane == 0, number, rows)


def slot_table(src, dst, row, count, blocks, zero_row, forward):
    sets, groups, cap = src.shape
    valid = (np.arange(cap, dtype=np.float32)[None, None, :] < count[:, :, None]).astype(F32)
    taken, given = (src, dst) if forward else (dst, src)
    given = given + blocks * np.arange(groups, dtype=np.float32)[None, :, None]
    values = jnp.stack([taken, given, row - zero_row], axis=1).reshape(sets, 3 * groups * cap)
    return pl.pallas_call(
        functools.partial(list_kernel, zero_row),
        out_shape=jax.ShapeDtypeStruct((sets, 128), F32),
        in_specs=[VMEM_SPEC] * 2,
        out_specs=VMEM_SPEC,
        cost_estimate=cost(1),
        name="slot_table",
    )(values, valid.reshape(sets, groups * cap))


def own_kernel(groups, blocks, zero_row, src, dst, row, counts, table):
    cap, owners = src.shape
    sets = table.shape[0]
    lane = lax.broadcasted_iota(jnp.int32, (owners, owners), 1)
    below = lax.broadcasted_iota(jnp.int32, (owners, owners), 0)
    same = lane // groups == below // groups
    number = counts[...].astype(F32)
    ahead = jnp.dot(number, (same & (below < lane)).astype(F32), preferred_element_type=F32)
    keys = [jnp.where(c < counts[...], ahead.astype(jnp.int32) + 1 + c, -1) for c in range(cap)]
    keys = jnp.concatenate(keys + [jnp.zeros((8 - cap, owners), jnp.int32)], axis=0).astype(F32)
    keys = keys.T.astype(jnp.int32)
    mine = lax.broadcasted_iota(jnp.int32, (sets, owners), 1) // groups == lax.broadcasted_iota(
        jnp.int32, (sets, owners), 0
    )
    which = lax.broadcasted_iota(jnp.int32, (1, owners), 1) % groups
    rows = jnp.zeros((sets, owners), F32)
    for c in range(cap):
        key = keys[:, c : c + 1]
        for f, value in enumerate(
            (src[c : c + 1, :], dst[c : c + 1, :] + which * blocks, row[c : c + 1, :] - zero_row)
        ):
            chosen = ((lane == key + f * PLACES) & (key > 0)).astype(F32)
            held = jnp.where(mine, value.astype(F32), 0.0)
            rows = rows + jnp.dot(held, chosen, preferred_element_type=F32)
    place = lax.broadcasted_iota(jnp.int32, rows.shape, 1)
    rows = jnp.where((place > 2 * PLACES) & (place <= 3 * PLACES), rows + float(zero_row), rows)
    used = jnp.sum(jnp.where(mine, number, 0.0), axis=1, keepdims=True)
    table[...] = jnp.where(place == 0, used, rows)


def own_table(src, dst, row, counts, groups, blocks, zero_row):
    owners = counts.shape[1]
    return pl.pallas_call(
        functools.partial(own_kernel, groups, blocks, zero_row),
        out_shape=jax.ShapeDtypeStruct((owners // groups, owners), F32),
        in_specs=[VMEM_SPEC] * 4,
        out_specs=VMEM_SPEC,
        cost_estimate=cost(1),
        name="own_table",
    )(src[0].T, dst[0].T, row[0].T, counts)


def remap_kernel(first, last, marked, sizes, own_rows, slots, order, lines, tables, *refs):
    arrays, refs = refs[: len(sizes)], refs[len(sizes) :]
    if not first:
        start, refs = refs[0], refs[1:]
    if marked:
        marks, refs = refs[0], refs[1:]
    outs, refs = (refs[:6], refs[6:]) if last else (refs[:1], refs[1:])
    blocks, total, products, tiles, held_rows, scalars, sems, late_sems, row_sems = refs
    features, width = total.shape[1:]
    sets = order.shape[0]
    size = blocks.shape[0] // sets
    at, row_copies, copies = 0, [], []
    for k, array in enumerate(arrays):
        if own_rows:
            for j in range(sizes[k] // size):
                row_copies.append(
                    pltpu.make_async_copy(
                        array.at[pl.ds(j * size + slots[0], 1), features - 8 : features],
                        tiles.at[at // size + j : at // size + j + 1],
                        row_sems.at[at // size + j],
                    )
                )
        part = blocks.at[at : at + sizes[k]]
        copies.append(pltpu.make_async_copy(array, part, sems.at[k]))
        at += sizes[k]
    for copy in row_copies + copies:
        copy.start()
    total[...] = jnp.zeros_like(total)
    products[...] = jnp.zeros_like(products)
    if own_rows:
        for p, copy in enumerate(row_copies):
            copy.wait()
            held_rows[p : p + 1, :] = tiles[p, 7:8, :].astype(jnp.int32)
        rows_copy = pltpu.make_async_copy(held_rows, scalars, late_sems.at[0])
        rows_copy.start()
        rows_copy.wait()
        slots = scalars

    def add(row, i):
        held = [products[u] for u in range(UNROLL)]
        for u in range(UNROLL):
            t = slots[row, 1 + PLACES + i * UNROLL + u]
            total[t] = total[t] + held[u]

    def one_set(p, carry):
        row = p if own_rows else order[p]

        def group(i, carry):
            made = []
            for u in range(UNROLL):
                value = blocks[p * size + slots[row, 1 + i * UNROLL + u]]
                high = value.astype(BF16).astype(F32)
                both = jnp.concatenate([high, value - high], axis=0).astype(BF16)
                weight = tables[slots[row, 1 + 2 * PLACES + i * UNROLL + u]]
                r = jnp.dot(both, weight, preferred_element_type=F32)
                made.append(r[:features, :width] + r[:features, width:] + r[features:, :width])
            add(*carry)
            for u in range(UNROLL):
                products[u] = made[u]
            return row, i

        return lax.fori_loop(0, (slots[row, 0] + UNROLL - 1) // UNROLL, group, carry)

    carry, at = (jnp.int32(0) if own_rows else order[0], jnp.int32(0)), 0
    for k, copy in enumerate(copies):
        copy.wait()
        carry = lax.fori_loop(at // size, (at + sizes[k]) // size, one_set, carry)
        at += sizes[k]
    add(*carry)
    if not first:
        for k in range(8):
            part = slice(k * size, (k + 1) * size)
            total[part] = total[part] + start[part]
    if marked:
        for b in range(total.shape[0]):
            total[b, features - 1 : features, :] = jnp.zeros((1, width), F32)
        each = marks.shape[0] // 8
        for k in range(8):
            for h in range(each):
                at = k * size + (lines[0] * 2 + lines[1]) * (size // 8) + h
                total[at, features - 1 : features, :] = marks[k * each + h : k * each + h + 1, :]
    copies = []
    if not last:
        copies.append(pltpu.make_async_copy(total, outs[0], sems.at[0]))
        copies[0].start()
    else:
        half = size // 2
        for k in range(4):
            core = lines[1] if k // 2 else 1 - lines[1]
            for place, away in enumerate(AWAY):
                owner = lax.rem(lines[0] + away, 4) * 2 + core
                out, at = (outs[k], place) if k < 2 or place < 3 else (outs[k + 2], 0)
                copies.append(
                    pltpu.make_async_copy(
                        total.at[pl.ds(owner * 2 * half + (k % 2) * half, half)],
                        out.at[at * half : (at + 1) * half],
                        sems.at[k * 4 + place],
                    )
                )
                copies[-1].start()
    for copy in copies:
        copy.wait()


AWAY = (2, 1, 3, 0)
REMAP_MIB = 16


def remap(slots, order, lines, arrays, tables, count, start, last=False, marks=None):
    block = arrays[0].shape[1:]
    sizes = [a.shape[0] for a in arrays]
    first = start is None
    marked = marks is not None
    own_rows = slots.ndim == 1
    sets = order.shape[0]
    large = tuple(arrays)
    small = (() if first else (start,)) + ((marks,) if marked else ())
    quarter = count // 4
    outs = (quarter,) * 2 + (quarter * 3 // 4,) * 2 + (quarter // 4,) * 2 if last else (count,)
    return pl.pallas_call(
        functools.partial(remap_kernel, first, last, marked, sizes, own_rows),
        out_shape=[jax.ShapeDtypeStruct((n,) + block, F32) for n in outs],
        in_specs=[SMEM_SPEC] * 3 + [VMEM_SPEC] + [HBM_SPEC] * len(large) + [VMEM_SPEC] * len(small),
        out_specs=[HBM_SPEC] * len(outs),
        scratch_shapes=[
            pltpu.VMEM((sum(sizes),) + block, F32),
            pltpu.VMEM((count,) + block, F32),
            pltpu.VMEM((UNROLL,) + block, F32),
            pltpu.VMEM((sets, 8, block[1]), F32),
            pltpu.VMEM((sets, 128), jnp.int32),
            pltpu.SMEM((sets, 128), jnp.int32),
            pltpu.SemaphoreType.DMA((16,)),
            pltpu.SemaphoreType.DMA((1,)),
            pltpu.SemaphoreType.DMA((sets,)),
        ],
        compiler_params=params(REMAP_MIB),
        cost_estimate=cost(8),
        name="remap",
    )(slots, order, lines, tables, *large, *small)


def step(value, along, other_core=False):
    ny = lax.axis_size("fy")
    pairs = []
    for y in range(ny):
        chip, core = divmod(y, 2)
        pairs.append((y, (chip + along) % (ny // 2) * 2 + (core ^ int(other_core))))
    return lax.ppermute(value, "fy", pairs)


def gather_sums(other, mine, own):
    n = own.shape[0]
    h = n // 2
    got = step(other, 0, True)
    far = mine[:n] + got[:n]
    far, mine, got = lax.optimization_barrier((far, mine, got))
    up, down = step(far[:h], 1), step(far[h:], -1)
    plus = mine[n : 2 * n] + got[n : 2 * n]
    minus = mine[2 * n :] + got[2 * n : 3 * n]
    plus = jnp.concatenate([plus[:h] + up, plus[h:]], axis=0)
    minus = jnp.concatenate([minus[:h], minus[h:] + down], axis=0)
    return own + got[3 * n :], step(plus, 1), step(minus, -1)


def hop(value, first, by):
    nx, ny = lax.axis_size("fx"), lax.axis_size("fy")
    side = math.isqrt(nx)
    pairs = []
    for x in range(nx):
        for y in range(ny):
            slow, fast = divmod(x, side)
            if first == (y % 2 == 0):
                fast = (fast + by) % side
            else:
                slow = (slow + by) % side
            pairs.append((x * ny + y, (slow * side + fast) * ny + y))
    return lax.ppermute(value, ("fx", "fy"), pairs)


def spread(own, given, before, weigh, count):
    barrier = lax.optimization_barrier
    own, given = barrier((own, given))
    p, m = hop(own, True, 1), hop(own, True, -1)
    bp, bm = hop(own, False, 1), hop(own, False, -1)
    ready = before(*given)
    p, m, bp, bm, ready = barrier((p, m, bp, bm, ready))
    slots, order, tables, marks, other = ready
    opp = hop(p, True, 1)
    pm = jnp.concatenate([p, m], axis=0)
    pmp, pmm = hop(pm, False, 1), hop(pm, False, -1)
    bo = hop(bp, False, 1)
    (sums,) = weigh(slots, order[:5], [own, p, m, bp, bm], tables, None, False, None)
    opp, sums = barrier((opp, sums))
    op, om = hop(opp, False, 1), hop(opp, False, -1)
    pmo = hop(pmm, False, -1)
    oo = hop(op, False, 1)
    (sums,) = weigh(slots, order[5:11], [opp, pmp, pmm, op], tables, sums, False, None)
    marks = None if isinstance(marks, tuple) else marks
    (sums,) = weigh(slots, order[11:12], [bo], tables, sums, False, None)
    return weigh(slots, order[12:], [om, pmo, oo], tables, sums, True, marks), other


def spread_order(mx, my):
    side = math.isqrt(lax.axis_size("fx"))
    slow, fast = mx // side, mx % side
    turned = my % 2
    places = [(0, 0), (1, 0), (-1, 0), (0, 1), (0, -1), (2, 0), (1, 1), (-1, 1), (1, -1), (-1, -1),
              (2, 1), (0, 2), (2, -1), (1, 2), (-1, 2), (2, 2)]
    a = jnp.array([p[0] for p in places], jnp.int32)
    b = jnp.array([p[1] for p in places], jnp.int32)
    from_fast = (fast - jnp.where(turned == 0, a, b) + side) % side
    from_slow = (slow - jnp.where(turned == 0, b, a) + side) % side
    return from_slow * side + from_fast


def gelu(x):
    inner = x * (0.7978845608028654 + (0.7978845608028654 * 0.044715) * (x * x))
    half = 0.5 * x
    return half + half * jnp.tanh(inner)


def summed(parts, b):
    own, plus, minus = parts
    return own[b] + (plus[b] + minus[b])


STEP = 16


def network_kernel(at, *refs):
    parts, (w_in, b_in, w_mid, b_mid, w_out), refs = refs[:3], refs[3:8], refs[8:]
    out, spare_rows = refs[-2:]
    features, width = out.shape[1:]
    count = parts[2].shape[0]

    def piece(i, carry):
        pairs = [i * STEP + k for k in range(0, STEP, 2)]
        blocks = [summed(parts, i * STEP + k) for k in range(STEP)]
        for k in range(STEP):
            spare_rows[pl.ds(i * STEP + k, 1), :] = blocks[k][features - 1 :]
        xs = [jnp.concatenate(blocks[k : k + 2], axis=1).astype(BF16) for k in range(0, STEP, 2)]
        firsts = [jnp.dot(w_in[...], x, preferred_element_type=F32) + b_in[...] for x in xs]
        firsts = [gelu(first).astype(BF16) for first in firsts]
        seconds = [jnp.dot(w_mid[...], h, preferred_element_type=F32) + b_mid[...] for h in firsts]
        seconds = [gelu(second).astype(BF16) for second in seconds]
        for b, second in zip(pairs, seconds):
            tend = jnp.dot(w_out[...], second, preferred_element_type=F32)
            out[at + b] = tend[:, :width]
            out[at + b + 1] = tend[:, width:]
        return carry

    lax.fori_loop(0, count // STEP, piece, 0)


def column_network(parts, weights, count, at, begun):
    block = parts[2].shape[1:]
    operands = tuple(parts) + tuple(weights) + (() if begun is None else (begun,))
    return pl.pallas_call(
        functools.partial(network_kernel, at),
        out_shape=(
            jax.ShapeDtypeStruct((count,) + block, F32),
            jax.ShapeDtypeStruct((parts[2].shape[0], block[1]), F32),
        ),
        in_specs=[VMEM_SPEC] * len(operands),
        out_specs=(VMEM_SPEC, VMEM_SPEC),
        input_output_aliases={} if begun is None else {len(operands) - 1: 0},
        compiler_params=params(),
        cost_estimate=cost(6),
        name="column_network",
    )(*operands)


def raise_kernel(*refs):
    levels, out = refs[-2:]
    width = out.shape[2]
    at = 0
    for parts in (refs[:3], refs[3:6]):
        count = parts[2].shape[0]
        for b in range(0, count, 2):
            pair = jnp.concatenate([summed(parts, b), summed(parts, b + 1)], axis=1)
            raised = jnp.dot(levels[...], pair, precision=HIGHEST, preferred_element_type=F32)
            out[at + b] = raised[:, :width]
            out[at + b + 1] = raised[:, width:]
        at += count


def raise_levels(halves, levels):
    count = sum(parts[2].shape[0] for parts in halves)
    shape = (count, levels.shape[0], halves[0][2].shape[2])
    return pl.pallas_call(
        raise_kernel,
        out_shape=jax.ShapeDtypeStruct(shape, F32),
        in_specs=[VMEM_SPEC] * 7,
        out_specs=VMEM_SPEC,
        compiler_params=params(),
        cost_estimate=cost(2),
        name="raise_levels",
    )(*halves[0], *halves[1], levels)


def level_matrix(brackets, fractions, nlev, variables, features):
    levels = nlev // variables
    cols = jnp.arange(levels, dtype=jnp.int32)
    lower = (cols[None, :] == brackets[:, None]).astype(F32)
    upper = (cols[None, :] == brackets[:, None] + 1).astype(F32)
    one = lower * (1.0 - fractions[:, None]) + upper * fractions[:, None]
    whole = (jnp.eye(variables, dtype=F32)[:, None, :, None] * one[None, :, None, :]).reshape(
        variables * one.shape[0], nlev
    )
    return jnp.pad(whole, ((0, features - whole.shape[0]), (0, 0)))


def per_device(
    state,
    coef,
    weight_table,
    src_blocks,
    dst_blocks,
    weight_rows,
    counts,
    brackets,
    fractions,
    w_in,
    b_in,
    w_mid,
    b_mid,
    w_out,
):
    nblocks, nlev, width = state.shape
    used_features = w_in.shape[1]
    features = -(-used_features // 8) * 8
    variables = used_features // brackets.shape[0]
    nx, ny = lax.axis_size("fx"), lax.axis_size("fy")
    mx, my = lax.axis_index("fx"), lax.axis_index("fy")
    ndev, cap = src_blocks.shape[1:]

    levels = level_matrix(brackets, fractions, nlev, variables, features)
    zero_row = weight_table.shape[0]
    order = spread_order(mx, my)
    spare = features - used_features
    place = mx.astype(jnp.int32).reshape(1)
    lines = jnp.stack([my // 2, my % 2]).astype(jnp.int32)
    one = 3 * cap + 1
    bands = ny * nblocks

    def weigh(slots, order, arrays, tables, start, last, marks):
        return remap(slots, order, lines, arrays, tables, bands, start, last, marks)

    def way_out(src, dst, row, cnt, weights, w_in, b_in, w_mid, b_mid, w_out):
        lists = jnp.concatenate([src[0], dst[0], row[0], cnt[0][:, None]], axis=1).astype(F32)
        lists = lists.reshape(nx, ny, one).transpose(1, 0, 2).reshape(ny, nx * one)
        lists = jnp.pad(lists, ((0, 0), (0, -nx * one % width))).reshape(-1, width)
        network = (
            jnp.pad(w_in, ((0, 0), (0, spare))),
            b_in[:, None],
            w_mid,
            b_mid[:, None],
            jnp.pad(w_out, ((0, spare), (0, 0))),
        )
        straight = jnp.arange(nx, dtype=jnp.int32)
        return place, straight, split_table(weights, False), lists, network

    def way_back(first, second, weights, order):
        rows = jnp.concatenate([first, second], axis=0).reshape(ny, -1, width)
        rows = rows[:, : -(-nx * one // width)].reshape(ny, -1)
        lists = rows[:, : nx * one].reshape(ny, nx, one).transpose(1, 0, 2)
        table = slot_table(
            lists[..., :cap],
            lists[..., cap : 2 * cap],
            lists[..., 2 * cap : 3 * cap],
            lists[..., 3 * cap],
            nblocks,
            zero_row,
            False,
        )
        return table.astype(jnp.int32), order, split_table(weights, True), (), ()

    own_rows = own_table(src_blocks, dst_blocks, weight_rows, counts, ny, nblocks, zero_row)
    field, source = diffuse(state, coef, levels, own_rows)
    given = (src_blocks, dst_blocks, weight_rows, counts, weight_table)
    given += (w_in, b_in, w_mid, b_mid, w_out)
    sums, network = spread(source, given, way_out, weigh, bands)
    half = nblocks // 2
    parts = gather_sums(*sums[0::2])
    tend, first = column_network(parts, network, nblocks, 0, None)
    parts = gather_sums(*sums[1::2])
    tend, second = column_network(parts, network, nblocks, half, tend)
    given = (first, second, weight_table, order)
    sums, _ = spread(tend, given, way_back, weigh, bands)
    halves = [gather_sums(*sums[k::2]) for k in range(2)]
    return field, raise_levels(halves, levels.T)


def solution(mesh):
    placed = (
        P("fy", None, "fx"),
        P("fy", "fx"),
        P(),
        P(("fx", "fy"), None, None),
        P(("fx", "fy"), None, None),
        P(("fx", "fy"), None, None),
        P(("fx", "fy"), None),
        P(),
        P(),
        P(),
        P(),
        P(),
        P(),
        P(),
    )
    return jax.shard_map(
        per_device,
        mesh=mesh,
        in_specs=placed,
        out_specs=(P("fy", None, "fx"), P("fy", None, "fx")),
        check_vma=False,
    )
```
